128 devices in a mesh: row: 8 (over z, x_lo), col: 16 (over x_hi, y, core).
Axes of the slice: x: 4 (x_hi: 2, x_lo: 2; x = x_hi * 2 + x_lo), y: 4, z: 4, core: 2. Of those that a mesh axis runs over, the one named last changes fastest.
Arguments:
- object_tile: float32 [2, 4096, 8192], P(None, 'row', 'col'), may hold values from -6 to 6
- probe: float32 [2, 256, 256], replicated, may hold values from -6 to 6
- amplitudes: float32 [8, 16, 16, 256, 256], P('row', 'col'), may hold values from 0 to 3
- positions: int32 [8, 16, 16, 2], P('row', 'col'), may hold values from 0 to 511, as said below
- counts: int32 [8, 16], P('row'), may hold values from 0 to 16, as said below
Outputs:
- object_grad: float32 [2, 4096, 8192], P(None, 'row', 'col')
- probe_grad: float32 [2, 256, 256], replicated
The draws below stay inside these ranges and needn't reach their ends.
Inputs may be any that keep to these rules, and one draw needn't show every extreme that they name: `positions`: offsets place every window inside the object: on the last row index of devices the row offset is at most 256, and on the last column index the column offset at most 256. Over each row index of devices the counts sum to exactly 128.
All inputs are finite; a program needn't handle non-finite values.
Results may differ from the reference program's by a relative error of at most 0.00014.
Values sent between devices are 32-bit elements; how exact they have to be, the bound alone decides.
A program may use at most 192 MiB of HBM per device.

```python
import jax
import jax.numpy as jnp
from jax import lax

P_SIZE = 256
TR = 512
TC = 512
CAP = 16
NR = 4096
NC = 8192
N_ROW = 8
N_COL = 16


def draw_positions(key, part):
    key = jax.random.fold_in(key, 11)
    key_rows, key_cols = jax.random.split(key)
    row_limit = jnp.where(jnp.arange(N_ROW) == N_ROW - 1, TR - P_SIZE + 1, TR).astype(jnp.int32)[:, None, None]
    col_limit = jnp.where(jnp.arange(N_COL) == N_COL - 1, TC - P_SIZE + 1, TC).astype(jnp.int32)[None, :, None]
    rows = jax.random.randint(key_rows, (N_ROW, N_COL, CAP), 0, row_limit, dtype=jnp.int32)
    cols = jax.random.randint(key_cols, (N_ROW, N_COL, CAP), 0, col_limit, dtype=jnp.int32)
    rows = rows.at[0, 0, 0].set(TR - 1)
    cols = cols.at[0, 0, 0].set(TC - 1)
    return jnp.stack([rows, cols], axis=-1).astype(jnp.int32)


def draw_counts(key, part):
    key = jax.random.fold_in(key, 23)

    def one_line(line_key):
        key_perm, key_load = jax.random.split(line_key)
        order = jax.random.permutation(key_perm, N_COL)
        loads = jax.random.randint(key_load, (N_COL // 2,), 0, CAP + 1, dtype=jnp.int32)
        loads = loads.at[0].set(CAP)
        values = jnp.stack([loads, CAP - loads], axis=1).reshape(-1)
        return jnp.zeros((N_COL,), jnp.int32).at[order].set(values)
    return jax.vmap(one_line)(jax.random.split(key, N_ROW)).astype(jnp.int32)


def levels(rng, shape, cuts, least, largest):
    level, own = 1.0, jax.random.fold_in(rng, 6)
    for axis_at, shards_of in cuts:
        heights = jnp.exp(jax.random.uniform(jax.random.fold_in(own, axis_at), (shards_of,), jnp.float32, least / len(cuts), largest / len(cuts)))
        level = level * jnp.repeat(heights, shape[axis_at] // shards_of).reshape([-1 if axis == axis_at else 1 for axis in range(len(shape))])
    return level


def centred(stream_key, shape, deviation, reach, shards=(), kind=jnp.bfloat16):
    loudness = levels(stream_key, shape, shards, -0.22, 0.18) if shards else 1.0
    result = jax.random.normal(stream_key, shape, jnp.float32) * deviation * loudness
    return jnp.minimum(jnp.maximum(result, -reach), reach).astype(kind)


def setup_inputs(seed: int = 0) -> dict:
    streams_of = jax.random.split(jax.random.key(seed), 6)
    return {
        "object_tile": centred(streams_of[0], (2, NR, NC), 1.0, 6.0, ((1, 8), (2, 16)), jnp.float32),
        "probe": centred(streams_of[1], (2, P_SIZE, P_SIZE), 1.0, 6.0, (), jnp.float32),
        "amplitudes": jnp.clip(3.0 * jax.random.uniform(streams_of[2], (N_ROW, N_COL, CAP, P_SIZE, P_SIZE), jnp.float32) ** levels(streams_of[2], (N_ROW, N_COL, CAP, P_SIZE, P_SIZE), ((0, 8), (1, 16)), -0.2, 0.2), 0.0, 3.0),
        "positions": draw_positions(jax.random.fold_in(streams_of[5], 71), 0),
        "counts": draw_counts(jax.random.fold_in(streams_of[5], 71), 0),
    }


smooth_term = 0.01

def slot_terms(window, probe, amp, live):
    exit_re = probe[0] * window[0] - probe[1] * window[1]
    exit_im = probe[0] * window[1] + probe[1] * window[0]
    wave = jnp.fft.fft2(exit_re + 1j * exit_im, norm='ortho')
    wave_re = jnp.real(wave)
    wave_im = jnp.imag(wave)
    model = jnp.sqrt(wave_re * wave_re + wave_im * wave_im + smooth_term)
    factor = 2.0 * (1.0 - amp / model) * live
    back = jnp.fft.ifft2(factor * wave_re + 1j * (factor * wave_im), norm='ortho')
    back_re = jnp.real(back)
    back_im = jnp.imag(back)
    obj_term = jnp.stack([probe[0] * back_re + probe[1] * back_im, probe[0] * back_im - probe[1] * back_re])
    probe_term = jnp.stack([window[0] * back_re + window[1] * back_im, window[0] * back_im - window[1] * back_re])
    return (obj_term.astype(object_dtype(window)), probe_term.astype(object_dtype(window)))

def object_dtype(array):
    return array.dtype

def reference(object_tile, probe, amplitudes, positions, counts):
    slot_ids = jnp.arange(CAP, dtype=jnp.int32)
    live = (slot_ids[None, None, :] < counts[:, :, None]).astype(object_tile.dtype).reshape(-1)
    row_base = (jnp.arange(N_ROW, dtype=jnp.int32) * TR)[:, None, None]
    col_base = (jnp.arange(N_COL, dtype=jnp.int32) * TC)[None, :, None]
    glob_rows = (positions[:, :, :, 0] + row_base).reshape(-1).astype(jnp.int32)
    glob_cols = (positions[:, :, :, 1] + col_base).reshape(-1).astype(jnp.int32)
    amps = amplitudes.reshape(-1, P_SIZE, P_SIZE)
    zero = jnp.int32(0)

    def step(carry, item):
        grad_obj, grad_probe = carry
        grow, gcol, amp, flag = item
        window = lax.dynamic_slice(object_tile, (zero, grow, gcol), (2, P_SIZE, P_SIZE))
        obj_term, probe_term = slot_terms(window, probe, amp, flag)
        current = lax.dynamic_slice(grad_obj, (zero, grow, gcol), (2, P_SIZE, P_SIZE))
        grad_obj = lax.dynamic_update_slice(grad_obj, current + obj_term, (zero, grow, gcol))
        return ((grad_obj, grad_probe + probe_term), None)
    start = (jnp.zeros_like(object_tile), jnp.zeros_like(probe))
    (grad_obj, grad_probe), _ = lax.scan(step, start, (glob_rows, glob_cols, amps, live))
    return (grad_obj, grad_probe)
```

```python
import functools
import math

import jax
import jax.numpy as jnp
import numpy as np
from jax import lax
from jax.experimental import pallas as pl
from jax.experimental.pallas import tpu as pltpu
from jax.sharding import PartitionSpec as P

smooth_term = 0.01
F32 = jnp.float32
BF16 = jnp.bfloat16
W = 256
H = 128
CH = 32
VMEM = pltpu.VMEM


def split_table(table):
    high = table.astype(jnp.bfloat16)
    low = (table - high.astype(np.float64)).astype(jnp.bfloat16)
    return high, low


def half_tables():
    n = np.arange(H)
    even = np.exp(-2j * np.pi * np.outer(n, n) / H) / 16.0
    odd = np.exp(-2j * np.pi * n / W)[:, None] * even

    def real_form(z):
        return np.block([[z.real, z.imag], [-z.imag, z.real]])

    return real_form(even), real_form(odd), real_form(even.conj().T), real_form(odd.conj().T)


def tables():
    even, odd, inv_even, inv_odd = half_tables()
    right, left = [], []
    for table in (even, odd, inv_even, inv_odd):
        high, low = split_table(table)
        right.append(np.concatenate([high, high, low], axis=0))
        high, low = split_table(table.T)
        left.append(np.concatenate([high, high, low], axis=1))
    return np.stack(right), np.stack(left)


def high_low(value):
    high = value.astype(BF16)
    return high, (value - high.astype(F32)).astype(BF16)


def put_cols(ref, rows, half, value):
    high, low = high_low(value)
    at = H * half
    ref[rows, at : at + H] = high
    ref[rows, W + at : W + at + H] = low
    ref[rows, 2 * W + at : 2 * W + at + H] = high


def put_rows(ref, row, cols, value):
    high, low = high_low(value)
    count = value.shape[0]
    ref[row : row + count, cols] = high
    ref[W + row : W + row + count, cols] = low
    ref[2 * W + row : 2 * W + row + count, cols] = high


def dot(a, b):
    return jnp.dot(a, b, preferred_element_type=F32)


def slot_work(r, c, ext, gext, probe, amp, right_t, left_t, win, xe, xo, ye, yo, ve, vo, pgrad):
    j0 = lax.shift_right_logical(c, 7)
    s = lax.bitwise_and(c, 127)
    back_shift = lax.bitwise_and(128 - s, 127)
    lane = lax.broadcasted_iota(jnp.int32, (CH, H), 1)
    first = lane < 128 - s
    for i in range(W // CH):
        rows = pl.ds(i * CH, CH)
        parts = []
        for p in range(2):
            t = [
                pltpu.roll(ext[p, j0 + q, pl.ds(r + i * CH, CH), :], back_shift, 1)
                for q in range(3)
            ]
            a = jnp.where(first, t[0], t[1])
            b = jnp.where(first, t[1], t[2])
            win[p, rows, 0:H] = a
            win[p, rows, H:W] = b
            parts.append((a, b))
        (are, bre), (aim, bim) = parts
        pra, prb = probe[0, rows, 0:H], probe[0, rows, H:W]
        pia, pib = probe[1, rows, 0:H], probe[1, rows, H:W]
        ea_re = pra * are - pia * aim
        ea_im = pra * aim + pia * are
        eb_re = prb * bre - pib * bim
        eb_im = prb * bim + pib * bre
        put_cols(xe, rows, 0, ea_re + eb_re)
        put_cols(xe, rows, 1, ea_im + eb_im)
        put_cols(xo, rows, 0, ea_re - eb_re)
        put_cols(xo, rows, 1, ea_im - eb_im)
    ye[...] = dot(xe[...], right_t[0])
    yo[...] = dot(xo[...], right_t[1])
    for i in range(H // CH):
        top = pl.ds(i * CH, CH)
        bot = pl.ds(H + i * CH, CH)
        for half, y in ((0, ye), (1, yo)):
            cols = pl.ds(H * half, H)
            for part in range(2):
                t, b = y[top, H * part : H * part + H], y[bot, H * part : H * part + H]
                put_rows(ve, H * part + i * CH, cols, t + b)
                put_rows(vo, H * part + i * CH, cols, t - b)
    ye[...] = dot(left_t[0], ve[...])
    yo[...] = dot(left_t[1], vo[...])
    for i in range(H // CH):
        for half, y, v in ((0, ye, ve), (1, yo, vo)):
            re = y[pl.ds(i * CH, CH), :]
            im = y[pl.ds(H + i * CH, CH), :]
            a = amp[pl.ds(H * half + i * CH, CH), :]
            f = 2.0 - (2.0 * a) * lax.rsqrt(re * re + im * im + smooth_term)
            put_rows(v, i * CH, slice(None), f * re)
            put_rows(v, H + i * CH, slice(None), f * im)
    ye[...] = dot(left_t[2], ve[...])
    yo[...] = dot(left_t[3], vo[...])
    for i in range(H // CH):
        for part in range(2):
            e = ye[pl.ds(H * part + i * CH, CH), :]
            o = yo[pl.ds(H * part + i * CH, CH), :]
            for at, value in ((0, e + o), (H, e - o)):
                rows = pl.ds(at + i * CH, CH)
                put_cols(xe, rows, part, value[:, 0:H])
                put_cols(xo, rows, part, value[:, H:W])
    ye[...] = dot(xe[...], right_t[2])
    yo[...] = dot(xo[...], right_t[3])
    later = lane >= s
    for i in range(W // CH):
        rows = pl.ds(i * CH, CH)
        e_re, e_im = ye[rows, 0:H], ye[rows, H:W]
        o_re, o_im = yo[rows, 0:H], yo[rows, H:W]
        terms = []
        for cols, b_re, b_im in ((slice(0, H), e_re + o_re, e_im + o_im), (slice(H, W), e_re - o_re, e_im - o_im)):
            pr, pi = probe[0, rows, cols], probe[1, rows, cols]
            wr, wi = win[0, rows, cols], win[1, rows, cols]
            at = cols.start * 2 + i * CH
            pgrad[at : at + CH, :] += wr * b_re + wi * b_im
            pgrad[2 * W + at : 2 * W + at + CH, :] += wr * b_im - wi * b_re
            terms.append((pr * b_re + pi * b_im, pr * b_im - pi * b_re))
        for p in range(2):
            ra = pltpu.roll(terms[0][p], s, 1)
            rb = pltpu.roll(terms[1][p], s, 1)
            at = pl.ds(r + i * CH, CH)
            gext[p, j0, at, :] += jnp.where(later, ra, 0.0)
            gext[p, j0 + 1, at, :] += jnp.where(later, rb, ra)
            gext[p, j0 + 2, at, :] += jnp.where(later, 0.0, rb)


def slots_kernel(
    pos, cnt, tile, right, below_l, below_r, corner, amps, probe, right_t, left_t,
    g_tile, g_right, g_below_l, g_below_r, g_corner, pgrad,
    ext, gext, amp_buf, win, xe, xo, ye, yo, ve, vo, in_sem, amp_sem, out_sem,
):
    def pieces(arrays, buf):
        t, rt, bl, br, cn = arrays
        out = []
        for j in range(4):
            out.append((t.at[:, :, pl.ds(H * j, H)], buf.at[:, j, pl.ds(0, 512), :]))
        for j in range(2):
            cols = pl.ds(H * j, H)
            out.append((rt.at[:, :, cols], buf.at[:, 4 + j, pl.ds(0, 512), :]))
            out.append((bl.at[:, :, cols], buf.at[:, j, pl.ds(512, 256), :]))
            out.append((br.at[:, :, cols], buf.at[:, 2 + j, pl.ds(512, 256), :]))
            out.append((cn.at[:, :, cols], buf.at[:, 4 + j, pl.ds(512, 256), :]))
        return out

    def amp_copy(k, slot):
        return pltpu.make_async_copy(amps.at[k], amp_buf.at[slot], amp_sem.at[slot])

    loads = [
        pltpu.make_async_copy(hbm, vm, in_sem.at[n])
        for n, (hbm, vm) in enumerate(pieces((tile, right, below_l, below_r, corner), ext))
    ]
    for copy in loads:
        copy.start()
    count = cnt[0]

    @pl.when(count > 0)
    def _():
        amp_copy(0, 0).start()

    gext[...] = jnp.zeros_like(gext)
    pgrad[...] = jnp.zeros_like(pgrad)
    for copy in loads:
        copy.wait()

    def body(k, _):
        slot = lax.bitwise_and(k, 1)

        @pl.when(k + 1 < count)
        def _():
            amp_copy(k + 1, 1 - slot).start()

        amp_copy(k, slot).wait()
        slot_work(
            pos[k, 0], pos[k, 1], ext, gext, probe, amp_buf.at[slot], right_t, left_t,
            win, xe, xo, ye, yo, ve, vo, pgrad,
        )
        return 0

    lax.fori_loop(0, count, body, 0)
    stores = [
        pltpu.make_async_copy(vm, hbm, out_sem.at[n])
        for n, (hbm, vm) in enumerate(pieces((g_tile, g_right, g_below_l, g_below_r, g_corner), gext))
    ]
    for copy in stores:
        copy.start()
    for copy in stores:
        copy.wait()


def run_slots(own_pos, count, tile, right, below_l, below_r, corner, amps, probe):
    right_t, left_t = tables()
    any_spec = pl.BlockSpec(memory_space=pl.ANY)
    vmem = pl.BlockSpec(memory_space=pltpu.VMEM)
    smem = pl.BlockSpec(memory_space=pltpu.SMEM)
    block = lambda *shape: jax.ShapeDtypeStruct(shape, F32)
    return pl.pallas_call(
        slots_kernel,
        out_shape=(
            block(2, 512, 512), block(2, 512, 256), block(2, 256, 256), block(2, 256, 256),
            block(2, 256, 256), block(4 * W, H),
        ),
        in_specs=[smem, smem] + [any_spec] * 6 + [vmem] * 3,
        out_specs=tuple([any_spec] * 5 + [vmem]),
        scratch_shapes=[
            VMEM((2, 6, 768, H), F32),
            VMEM((2, 6, 768, H), F32),
            VMEM((2, W, W), F32),
            VMEM((2, W, W), F32),
            VMEM((W, 3 * W), BF16),
            VMEM((W, 3 * W), BF16),
            VMEM((W, W), F32),
            VMEM((W, W), F32),
            VMEM((3 * W, W), BF16),
            VMEM((3 * W, W), BF16),
            pltpu.SemaphoreType.DMA((12,)),
            pltpu.SemaphoreType.DMA((2,)),
            pltpu.SemaphoreType.DMA((12,)),
        ],
        compiler_params=pltpu.CompilerParams(vmem_limit_bytes=48 * 1024 * 1024),
        name="slots",
    )(own_pos, count, tile, right, below_l, below_r, corner, amps, probe, jnp.asarray(right_t), jnp.asarray(left_t))


def reorder_kernel(amp_l, amp_r, select_t, amp_out):
    half = jnp.concatenate(
        [
            jnp.concatenate([ref[0, pl.ds(start, H, stride=2), :] for ref in (amp_l, amp_r)], axis=1)
            for start in range(2)
        ],
        axis=0,
    )
    amp_out[0] = jnp.dot(half, select_t[...], precision=lax.Precision.HIGHEST, preferred_element_type=F32)


def reorder(amps):
    n = np.arange(H)
    select = np.zeros((W, W), np.float32)
    select[2 * n, n] = 1.0
    select[2 * n + 1, H + n] = 1.0
    return pl.pallas_call(
        reorder_kernel,
        grid=(amps.shape[0],),
        out_shape=jax.ShapeDtypeStruct(amps.shape, F32),
        in_specs=[
            pl.BlockSpec((1, W, H), lambda k: (k, 0, 0)),
            pl.BlockSpec((1, W, H), lambda k: (k, 0, 1)),
            pl.BlockSpec((W, W), lambda k: (0, 0)),
        ],
        out_specs=pl.BlockSpec((1, W, W), lambda k: (k, 0, 0)),
        name="reorder",
    )(amps, amps, jnp.asarray(select))


MESH = pl.DeviceIdType.MESH


def total_kernel(part, out, full, got0, acc0, got1, acc1, got2, s_send, s_recv, z_send, z_recv, n_send, n_recv):
    row, col = lax.axis_index("row"), lax.axis_index("col")
    z, x_lo = row // 2, row % 2
    x_hi, y, core = col // 8, (col // 2) % 4, col % 2
    plane = (x_hi * 2 + x_lo) * 4 + y

    mate = (row, col + 1 - 2 * core)

    def z_peer(q):
        return (z + q) % 4

    def z_id(q):
        return (z_peer(q) * 2 + x_lo, col)

    def plane_peer(q):
        return (plane + q) % 16

    def plane_id(q):
        n = plane_peer(q)
        x = n // 4
        return (z * 2 + x % 2, (x // 2) * 8 + (n % 4) * 2 + core)

    barrier = pltpu.get_barrier_semaphore()
    pl.semaphore_signal(barrier, inc=1, device_id=mate, device_id_type=MESH)
    for q in range(1, 4):
        pl.semaphore_signal(barrier, inc=1, device_id=z_id(q), device_id_type=MESH)
    for q in range(1, 16):
        pl.semaphore_signal(barrier, inc=1, device_id=plane_id(q), device_id_type=MESH)
    pl.semaphore_wait(barrier, 19)

    def block(start, count):
        return pl.ds(pl.multiple_of(start, 8), count)

    def send(src, dst, send_sem, recv_sem, device):
        return pltpu.make_async_remote_copy(
            src_ref=src, dst_ref=dst, send_sem=send_sem, recv_sem=recv_sem,
            device_id=device, device_id_type=MESH,
        )

    def exchange(copies):
        for copy in copies:
            copy.start()
        for copy in copies:
            copy.wait()

    exchange([send(part.at[block((1 - core) * 512, 512)], got0, s_send.at[0], s_recv.at[0], mate)])
    acc0[...] = part[block(core * 512, 512), :] + got0[...]
    exchange([
        send(acc0.at[block(z_peer(q) * 128, 128)], got1.at[q - 1], z_send.at[q - 1], z_recv.at[q - 1], z_id(q))
        for q in range(1, 4)
    ])
    acc1[...] = acc0[block(z * 128, 128), :] + got1[0] + got1[1] + got1[2]
    exchange([
        send(acc1.at[block(plane_peer(q) * 8, 8)], got2.at[q - 1], n_send.at[q - 1], n_recv.at[q - 1], plane_id(q))
        for q in range(1, 16)
    ])
    mine = acc1[block(plane * 8, 8), :]
    for q in range(15):
        mine = mine + got2[q]
    base0 = core * 512
    base1 = base0 + z * 128
    own = block(base1 + plane * 8, 8)
    full[own, :] = mine
    exchange([
        send(full.at[own], full.at[own], n_send.at[14 + q], n_recv.at[14 + q], plane_id(q))
        for q in range(1, 16)
    ])
    own = block(base1, 128)
    exchange([
        send(full.at[own], full.at[own], z_send.at[2 + q], z_recv.at[2 + q], z_id(q))
        for q in range(1, 4)
    ])
    own = block(base0, 512)
    exchange([send(full.at[own], full.at[own], s_send.at[1], s_recv.at[1], mate)])
    for p in range(2):
        for half in range(2):
            out[p, :, pl.ds(H * half, H)] = full[pl.ds((2 * p + half) * W, W), :]


def total(part):
    dma = pltpu.SemaphoreType.DMA
    return pl.pallas_call(
        total_kernel,
        out_shape=jax.ShapeDtypeStruct((2, W, W), F32),
        in_specs=[pl.BlockSpec(memory_space=pltpu.VMEM)],
        out_specs=pl.BlockSpec(memory_space=pltpu.VMEM),
        scratch_shapes=[
            VMEM((1024, H), F32),
            VMEM((512, H), F32),
            VMEM((512, H), F32),
            VMEM((3, 128, H), F32),
            VMEM((128, H), F32),
            VMEM((15, 8, H), F32),
            dma((2,)), dma((2,)), dma((6,)), dma((6,)), dma((30,)), dma((30,)),
        ],
        compiler_params=pltpu.CompilerParams(collective_id=0, has_side_effects=True),
        name="total",
    )(part)


def fold_kernel(tile, right, below_l, below_r, out):
    out[:, :, W:] = tile[:, :, W:]
    out[:, :, :W] = tile[:, :, :W] + right[...]

    @pl.when(pl.program_id(0) < 2)
    def _():
        out[:, :, :W] += below_l[...]
        out[:, :, W:] += below_r[...]


def fold(tile, right, below_l, below_r):
    rows = lambda i: (0, i, 0)
    upper = lambda i: (0, jnp.minimum(i, 1), 0)
    return pl.pallas_call(
        fold_kernel,
        grid=(4,),
        out_shape=jax.ShapeDtypeStruct((2, 512, 512), F32),
        in_specs=[
            pl.BlockSpec((2, 128, 512), rows),
            pl.BlockSpec((2, 128, 256), rows),
            pl.BlockSpec((2, 128, 256), upper),
            pl.BlockSpec((2, 128, 256), upper),
        ],
        out_specs=pl.BlockSpec((2, 128, 512), rows),
        name="fold",
    )(tile, right, below_l, below_r)


def from_behind(value, axis, steps):
    count = lax.axis_size(axis)
    initial, last = (max(0, -steps), min(count, count - steps))
    return lax.ppermute(value, axis, [(source, source + steps) for source in range(initial, last)])


def on_device(object_tile, probe, amplitudes, positions, counts):
    right = from_behind(object_tile[:, :, :W], "col", -1)
    below_l = from_behind(object_tile[:, :W, :W], "row", -1)
    below_r = from_behind(object_tile[:, :W, W:], "row", -1)
    corner = from_behind(below_l, "col", -1)
    amps = reorder(amplitudes[0, 0])
    count = lax.dynamic_slice(counts[0], (lax.axis_index("col"),), (1,))
    g_tile, g_right, g_below_l, g_below_r, g_corner, part = run_slots(
        positions[0, 0], count, object_tile, right, below_l, below_r, corner, amps, probe
    )
    to_corner = from_behind(g_corner, "col", 1)
    to_below_r = from_behind(g_below_r, "row", 1)
    to_right = from_behind(g_right, "col", 1)
    to_below_l = from_behind(g_below_l + to_corner, "row", 1)
    probe_grad = total(part)
    return (fold(g_tile, to_right, to_below_l, to_below_r), probe_grad)


def solution(mesh):
    in_specs = (
        P(None, "row", "col"),
        P(),
        P("row", "col", None, None, None),
        P("row", "col", None, None),
        P("row", None),
    )
    out_specs = (P(None, "row", "col"), P())
    return jax.shard_map(
        on_device, mesh=mesh, in_specs=in_specs, out_specs=out_specs, check_vma=False
    )
```

```python
import functools
import math

import jax
import jax.numpy as jnp
import numpy as np
from jax import lax
from jax.experimental import pallas as pl
from jax.experimental.pallas import tpu as pltpu
from jax.sharding import PartitionSpec as P

smooth_term = 0.01
F32 = jnp.float32
BF16 = jnp.bfloat16
W = 256
H = 128
CH = 32
VMEM = pltpu.VMEM


def split_table(table):
    high = table.astype(jnp.bfloat16)
    low = (table - high.astype(np.float64)).astype(jnp.bfloat16)
    return high, low


def half_tables():
    n = np.arange(H)
    even = np.exp(-2j * np.pi * np.outer(n, n) / H) / 16.0
    odd = np.exp(-2j * np.pi * n / W)[:, None] * even

    def real_form(z):
        return np.block([[z.real, z.imag], [-z.imag, z.real]])

    return real_form(even), real_form(odd), real_form(even.conj().T), real_form(odd.conj().T)


def tables():
    even, odd, inv_even, inv_odd = half_tables()
    right, left = [], []
    for table in (even, odd, inv_even, inv_odd):
        high, low = split_table(table)
        right.append(np.concatenate([high, high, low], axis=0))
        high, low = split_table(table.T)
        left.append(np.concatenate([high, high, low], axis=1))
    return np.stack(right), np.stack(left)


def high_low(value):
    high = value.astype(BF16)
    return high, (value - high.astype(F32)).astype(BF16)


def put_cols(ref, rows, half, value):
    high, low = high_low(value)
    at = H * half
    ref[rows, at : at + H] = high
    ref[rows, W + at : W + at + H] = low
    ref[rows, 2 * W + at : 2 * W + at + H] = high


def put_rows(ref, row, cols, value):
    high, low = high_low(value)
    count = value.shape[0]
    ref[row : row + count, cols] = high
    ref[W + row : W + row + count, cols] = low
    ref[2 * W + row : 2 * W + row + count, cols] = high


def dot(a, b):
    return jnp.dot(a, b, preferred_element_type=F32)


def slot_work(r, c, ext, gext, probe, amp, right_t, left_t, win, xe, xo, ye, yo, ve, vo, pgrad):
    j0 = lax.shift_right_logical(c, 7)
    s = lax.bitwise_and(c, 127)
    back_shift = lax.bitwise_and(128 - s, 127)
    lane = lax.broadcasted_iota(jnp.int32, (CH, H), 1)
    first = lane < 128 - s
    for i in range(W // CH):
        rows = pl.ds(i * CH, CH)
        parts = []
        for p in range(2):
            t = [
                pltpu.roll(ext[p, j0 + q, pl.ds(r + i * CH, CH), :], back_shift, 1)
                for q in range(3)
            ]
            a = jnp.where(first, t[0], t[1])
            b = jnp.where(first, t[1], t[2])
            win[p, rows, 0:H] = a
            win[p, rows, H:W] = b
            parts.append((a, b))
        (are, bre), (aim, bim) = parts
        pra, prb = probe[0, rows, 0:H], probe[0, rows, H:W]
        pia, pib = probe[1, rows, 0:H], probe[1, rows, H:W]
        ea_re = pra * are - pia * aim
        ea_im = pra * aim + pia * are
        eb_re = prb * bre - pib * bim
        eb_im = prb * bim + pib * bre
        put_cols(xe, rows, 0, ea_re + eb_re)
        put_cols(xe, rows, 1, ea_im + eb_im)
        put_cols(xo, rows, 0, ea_re - eb_re)
        put_cols(xo, rows, 1, ea_im - eb_im)
    ye[...] = dot(xe[...], right_t[0])
    yo[...] = dot(xo[...], right_t[1])
    for i in range(H // CH):
        top = pl.ds(i * CH, CH)
        bot = pl.ds(H + i * CH, CH)
        for half, y in ((0, ye), (1, yo)):
            cols = pl.ds(H * half, H)
            for part in range(2):
                t, b = y[top, H * part : H * part + H], y[bot, H * part : H * part + H]
                put_rows(ve, H * part + i * CH, cols, t + b)
                put_rows(vo, H * part + i * CH, cols, t - b)
    ye[...] = dot(left_t[0], ve[...])
    yo[...] = dot(left_t[1], vo[...])
    for i in range(H // CH):
        for half, y, v in ((0, ye, ve), (1, yo, vo)):
            re = y[pl.ds(i * CH, CH), :]
            im = y[pl.ds(H + i * CH, CH), :]
            a = amp[pl.ds(H * half + i * CH, CH), :]
            f = 2.0 - (2.0 * a) * lax.rsqrt(re * re + im * im + smooth_term)
            put_rows(v, i * CH, slice(None), f * re)
            put_rows(v, H + i * CH, slice(None), f * im)
    ye[...] = dot(left_t[2], ve[...])
    yo[...] = dot(left_t[3], vo[...])
    for i in range(H // CH):
        for part in range(2):
            e = ye[pl.ds(H * part + i * CH, CH), :]
            o = yo[pl.ds(H * part + i * CH, CH), :]
            for at, value in ((0, e + o), (H, e - o)):
                rows = pl.ds(at + i * CH, CH)
                put_cols(xe, rows, part, value[:, 0:H])
                put_cols(xo, rows, part, value[:, H:W])
    ye[...] = dot(xe[...], right_t[2])
    yo[...] = dot(xo[...], right_t[3])
    later = lane >= s
    for i in range(W // CH):
        rows = pl.ds(i * CH, CH)
        e_re, e_im = ye[rows, 0:H], ye[rows, H:W]
        o_re, o_im = yo[rows, 0:H], yo[rows, H:W]
        terms = []
        for cols, b_re, b_im in ((slice(0, H), e_re + o_re, e_im + o_im), (slice(H, W), e_re - o_re, e_im - o_im)):
            pr, pi = probe[0, rows, cols], probe[1, rows, cols]
            wr, wi = win[0, rows, cols], win[1, rows, cols]
            at = cols.start * 2 + i * CH
            pgrad[at : at + CH, :] += wr * b_re + wi * b_im
            pgrad[2 * W + at : 2 * W + at + CH, :] += wr * b_im - wi * b_re
            terms.append((pr * b_re + pi * b_im, pr * b_im - pi * b_re))
        for p in range(2):
            ra = pltpu.roll(terms[0][p], s, 1)
            rb = pltpu.roll(terms[1][p], s, 1)
            at = pl.ds(r + i * CH, CH)
            gext[p, j0, at, :] += jnp.where(later, ra, 0.0)
            gext[p, j0 + 1, at, :] += jnp.where(later, rb, ra)
            gext[p, j0 + 2, at, :] += jnp.where(later, 0.0, rb)


def slots_kernel(
    pos, cnt, tile, right, below_l, below_r, corner, amps, probe, right_t, left_t,
    g_tile, g_right, g_below_l, g_below_r, g_corner, pgrad,
    ext, gext, amp_buf, win, xe, xo, ye, yo, ve, vo, in_sem, amp_sem, out_sem,
):
    def pieces(arrays, buf):
        t, rt, bl, br, cn = arrays
        out = []
        for j in range(4):
            out.append((t.at[:, :, pl.ds(H * j, H)], buf.at[:, j, pl.ds(0, 512), :]))
        for j in range(2):
            cols = pl.ds(H * j, H)
            out.append((rt.at[:, :, cols], buf.at[:, 4 + j, pl.ds(0, 512), :]))
            out.append((bl.at[:, :, cols], buf.at[:, j, pl.ds(512, 256), :]))
            out.append((br.at[:, :, cols], buf.at[:, 2 + j, pl.ds(512, 256), :]))
            out.append((cn.at[:, :, cols], buf.at[:, 4 + j, pl.ds(512, 256), :]))
        return out

    def amp_copy(k, slot):
        return pltpu.make_async_copy(amps.at[k], amp_buf.at[slot], amp_sem.at[slot])

    loads = [
        pltpu.make_async_copy(hbm, vm, in_sem.at[n])
        for n, (hbm, vm) in enumerate(pieces((tile, right, below_l, below_r, corner), ext))
    ]
    for copy in loads:
        copy.start()
    count = cnt[0]

    @pl.when(count > 0)
    def _():
        amp_copy(0, 0).start()

    gext[...] = jnp.zeros_like(gext)
    pgrad[...] = jnp.zeros_like(pgrad)
    for copy in loads:
        copy.wait()

    def body(k, _):
        slot = lax.bitwise_and(k, 1)

        @pl.when(k + 1 < count)
        def _():
            amp_copy(k + 1, 1 - slot).start()

        amp_copy(k, slot).wait()
        slot_work(
            pos[k, 0], pos[k, 1], ext, gext, probe, amp_buf.at[slot], right_t, left_t,
            win, xe, xo, ye, yo, ve, vo, pgrad,
        )
        return 0

    lax.fori_loop(0, count, body, 0)
    stores = [
        pltpu.make_async_copy(vm, hbm, out_sem.at[n])
        for n, (hbm, vm) in enumerate(pieces((g_tile, g_right, g_below_l, g_below_r, g_corner), gext))
    ]
    for copy in stores:
        copy.start()
    for copy in stores:
        copy.wait()


def run_slots(own_pos, count, tile, right, below_l, below_r, corner, amps, probe):
    right_t, left_t = tables()
    any_spec = pl.BlockSpec(memory_space=pl.ANY)
    vmem = pl.BlockSpec(memory_space=pltpu.VMEM)
    smem = pl.BlockSpec(memory_space=pltpu.SMEM)
    block = lambda *shape: jax.ShapeDtypeStruct(shape, F32)
    return pl.pallas_call(
        slots_kernel,
        out_shape=(
            block(2, 512, 512), block(2, 512, 256), block(2, 256, 256), block(2, 256, 256),
            block(2, 256, 256), block(4 * W, H),
        ),
        in_specs=[smem, smem] + [any_spec] * 6 + [vmem] * 3,
        out_specs=tuple([any_spec] * 5 + [vmem]),
        scratch_shapes=[
            VMEM((2, 6, 768, H), F32),
            VMEM((2, 6, 768, H), F32),
            VMEM((2, W, W), F32),
            VMEM((2, W, W), F32),
            VMEM((W, 3 * W), BF16),
            VMEM((W, 3 * W), BF16),
            VMEM((W, W), F32),
            VMEM((W, W), F32),
            VMEM((3 * W, W), BF16),
            VMEM((3 * W, W), BF16),
            pltpu.SemaphoreType.DMA((12,)),
            pltpu.SemaphoreType.DMA((2,)),
            pltpu.SemaphoreType.DMA((12,)),
        ],
        compiler_params=pltpu.CompilerParams(vmem_limit_bytes=48 * 1024 * 1024),
        name="slots",
    )(own_pos, count, tile, right, below_l, below_r, corner, amps, probe, jnp.asarray(right_t), jnp.asarray(left_t))


MESH = pl.DeviceIdType.MESH
N_ROW, N_COL = 8, 16
SEAM = 7
HEAD = 64
AHEAD_Y, BACK_Y = 0, 3
ANY = pl.ANY


def place():
    row, col = lax.axis_index("row"), lax.axis_index("col")
    z, x_lo = row // 2, row % 2
    x_hi, y, core = col // 8, (col // 2) % 4, col % 2
    return row, col, x_hi * 2 + x_lo, y, z, core


def at_chip(x, y, z, core):
    return (z * 2 + x % 2, (x // 2) * 8 + y * 2 + core)


def remote(src, dst, sems, n, device):
    return pltpu.make_async_remote_copy(
        src_ref=src, dst_ref=dst, send_sem=sems[0].at[n], recv_sem=sems[1].at[n],
        device_id=device, device_id_type=MESH,
    )


def block(start, count):
    return pl.ds(pl.multiple_of(start, 8), count)


def greet(devices):
    barrier = pltpu.get_barrier_semaphore()
    for device in devices:
        pl.semaphore_signal(barrier, inc=1, device_id=device, device_id_type=MESH)
    return barrier


def back_kernel(
    g_tile, g_right, g_below_l, g_below_r, g_corner, part, out, out_p,
    corner_in, right_in, below_l_in, below_r_in, seam_in, relay_in, below_sum,
    full, got0, acc0, got1, acc1, got2,
    h_send, h_recv, m_send, m_recv, p_send, p_recv, x_send, x_recv,
):
    row, col, x, y, z, core = place()
    down, up = ((row + 1) % N_ROW, col), ((row + N_ROW - 1) % N_ROW, col)
    right, left = (row, (col + 1) % N_COL), (row, (col + N_COL - 1) % N_COL)
    mate = (row, col + 1 - 2 * core)
    group = z * 4 + y

    def group_peer(q):
        return (group + q) % 16

    def group_id(q):
        n = group_peer(q)
        return at_chip(x, n % 4, n // 4, core)

    def x_id(q):
        return at_chip((x + q) % 4, y, z, core)

    at_seam, past_seam = col == SEAM, col == SEAM + 1
    x_plus, x_minus = (x + 1) % 4, (x + 3) % 4
    is_relay = (y == BACK_Y) & (core == x // 2)
    has_down, has_up = row < N_ROW - 1, row > 0
    sends_right = (col < N_COL - 1) & (col != SEAM)
    gets_left = (col > 0) & (col != SEAM + 1)
    relay_plus = at_chip(x_plus, BACK_Y, z, x_plus // 2)
    relay_minus = at_chip(x_minus, BACK_Y, z, x_minus // 2)
    serves_upper = (x == 1) | (x == 2)
    relay_source = at_chip(jnp.where(serves_upper, x_minus, x_plus), 3, z, 1)
    relay_dest = at_chip(jnp.where(serves_upper, x_plus, x_minus), 0, z, 0)
    diagonal = ((row + 1) % N_ROW, SEAM + 1)
    diagonal_from = ((row + N_ROW - 1) % N_ROW, SEAM)

    barrier = greet([mate, down, up, left, right] + [group_id(q) for q in range(1, 16)] + [x_id(q) for q in range(1, 4)])

    @pl.when(at_seam)
    def _():
        greet([relay_plus, relay_minus, diagonal])

    @pl.when(past_seam)
    def _():
        greet([relay_plus, relay_minus, diagonal_from])

    @pl.when(is_relay)
    def _():
        greet([relay_source, relay_dest])

    extra = jnp.where(at_seam | past_seam, 3, 0) + jnp.where(is_relay, 2, 0)
    pl.semaphore_wait(barrier, 23 + extra)

    halo = (h_send, h_recv)
    corner = remote(g_corner, corner_in, halo, 0, right)
    below_r = remote(g_below_r, below_r_in, halo, 1, down)
    cols = remote(g_right, right_in, halo, 2, right)
    head, tail = pl.ds(0, HEAD), pl.ds(HEAD, W - HEAD)
    below_l = remote(below_sum.at[:, head, :], below_l_in.at[:, head, :], halo, 3, down)
    below_l2 = remote(below_sum.at[:, tail, :], below_l_in.at[:, tail, :], halo, 9, down)
    seam_corner = remote(g_corner, seam_in, halo, 4, diagonal)
    upper, lower = pl.ds(0, W), pl.ds(W, W)
    to_plus = remote(g_right.at[:, upper, :], relay_in, halo, 5, relay_plus)
    to_minus = remote(g_right.at[:, lower, :], relay_in, (h_send, h_recv), 6, relay_minus)
    relay_upper = remote(relay_in, right_in.at[:, upper, :], halo, 7, relay_dest)
    relay_lower = remote(relay_in, right_in.at[:, lower, :], halo, 8, relay_dest)

    def when(cond, *actions):
        @pl.when(cond)
        def _():
            for action in actions:
                action()

    when(at_seam, to_plus.start, to_minus.start)
    when(at_seam & has_down, seam_corner.start)
    when(sends_right, corner.start)
    when(has_down, below_r.start)
    swap = remote(part.at[block((1 - core) * 512, 512)], got0, (m_send, m_recv), 0, mate)
    swap.start()
    swap.wait()
    acc0[...] = part[block(core * 512, 512), :] + got0[...]
    spread = [
        remote(acc0.at[block(group_peer(q) * 32, 32)], got1.at[q - 1], (p_send, p_recv), q - 1, group_id(q))
        for q in range(1, 16)
    ]
    for copy in spread:
        copy.start()
    when(sends_right, corner.wait_send, cols.start)
    when(is_relay & serves_upper, to_plus.wait_recv, relay_upper.start)
    when(is_relay & jnp.logical_not(serves_upper), to_minus.wait_recv, relay_lower.start)
    below_sum[...] = g_below_l[...]

    @pl.when(gets_left)
    def _():
        corner.wait_recv()
        below_sum[...] += corner_in[...]

    for copy in spread:
        copy.wait()
    total = acc0[block(group * 32, 32), :]
    for q in range(15):
        total = total + got1[q]
    acc1[...] = total
    spread = [
        remote(acc1.at[block((x + q) % 4 * 8, 8)], got2.at[q - 1], (x_send, x_recv), q - 1, x_id(q))
        for q in range(1, 4)
    ]
    for copy in spread:
        copy.start()
    when(has_down, below_l.start)
    for copy in spread:
        copy.wait()
    base1 = core * 512 + group * 32
    own = block(base1 + x * 8, 8)
    full[own, :] = acc1[block(x * 8, 8), :] + got2[0] + got2[1] + got2[2]

    def gather(copies):
        for copy in copies:
            copy.start()
        for copy in copies:
            copy.wait()

    spread = [remote(full.at[own], full.at[own], (x_send, x_recv), 2 + q, x_id(q)) for q in range(1, 4)]
    for copy in spread:
        copy.start()
    when(has_down, below_l2.start)
    for copy in spread:
        copy.wait()
    own1 = block(base1, 32)
    gather([remote(full.at[own1], full.at[own1], (p_send, p_recv), 14 + q, group_id(q)) for q in range(1, 16)])
    own0 = block(core * 512, 512)
    gather([remote(full.at[own0], full.at[own0], (m_send, m_recv), 1, mate)])
    for p in range(2):
        for half in range(2):
            out_p[p, :, pl.ds(H * half, H)] = full[pl.ds((2 * p + half) * W, W), :]

    out[...] = g_tile[...]

    @pl.when(has_up)
    def _():
        below_r.wait_recv()
        out[:, :W, W:] += below_r_in[...]
        below_l.wait_recv()
        below_l2.wait_recv()
        out[:, :W, :W] += below_l_in[...]

    @pl.when(gets_left)
    def _():
        cols.wait_recv()
        out[:, :, :W] += right_in[...]

    @pl.when(past_seam)
    def _():
        relay_upper.wait_recv()
        relay_lower.wait_recv()
        out[:, :, :W] += right_in[...]

    @pl.when(past_seam & has_up)
    def _():
        seam_corner.wait_recv()
        out[:, :W, :W] += seam_in[...]

    when(sends_right, cols.wait_send)
    when(has_down, below_r.wait_send, below_l.wait_send, below_l2.wait_send)
    when(at_seam, to_plus.wait_send, to_minus.wait_send)
    when(at_seam & has_down, seam_corner.wait_send)
    when(is_relay & serves_upper, relay_upper.wait_send)
    when(is_relay & jnp.logical_not(serves_upper), relay_lower.wait_send)


def back(g_tile, g_right, g_below_l, g_below_r, g_corner, part):
    dma = pltpu.SemaphoreType.DMA
    vmem = pl.BlockSpec(memory_space=pltpu.VMEM)
    square = VMEM((2, W, W), F32)
    return pl.pallas_call(
        back_kernel,
        out_shape=(jax.ShapeDtypeStruct((2, 512, 512), F32), jax.ShapeDtypeStruct((2, W, W), F32)),
        in_specs=[vmem] * 6,
        out_specs=(vmem, vmem),
        scratch_shapes=[
            square, VMEM((2, 512, W), F32), square, square, square, square, square,
            VMEM((1024, H), F32), VMEM((512, H), F32), VMEM((512, H), F32),
            VMEM((15, 32, H), F32), VMEM((32, H), F32), VMEM((3, 8, H), F32),
            dma((10,)), dma((10,)), dma((2,)), dma((2,)), dma((30,)), dma((30,)), dma((6,)), dma((6,)),
        ],
        compiler_params=pltpu.CompilerParams(
            collective_id=1, has_side_effects=True, vmem_limit_bytes=40 * 1024 * 1024
        ),
        name="back",
    )(g_tile, g_right, g_below_l, g_below_r, g_corner, part)


def ahead_kernel(
    tile, amps, select_t, right, below_l, below_r, corner, amps_out,
    relay_in, amp_buf, h_send, h_recv, a_sem,
):
    row, col, x, y, z, core = place()
    down, up = ((row + 1) % N_ROW, col), ((row + N_ROW - 1) % N_ROW, col)
    to_right, to_left = (row, (col + 1) % N_COL), (row, (col + N_COL - 1) % N_COL)
    at_seam, past_seam = col == SEAM, col == SEAM + 1
    is_relay = (y == AHEAD_Y) & (core == x // 2)
    has_down, has_up = row < N_ROW - 1, row > 0
    sends_left = (col > 0) & (col != SEAM + 1)
    gets_right = (col < N_COL - 1) & (col != SEAM)
    x_plus, x_minus = (x + 1) % 4, (x + 3) % 4
    relay_plus, relay_minus = at_chip(x_plus, AHEAD_Y, z, x_plus // 2), at_chip(x_minus, AHEAD_Y, z, x_minus // 2)
    serves_upper = (x == 3) | (x == 0)
    relay_source = at_chip(jnp.where(serves_upper, x_minus, x_plus), 0, z, 0)
    relay_dest = at_chip(jnp.where(serves_upper, x_plus, x_minus), 3, z, 1)

    def when(cond, *actions):
        @pl.when(cond)
        def _():
            for action in actions:
                action()

    halves = [
        pltpu.make_async_copy(amps.at[:, :, pl.ds(H * n, H)], amp_buf.at[:, n], a_sem.at[n])
        for n in range(2)
    ]
    for copy in halves:
        copy.start()
    barrier = greet([down, up, to_left, to_right])

    @pl.when(past_seam)
    def _():
        greet([relay_plus, relay_minus, ((row + N_ROW - 1) % N_ROW, SEAM)])

    @pl.when(at_seam)
    def _():
        greet([relay_plus, relay_minus, ((row + 1) % N_ROW, SEAM + 1)])

    @pl.when(is_relay)
    def _():
        greet([relay_source, relay_dest])

    extra = jnp.where(at_seam | past_seam, 3, 0) + jnp.where(is_relay, 2, 0)
    pl.semaphore_wait(barrier, 4 + extra)

    halo = (h_send, h_recv)
    upper, lower, every = pl.ds(0, W), pl.ds(W, W), pl.ds(0, 512)
    first, last = pl.ds(0, W), pl.ds(W, W)
    cols = remote(tile.at[:, every, first], right, halo, 0, to_left)
    rows_l = remote(tile.at[:, upper, first], below_l, halo, 1, up)
    rows_r = remote(tile.at[:, upper, last], below_r, halo, 2, up)
    on_left = remote(below_l, corner, halo, 3, to_left)
    seam_corner = remote(tile.at[:, upper, first], corner, halo, 4, ((row + N_ROW - 1) % N_ROW, SEAM))
    to_plus = remote(tile.at[:, upper, first], relay_in, halo, 5, relay_plus)
    to_minus = remote(tile.at[:, lower, first], relay_in, halo, 6, relay_minus)
    relay_upper = remote(relay_in, right.at[:, upper, :], halo, 7, relay_dest)
    relay_lower = remote(relay_in, right.at[:, lower, :], halo, 8, relay_dest)

    when(past_seam, to_plus.start, to_minus.start)
    when(past_seam & has_up, seam_corner.start)
    when(has_up, rows_l.start)
    when(sends_left, cols.start)
    when(has_up & jnp.logical_not(is_relay), rows_r.start)
    for copy in halves:
        copy.wait()

    def reorder_slot(k, _):
        half = jnp.concatenate(
            [
                jnp.concatenate([amp_buf[k, n, pl.ds(start, H, stride=2), :] for n in range(2)], axis=1)
                for start in range(2)
            ],
            axis=0,
        )
        high, mid = high_low(half)
        low = (half - high.astype(F32) - mid.astype(F32)).astype(BF16)
        amps_out[k] = dot(jnp.concatenate([high, mid, low], axis=1), select_t[...])
        return 0

    lax.fori_loop(0, amps.shape[0], reorder_slot, 0)
    when(is_relay & serves_upper, to_plus.wait_recv, relay_upper.start)
    when(is_relay & jnp.logical_not(serves_upper), to_minus.wait_recv, relay_lower.start)
    when(is_relay & has_up, rows_r.start)
    when(has_down, rows_l.wait_recv)
    when(has_down & sends_left, on_left.start)
    when(has_down, rows_r.wait_recv)
    when(gets_right, cols.wait_recv)
    when(at_seam, relay_upper.wait_recv, relay_lower.wait_recv)
    when(gets_right & has_down, on_left.wait_recv)
    when(at_seam & has_down, seam_corner.wait_recv)
    when(sends_left, cols.wait_send)
    when(has_up, rows_l.wait_send, rows_r.wait_send)
    when(has_down & sends_left, on_left.wait_send)
    when(past_seam, to_plus.wait_send, to_minus.wait_send)
    when(past_seam & has_up, seam_corner.wait_send)
    when(is_relay & serves_upper, relay_upper.wait_send)
    when(is_relay & jnp.logical_not(serves_upper), relay_lower.wait_send)


def ahead(tile, amps):
    n = np.arange(H)
    select = np.zeros((W, W), np.float32)
    select[2 * n, n] = 1.0
    select[2 * n + 1, H + n] = 1.0
    select = jnp.asarray(np.concatenate([select] * 3, axis=0).astype(jnp.bfloat16))
    dma = pltpu.SemaphoreType.DMA
    vmem = pl.BlockSpec(memory_space=pltpu.VMEM)
    any_spec = pl.BlockSpec(memory_space=pl.ANY)
    square = jax.ShapeDtypeStruct((2, W, W), F32)
    return pl.pallas_call(
        ahead_kernel,
        out_shape=(jax.ShapeDtypeStruct((2, 512, W), F32), square, square, square, jax.ShapeDtypeStruct(amps.shape, F32)),
        in_specs=[any_spec, any_spec, vmem],
        out_specs=(any_spec, any_spec, any_spec, any_spec, vmem),
        scratch_shapes=[VMEM((2, W, W), F32), VMEM((amps.shape[0], 2, W, H), F32), dma((9,)), dma((9,)), dma((2,))],
        compiler_params=pltpu.CompilerParams(
            collective_id=0, has_side_effects=True, vmem_limit_bytes=40 * 1024 * 1024
        ),
        name="ahead",
    )(tile, amps, select)


def on_device(object_tile, probe, amplitudes, positions, counts):
    right, below_l, below_r, corner, amps = ahead(object_tile, amplitudes[0, 0])
    count = lax.dynamic_slice(counts[0], (lax.axis_index("col"),), (1,))
    g_tile, g_right, g_below_l, g_below_r, g_corner, part = run_slots(
        positions[0, 0], count, object_tile, right, below_l, below_r, corner, amps, probe
    )
    return back(g_tile, g_right, g_below_l, g_below_r, g_corner, part)


def solution(mesh):
    in_specs = (
        P(None, "row", "col"),
        P(),
        P("row", "col", None, None, None),
        P("row", "col", None, None),
        P("row", None),
    )
    out_specs = (P(None, "row", "col"), P())
    return jax.shard_map(
        on_device, mesh=mesh, in_specs=in_specs, out_specs=out_specs, check_vma=False
    )
```

```python
import math

import jax
import jax.numpy as jnp
import numpy as np
from jax import lax
from jax.experimental import pallas as pl
from jax.experimental.pallas import tpu as pltpu
from jax.sharding import PartitionSpec as P

smooth_term = 0.01
F32 = jnp.float32
BF16 = jnp.bfloat16
W = 256
H = 128
T = 512
CH = 32
TILES = 6
VMEM = pltpu.VMEM
MESH = pl.DeviceIdType.MESH
N_ROW, N_COL = 8, 16
SEAM = 7
AHEAD_Y, BACK_Y = 0, 3
EXT = (2, TILES, T + W, H)
MIB = 1024 * 1024


def tables():
    n = np.arange(H)
    even = np.exp(-2j * np.pi * np.outer(n, n) / H) / math.sqrt(W)
    odd = np.exp(-2j * np.pi * n / W)[:, None] * even

    def real_form(z):
        return np.block([[z.real, z.imag], [-z.imag, z.real]])

    pair = [real_form(even), real_form(odd)]
    return np.stack(pair + [table.T for table in pair]).astype(np.float32)


def high_low(value):
    high = value.astype(BF16)
    return high, (value - high.astype(F32)).astype(BF16)


def put(ref, rows, cols, value):
    ref[0, rows, cols], ref[1, rows, cols] = high_low(value)


def dot(a, b):
    return jnp.dot(a, b, preferred_element_type=F32)


def by_right(x, t, n):
    return dot(x[0], t[n, 0]) + dot(x[1], t[n, 0]) + dot(x[0], t[n, 1])


def by_left(x, t, n):
    return dot(t[n, 0], x[0]) + dot(t[n, 0], x[1]) + dot(t[n, 1], x[0])


def slot_steps(r, c, live, ext, gext, probe, amp, t, win, xe, xo, ye, yo, pgrad):
    j0 = lax.shift_right_logical(c, 7)
    s = lax.bitwise_and(c, 127)
    back_shift = lax.bitwise_and(128 - s, 127)
    lane = lax.broadcasted_iota(jnp.int32, (CH, H), 1)
    first = lane < 128 - s
    left, right, both = pl.ds(0, H), pl.ds(H, H), pl.ds(0, W)
    for i in range(W // CH):
        rows = pl.ds(i * CH, CH)
        parts = []
        for p in range(2):
            q = [
                pltpu.roll(ext[p, j0 + n, pl.ds(r + i * CH, CH), :], back_shift, 1)
                for n in range(3)
            ]
            a = jnp.where(first, q[0], q[1])
            b = jnp.where(first, q[1], q[2])
            win[p, rows, left] = a
            win[p, rows, right] = b
            parts.append((a, b))
        (are, bre), (aim, bim) = parts
        pra, prb = probe[0, rows, left], probe[0, rows, right]
        pia, pib = probe[1, rows, left], probe[1, rows, right]
        ea_re = pra * are - pia * aim
        ea_im = pra * aim + pia * are
        eb_re = prb * bre - pib * bim
        eb_im = prb * bim + pib * bre
        put(xe, rows, left, ea_re + eb_re)
        put(xe, rows, right, ea_im + eb_im)
        put(xo, rows, left, ea_re - eb_re)
        put(xo, rows, right, ea_im - eb_im)
    yield
    ye[...] = by_right(xe, t, 0)
    yo[...] = by_right(xo, t, 1)
    yield
    for i in range(H // CH):
        top = pl.ds(i * CH, CH)
        bot = pl.ds(H + i * CH, CH)
        for cols, y in ((left, ye), (right, yo)):
            for part, lanes in ((0, left), (H, right)):
                a, b = y[top, lanes], y[bot, lanes]
                put(xe, pl.ds(part + i * CH, CH), cols, a + b)
                put(xo, pl.ds(part + i * CH, CH), cols, a - b)
    yield
    ye[...] = by_left(xe, t, 2)
    yo[...] = by_left(xo, t, 3)
    yield
    for i in range(H // CH):
        for at, y, x in ((0, ye, xe), (H, yo, xo)):
            re = y[pl.ds(i * CH, CH), :]
            im = y[pl.ds(H + i * CH, CH), :]
            a = amp[pl.ds(at + i * CH, CH), :]
            f = (2.0 - (2.0 * a) * lax.rsqrt(re * re + im * im + smooth_term)) * live
            put(x, pl.ds(i * CH, CH), both, f * re)
            put(x, pl.ds(H + i * CH, CH), both, f * im)
    yield
    ye[...] = by_left(xe, t, 0)
    yo[...] = by_left(xo, t, 1)
    yield
    for i in range(H // CH):
        for part, lanes in ((0, left), (H, right)):
            e = ye[pl.ds(part + i * CH, CH), :]
            o = yo[pl.ds(part + i * CH, CH), :]
            for at, value in ((0, e + o), (H, e - o)):
                rows = pl.ds(at + i * CH, CH)
                put(xe, rows, lanes, value[:, 0:H])
                put(xo, rows, lanes, value[:, H:W])
    yield
    ye[...] = by_right(xe, t, 2)
    yo[...] = by_right(xo, t, 3)
    yield
    later = lane >= s
    for i in range(W // CH):
        rows = pl.ds(i * CH, CH)
        e_re, e_im = ye[rows, left], ye[rows, right]
        o_re, o_im = yo[rows, left], yo[rows, right]
        terms = []
        for n, cols, b_re, b_im in ((0, left, e_re + o_re, e_im + o_im), (1, right, e_re - o_re, e_im - o_im)):
            pr, pi = probe[0, rows, cols], probe[1, rows, cols]
            wr, wi = win[0, rows, cols], win[1, rows, cols]
            pgrad[n, rows, :] += wr * b_re + wi * b_im
            pgrad[2 + n, rows, :] += wr * b_im - wi * b_re
            terms.append((pr * b_re + pi * b_im, pr * b_im - pi * b_re))
        for p in range(2):
            ra = pltpu.roll(terms[0][p], s, 1)
            rb = pltpu.roll(terms[1][p], s, 1)
            at = pl.ds(r + i * CH, CH)
            gext[p, j0, at, :] += jnp.where(later, ra, 0.0)
            gext[p, j0 + 1, at, :] += jnp.where(later, rb, ra)
            gext[p, j0 + 2, at, :] += jnp.where(later, 0.0, rb)
    yield


def interleave(streams, lag):
    waiting = [[stream, n * lag] for n, stream in enumerate(streams)]
    while waiting:
        for item in list(waiting):
            if item[1] > 0:
                item[1] -= 1
            elif next(item[0], waiting) is waiting:
                waiting.remove(item)


def slots_kernel(
    pos, counts, ext, amps, probe, table, gext, pgrad, amp_buf, t, win, xe, xo, ye, yo, amp_sem
):
    count = counts[0, lax.axis_index("col")]
    groups = lax.div(count + U - 1, U)

    def amp_copy(n, buf):
        return pltpu.make_async_copy(amps.at[pl.ds(U * n, U)], amp_buf.at[buf], amp_sem.at[buf])

    @pl.when(count > 0)
    def _():
        amp_copy(0, 0).start()

    gext[...] = jnp.zeros_like(gext)
    pgrad[...] = jnp.zeros_like(pgrad)
    for n in range(4):
        t[n, 0], t[n, 1] = high_low(table[n])

    def body(n, _):
        buf = lax.bitwise_and(n, 1)

        @pl.when(n + 1 < groups)
        def _():
            amp_copy(n + 1, 1 - buf).start()

        amp_copy(n, buf).wait()
        streams = []
        for u in range(U):
            k = U * n + u
            live = (k < count).astype(F32)
            streams.append(
                slot_steps(
                    pos[0, k], pos[1, k], live, ext, gext, probe, amp_buf.at[buf, u], t,
                    win.at[u], xe.at[u], xo.at[u], ye.at[u], yo.at[u], pgrad,
                )
            )
        interleave(streams, LAG)
        return 0

    lax.fori_loop(0, groups, body, 0)


LAG = 1
U = 4


def run_slots(own_pos, counts, ext, amps, probe):
    vmem = pl.BlockSpec(memory_space=pltpu.VMEM)
    smem = pl.BlockSpec(memory_space=pltpu.SMEM)
    return pl.pallas_call(
        slots_kernel,
        out_shape=(jax.ShapeDtypeStruct(EXT, F32), jax.ShapeDtypeStruct((4, W, H), F32)),
        in_specs=[smem, smem, vmem, pl.BlockSpec(memory_space=pl.ANY), vmem, vmem],
        out_specs=(vmem, vmem),
        scratch_shapes=[
            VMEM((2, U, W, W), F32),
            VMEM((4, 2, W, W), BF16),
            VMEM((U, 2, W, W), F32),
            VMEM((U, 2, W, W), BF16),
            VMEM((U, 2, W, W), BF16),
            VMEM((U, W, W), F32),
            VMEM((U, W, W), F32),
            pltpu.SemaphoreType.DMA((2,)),
        ],
        compiler_params=pltpu.CompilerParams(vmem_limit_bytes=40 * MIB),
        name="slots",
    )(own_pos, counts, ext, amps, probe, jnp.asarray(tables()))


def place():
    row, col = lax.axis_index("row"), lax.axis_index("col")
    z, x_lo = row // 2, row % 2
    x_hi, y, core = col // 8, (col // 2) % 4, col % 2
    return row, col, x_hi * 2 + x_lo, y, z, core


def at_chip(x, y, z, core):
    return (z * 2 + x % 2, (x // 2) * 8 + y * 2 + core)


def remote(src, dst, sems, n, device):
    return pltpu.make_async_remote_copy(
        src_ref=src, dst_ref=dst, send_sem=sems[0].at[n], recv_sem=sems[1].at[n],
        device_id=device, device_id_type=MESH,
    )


def block(start, count):
    return pl.ds(pl.multiple_of(start, 8), count)


def greet(devices):
    barrier = pltpu.get_barrier_semaphore()
    for device in devices:
        pl.semaphore_signal(barrier, inc=1, device_id=device, device_id_type=MESH)
    return barrier


def when(cond, *actions):
    @pl.when(cond)
    def _():
        for action in actions:
            action()


def area(ref, tile, row, rows):
    return ref.at[:, pl.ds(tile, 2), pl.ds(row, rows), :]


def back_kernel(
    gext, part, out, out_p, corner_in, right_in, below_l_in, below_r_in, seam_in, relay_in, below_sum,
    full, got0, acc0, got1, acc1, got2,
    h_send, h_recv, r_send, r_recv, m_send, m_recv, p_send, p_recv, x_send, x_recv,
):
    row, col, x, y, z, core = place()
    down, up = ((row + 1) % N_ROW, col), ((row + N_ROW - 1) % N_ROW, col)
    right, left = (row, (col + 1) % N_COL), (row, (col + N_COL - 1) % N_COL)
    mate = (row, col + 1 - 2 * core)
    pair, place_in_pair = (x + 1) // 2 % 2, x // 2
    near, far = place_in_pair * 4 + y, pair * 4 + z

    def near_peer(q):
        return (near + q) % 8

    def near_id(q):
        n = near_peer(q)
        return at_chip(pair + n // 4 * (3 - 2 * pair), n % 4, z, core)

    def far_peer(q):
        return (far + q) % 8

    def far_id(q):
        n = far_peer(q)
        return at_chip(n // 4 + place_in_pair * (3 - 2 * (n // 4)), y, n % 4, core)

    at_seam, past_seam = col == SEAM, col == SEAM + 1
    x_plus, x_minus = (x + 1) % 4, (x + 3) % 4
    is_relay = (y == BACK_Y) & (core == x // 2)
    has_down, has_up = row < N_ROW - 1, row > 0
    sends_right = (col < N_COL - 1) & (col != SEAM)
    gets_left = (col > 0) & (col != SEAM + 1)
    relay_plus = at_chip(x_plus, BACK_Y, z, x_plus // 2)
    relay_minus = at_chip(x_minus, BACK_Y, z, x_minus // 2)
    serves_upper = (x == 1) | (x == 2)
    relay_source = at_chip(jnp.where(serves_upper, x_minus, x_plus), 3, z, 1)
    relay_dest = at_chip(jnp.where(serves_upper, x_plus, x_minus), 0, z, 0)
    diagonal = ((row + 1) % N_ROW, SEAM + 1)
    diagonal_from = ((row + N_ROW - 1) % N_ROW, SEAM)

    barrier = greet([mate, down, up, left, right] + [near_id(q) for q in range(1, 8)] + [far_id(q) for q in range(1, 8)])

    @pl.when(at_seam)
    def _():
        greet([relay_plus, relay_minus, diagonal])

    @pl.when(past_seam)
    def _():
        greet([relay_plus, relay_minus, diagonal_from])

    @pl.when(is_relay)
    def _():
        greet([relay_source, relay_dest])

    extra = jnp.where(at_seam | past_seam, 3, 0) + jnp.where(is_relay, 2, 0)
    pl.semaphore_wait(barrier, 19 + extra)

    halo = (h_send, h_recv)
    corner = remote(area(gext, 4, T, W), corner_in, halo, 0, right)
    cols = remote(area(gext, 4, 0, W), area(right_in, 0, 0, W), halo, 1, right)
    cols2 = remote(area(gext, 4, W, W), area(right_in, 0, W, W), halo, 2, right)
    seam_corner = remote(area(gext, 4, T, W), seam_in, halo, 3, diagonal)
    to_plus = remote(area(gext, 4, 0, W), relay_in, halo, 4, relay_plus)
    to_minus = remote(area(gext, 4, W, W), relay_in, halo, 5, relay_minus)
    relay_upper = remote(relay_in, area(right_in, 0, 0, W), halo, 6, relay_dest)
    relay_lower = remote(relay_in, area(right_in, 0, W, W), halo, 7, relay_dest)
    pieces_r, pieces_l = [], []
    at = 0
    for n, rows in enumerate(PIECES_R):
        pieces_r.append(remote(area(gext, 2, T + at, rows), area(below_r_in, 0, at, rows), (r_send, r_recv), n, down))
        at += rows
    at = 0
    for n, rows in enumerate(PIECES_L):
        sems = (r_send, r_recv)
        pieces_l.append(remote(area(below_sum, 0, at, rows), area(below_l_in, 0, at, rows), sems, len(PIECES_R) + n, down))
        at += rows

    def start(copies):
        for copy in copies:
            copy.start()

    def wait(copies):
        for copy in copies:
            copy.wait()

    swap = remote(part.at[pl.ds(2 * (1 - core), 2)], got0, (m_send, m_recv), 0, mate)
    swap.start()
    when(at_seam, to_plus.start, to_minus.start)
    when(at_seam & has_down, seam_corner.start)
    when(sends_right, corner.start)
    when(has_down, pieces_r[0].start)
    swap.wait()
    for n in range(2):
        acc0[pl.ds(n * W, W), :] = part[2 * core + n] + got0[n]
    spread = [
        remote(acc0.at[block(near_peer(q) * 64, 64)], got1.at[q - 1], (p_send, p_recv), q - 1, near_id(q))
        for q in range(1, 8)
    ]
    start(spread)
    when(sends_right, cols.start)
    below_sum[...] = area(gext, 0, T, W)[...]

    @pl.when(gets_left)
    def _():
        corner.wait_recv()
        below_sum[...] += corner_in[...]

    wait(spread)
    total = acc0[block(near * 64, 64), :]
    for q in range(7):
        total = total + got1[q]
    acc1[...] = total
    when(is_relay & serves_upper, to_plus.wait_recv, relay_upper.start)
    when(is_relay & jnp.logical_not(serves_upper), to_minus.wait_recv, relay_lower.start)
    spread = [
        remote(acc1.at[block(far_peer(q) * 8, 8)], got2.at[q - 1], (x_send, x_recv), q - 1, far_id(q))
        for q in range(1, 8)
    ]
    start(spread)
    wait(spread)
    base1 = core * 512 + near * 64
    own = block(base1 + far * 8, 8)
    total = acc1[block(far * 8, 8), :]
    for q in range(7):
        total = total + got2[q]
    full[own, :] = total
    spread = [remote(full.at[own], full.at[own], (x_send, x_recv), 6 + q, far_id(q)) for q in range(1, 8)]
    start(spread)
    wait(spread)
    own1 = block(base1, 64)
    spread = [remote(full.at[own1], full.at[own1], (p_send, p_recv), 6 + q, near_id(q)) for q in range(1, 8)]
    start(spread)
    when(has_down, *[copy.start for copy in pieces_r[1:] + pieces_l])
    when(sends_right, cols2.start)
    for n in range(T // H):
        out[:, :, pl.ds(n * H, H)] = gext[:, n, pl.ds(0, T), :]
    wait(spread)
    own0 = block(core * 512, 512)
    swap = remote(full.at[own0], full.at[own0], (m_send, m_recv), 1, mate)
    swap.start()
    swap.wait()
    for p in range(2):
        for half in range(2):
            out_p[p, :, pl.ds(H * half, H)] = full[pl.ds((2 * p + half) * W, W), :]

    def add(value, rows, at):
        for n in range(2):
            out[:, pl.ds(0, rows), pl.ds((at + n) * H, H)] += value[:, n]

    @pl.when(has_up)
    def _():
        for copy in pieces_r:
            copy.wait_recv()
        add(below_r_in, W, 2)

    @pl.when(gets_left)
    def _():
        cols.wait_recv()
        cols2.wait_recv()
        add(right_in, T, 0)

    @pl.when(past_seam)
    def _():
        relay_upper.wait_recv()
        relay_lower.wait_recv()
        add(right_in, T, 0)

    @pl.when(has_up)
    def _():
        for copy in pieces_l:
            copy.wait_recv()
        add(below_l_in, W, 0)

    @pl.when(past_seam & has_up)
    def _():
        seam_corner.wait_recv()
        add(seam_in, W, 0)

    when(sends_right, corner.wait_send, cols.wait_send, cols2.wait_send)
    when(has_down, *[copy.wait_send for copy in pieces_r + pieces_l])
    when(at_seam, to_plus.wait_send, to_minus.wait_send)
    when(at_seam & has_down, seam_corner.wait_send)
    when(is_relay & serves_upper, relay_upper.wait_send)
    when(is_relay & jnp.logical_not(serves_upper), relay_lower.wait_send)


PIECES_R = (128, 128)
PIECES_L = (256,)


def back(gext, part):
    dma = pltpu.SemaphoreType.DMA
    vmem = pl.BlockSpec(memory_space=pltpu.VMEM)
    square = VMEM((2, 2, W, H), F32)
    return pl.pallas_call(
        back_kernel,
        out_shape=(jax.ShapeDtypeStruct((2, T, T), F32), jax.ShapeDtypeStruct((2, W, W), F32)),
        in_specs=[vmem, vmem],
        out_specs=(vmem, vmem),
        scratch_shapes=[
            square, VMEM((2, 2, T, H), F32), square, square, square, square, square,
            VMEM((4 * W, H), F32), VMEM((2, W, H), F32), VMEM((2 * W, H), F32),
            VMEM((7, 64, H), F32), VMEM((64, H), F32), VMEM((7, 8, H), F32),
            dma((8,)), dma((8,)), dma((3,)), dma((3,)), dma((2,)), dma((2,)), dma((14,)), dma((14,)), dma((14,)), dma((14,)),
        ],
        compiler_params=pltpu.CompilerParams(
            collective_id=1, has_side_effects=True, vmem_limit_bytes=40 * MIB
        ),
        name="back",
    )(gext, part)


def ahead_kernel(tile, amps, select_t, ext, amps_out, relay_in, amp_buf, h_send, h_recv, t_sem, a_sem):
    row, col, x, y, z, core = place()
    down, up = ((row + 1) % N_ROW, col), ((row + N_ROW - 1) % N_ROW, col)
    to_right, to_left = (row, (col + 1) % N_COL), (row, (col + N_COL - 1) % N_COL)
    at_seam, past_seam = col == SEAM, col == SEAM + 1
    has_down, has_up = row < N_ROW - 1, row > 0
    sends_left = (col > 0) & (col != SEAM + 1)
    gets_right = (col < N_COL - 1) & (col != SEAM)
    x_plus, x_minus = (x + 1) % 4, (x + 3) % 4
    is_relay = (y == AHEAD_Y) & (core == x // 2)
    relay_plus, relay_minus = at_chip(x_plus, AHEAD_Y, z, x_plus // 2), at_chip(x_minus, AHEAD_Y, z, x_minus // 2)
    serves_upper = (x == 3) | (x == 0)
    relay_source = at_chip(jnp.where(serves_upper, x_minus, x_plus), 0, z, 0)
    relay_dest = at_chip(jnp.where(serves_upper, x_plus, x_minus), 3, z, 1)

    lanes = [
        pltpu.make_async_copy(tile.at[:, :, pl.ds(H * n, H)], ext.at[:, n, pl.ds(0, T), :], t_sem.at[n])
        for n in range(T // H)
    ]
    halves = [
        pltpu.make_async_copy(amps.at[:, :, pl.ds(H * n, H)], amp_buf.at[:, n], a_sem.at[n])
        for n in range(2)
    ]
    for copy in lanes + halves:
        copy.start()
    barrier = greet([down, up, to_left, to_right])

    @pl.when(past_seam)
    def _():
        greet([relay_plus, relay_minus, ((row + N_ROW - 1) % N_ROW, SEAM)])

    @pl.when(at_seam)
    def _():
        greet([relay_plus, relay_minus, ((row + 1) % N_ROW, SEAM + 1)])

    @pl.when(is_relay)
    def _():
        greet([relay_source, relay_dest])

    extra = jnp.where(at_seam | past_seam, 3, 0) + jnp.where(is_relay, 2, 0)
    pl.semaphore_wait(barrier, 4 + extra)

    halo = (h_send, h_recv)
    cols = remote(area(ext, 0, 0, T), area(ext, 4, 0, T), halo, 0, to_left)
    rows_l = remote(area(ext, 0, 0, W), area(ext, 0, T, W), halo, 1, up)
    rows_r = remote(area(ext, 2, 0, W), area(ext, 2, T, W), halo, 2, up)
    on_left = remote(area(ext, 0, T, W), area(ext, 4, T, W), halo, 3, to_left)
    seam_corner = remote(area(ext, 0, 0, W), area(ext, 4, T, W), halo, 4, ((row + N_ROW - 1) % N_ROW, SEAM))
    to_plus = remote(area(ext, 0, 0, W), relay_in, halo, 5, relay_plus)
    to_minus = remote(area(ext, 0, W, W), relay_in, halo, 6, relay_minus)
    relay_upper = remote(relay_in, area(ext, 4, 0, W), halo, 7, relay_dest)
    relay_lower = remote(relay_in, area(ext, 4, W, W), halo, 8, relay_dest)

    lanes[0].wait()
    lanes[1].wait()
    when(past_seam, to_plus.start, to_minus.start)
    when(past_seam & has_up, seam_corner.start)
    when(has_up, rows_l.start)
    when(sends_left, cols.start)
    lanes[2].wait()
    lanes[3].wait()
    when(has_up & jnp.logical_not(is_relay), rows_r.start)
    for copy in halves:
        copy.wait()

    def reorder_slot(k, _):
        half = jnp.concatenate(
            [
                jnp.concatenate([amp_buf[k, n, pl.ds(start, H, stride=2), :] for n in range(2)], axis=1)
                for start in range(2)
            ],
            axis=0,
        )
        high, mid = high_low(half)
        low = (half - high.astype(F32) - mid.astype(F32)).astype(BF16)
        chosen = select_t[...].astype(BF16)
        amps_out[k] = dot(high, chosen) + dot(mid, chosen) + dot(low, chosen)
        return 0

    lax.fori_loop(0, amps.shape[0], reorder_slot, 0)
    when(is_relay & serves_upper, to_plus.wait_recv, relay_upper.start)
    when(is_relay & jnp.logical_not(serves_upper), to_minus.wait_recv, relay_lower.start)
    when(is_relay & has_up, rows_r.start)
    when(has_down, rows_l.wait_recv)
    when(has_down & sends_left, on_left.start)
    when(has_down, rows_r.wait_recv)
    when(gets_right, cols.wait_recv)
    when(at_seam, relay_upper.wait_recv, relay_lower.wait_recv)
    when(gets_right & has_down, on_left.wait_recv)
    when(at_seam & has_down, seam_corner.wait_recv)
    when(sends_left, cols.wait_send)
    when(has_up, rows_l.wait_send, rows_r.wait_send)
    when(has_down & sends_left, on_left.wait_send)
    when(past_seam, to_plus.wait_send, to_minus.wait_send)
    when(past_seam & has_up, seam_corner.wait_send)
    when(is_relay & serves_upper, relay_upper.wait_send)
    when(is_relay & jnp.logical_not(serves_upper), relay_lower.wait_send)


def ahead(tile, amps):
    n = np.arange(H)
    select = np.zeros((W, W), np.float32)
    select[2 * n, n] = 1.0
    select[2 * n + 1, H + n] = 1.0
    dma = pltpu.SemaphoreType.DMA
    vmem = pl.BlockSpec(memory_space=pltpu.VMEM)
    any_spec = pl.BlockSpec(memory_space=pl.ANY)
    return pl.pallas_call(
        ahead_kernel,
        out_shape=(jax.ShapeDtypeStruct(EXT, F32), jax.ShapeDtypeStruct(amps.shape, F32)),
        in_specs=[any_spec, any_spec, vmem],
        out_specs=(vmem, vmem),
        scratch_shapes=[
            VMEM((2, 2, W, H), F32), VMEM((amps.shape[0], 2, W, H), F32),
            dma((9,)), dma((9,)), dma((T // H,)), dma((2,)),
        ],
        compiler_params=pltpu.CompilerParams(
            collective_id=0, has_side_effects=True, vmem_limit_bytes=40 * MIB
        ),
        name="ahead",
    )(tile, amps, jnp.asarray(select))


def on_device(object_tile, probe, amplitudes, positions, counts):
    ext, amps = ahead(object_tile, amplitudes[0, 0])
    gext, part = run_slots(positions[0, 0].T, counts, ext, amps, probe)
    return back(gext, part)


def solution(mesh):
    in_specs = (
        P(None, "row", "col"),
        P(),
        P("row", "col", None, None, None),
        P("row", "col", None, None),
        P("row", None),
    )
    out_specs = (P(None, "row", "col"), P())
    return jax.shard_map(
        on_device, mesh=mesh, in_specs=in_specs, out_specs=out_specs, check_vma=False
    )
```

```python
import math

import jax
import jax.numpy as jnp
import numpy as np
from jax import lax
from jax.experimental import pallas as pl
from jax.experimental.pallas import tpu as pltpu
from jax.sharding import PartitionSpec as P

smooth_term = 0.01
F32 = jnp.float32
BF16 = jnp.bfloat16
W = 256
H = 128
T = 512
CH = 32
TILES = 6
VMEM = pltpu.VMEM
MESH = pl.DeviceIdType.MESH
N_ROW, N_COL = 8, 16
SEAM = 7
BACK_Y = 3
EXT = (2, TILES, T + W, H)
MIB = 1024 * 1024


def tables():
    n = np.arange(H)
    even = np.exp(-2j * np.pi * np.outer(n, n) / H) / math.sqrt(W)
    odd = np.exp(-2j * np.pi * n / W)[:, None] * even

    def real_form(z):
        return np.block([[z.real, z.imag], [-z.imag, z.real]])

    pair = [real_form(even), real_form(odd)]
    return np.stack(pair + [table.T for table in pair]).astype(np.float32)


def high_low(value):
    high = value.astype(BF16)
    return high, (value - high.astype(F32)).astype(BF16)


def put(ref, rows, cols, value):
    ref[0, rows, cols], ref[1, rows, cols] = high_low(value)


def dot(a, b):
    return jnp.dot(a, b, preferred_element_type=F32)


def by_right(x, t, n):
    return dot(x[0], t[n, 0]) + dot(x[1], t[n, 0]) + dot(x[0], t[n, 1])


def by_left(x, t, n):
    return dot(t[n, 0], x[0]) + dot(t[n, 0], x[1]) + dot(t[n, 1], x[0])


def slot_steps(r, c, live, ext, gext, probe, amp, t, win, xe, xo, ye, yo, pgrad):
    j0 = lax.shift_right_logical(c, 7)
    s = lax.bitwise_and(c, 127)
    back_shift = lax.bitwise_and(128 - s, 127)
    lane = lax.broadcasted_iota(jnp.int32, (CH, H), 1)
    first = lane < 128 - s
    left, right, both = pl.ds(0, H), pl.ds(H, H), pl.ds(0, W)
    for i in range(W // CH):
        rows = pl.ds(i * CH, CH)
        parts = []
        for p in range(2):
            q = [
                pltpu.roll(ext[p, j0 + n, pl.ds(r + i * CH, CH), :], back_shift, 1)
                for n in range(3)
            ]
            a = jnp.where(first, q[0], q[1])
            b = jnp.where(first, q[1], q[2])
            win[p, rows, left] = a
            win[p, rows, right] = b
            parts.append((a, b))
        (are, bre), (aim, bim) = parts
        pra, prb = probe[0, rows, left], probe[0, rows, right]
        pia, pib = probe[1, rows, left], probe[1, rows, right]
        ea_re = pra * are - pia * aim
        ea_im = pra * aim + pia * are
        eb_re = prb * bre - pib * bim
        eb_im = prb * bim + pib * bre
        put(xe, rows, left, ea_re + eb_re)
        put(xe, rows, right, ea_im + eb_im)
        put(xo, rows, left, ea_re - eb_re)
        put(xo, rows, right, ea_im - eb_im)
    yield
    ye[...] = by_right(xe, t, 0)
    yo[...] = by_right(xo, t, 1)
    yield
    for i in range(H // CH):
        top = pl.ds(i * CH, CH)
        bot = pl.ds(H + i * CH, CH)
        for cols, y in ((left, ye), (right, yo)):
            for part, lanes in ((0, left), (H, right)):
                a, b = y[top, lanes], y[bot, lanes]
                put(xe, pl.ds(part + i * CH, CH), cols, a + b)
                put(xo, pl.ds(part + i * CH, CH), cols, a - b)
    yield
    ye[...] = by_left(xe, t, 2)
    yo[...] = by_left(xo, t, 3)
    yield
    for i in range(H // CH):
        for at, y, x in ((0, ye, xe), (H, yo, xo)):
            re = y[pl.ds(i * CH, CH), :]
            im = y[pl.ds(H + i * CH, CH), :]
            a = amp[pl.ds(at + i * CH, CH), :]
            f = (2.0 - (2.0 * a) * lax.rsqrt(re * re + im * im + smooth_term)) * live
            put(x, pl.ds(i * CH, CH), both, f * re)
            put(x, pl.ds(H + i * CH, CH), both, f * im)
    yield
    ye[...] = by_left(xe, t, 0)
    yo[...] = by_left(xo, t, 1)
    yield
    for i in range(H // CH):
        for part, lanes in ((0, left), (H, right)):
            e = ye[pl.ds(part + i * CH, CH), :]
            o = yo[pl.ds(part + i * CH, CH), :]
            for at, value in ((0, e + o), (H, e - o)):
                rows = pl.ds(at + i * CH, CH)
                put(xe, rows, lanes, value[:, 0:H])
                put(xo, rows, lanes, value[:, H:W])
    yield
    ye[...] = by_right(xe, t, 2)
    yo[...] = by_right(xo, t, 3)
    yield
    later = lane >= s
    for i in range(W // CH):
        rows = pl.ds(i * CH, CH)
        e_re, e_im = ye[rows, left], ye[rows, right]
        o_re, o_im = yo[rows, left], yo[rows, right]
        terms = []
        for n, cols, b_re, b_im in ((0, left, e_re + o_re, e_im + o_im), (1, right, e_re - o_re, e_im - o_im)):
            pr, pi = probe[0, rows, cols], probe[1, rows, cols]
            wr, wi = win[0, rows, cols], win[1, rows, cols]
            pgrad[n, rows, :] += wr * b_re + wi * b_im
            pgrad[2 + n, rows, :] += wr * b_im - wi * b_re
            terms.append((pr * b_re + pi * b_im, pr * b_im - pi * b_re))
        for p in range(2):
            ra = pltpu.roll(terms[0][p], s, 1)
            rb = pltpu.roll(terms[1][p], s, 1)
            at = pl.ds(r + i * CH, CH)
            gext[p, j0, at, :] += jnp.where(later, ra, 0.0)
            gext[p, j0 + 1, at, :] += jnp.where(later, rb, ra)
            gext[p, j0 + 2, at, :] += jnp.where(later, 0.0, rb)
    yield


def interleave(streams, lag):
    waiting = [[stream, n * lag] for n, stream in enumerate(streams)]
    while waiting:
        for item in list(waiting):
            if item[1] > 0:
                item[1] -= 1
            elif next(item[0], waiting) is waiting:
                waiting.remove(item)


def slots_kernel(
    pos, counts, ext, amps, probe, table, gext, pgrad, amp_buf, t, win, xe, xo, ye, yo, amp_sem
):
    count = counts[0, lax.axis_index("col")]
    groups = lax.div(count + U - 1, U)

    def amp_copy(n, buf):
        return pltpu.make_async_copy(amps.at[pl.ds(U * n, U)], amp_buf.at[buf], amp_sem.at[buf])

    @pl.when(count > 0)
    def _():
        amp_copy(0, 0).start()

    gext[...] = jnp.zeros_like(gext)
    pgrad[...] = jnp.zeros_like(pgrad)
    for n in range(4):
        t[n, 0], t[n, 1] = high_low(table[n])

    def body(n, _):
        buf = lax.bitwise_and(n, 1)

        @pl.when(n + 1 < groups)
        def _():
            amp_copy(n + 1, 1 - buf).start()

        amp_copy(n, buf).wait()
        streams = []
        for u in range(U):
            k = U * n + u
            live = (k < count).astype(F32)
            streams.append(
                slot_steps(
                    pos[0, k], pos[1, k], live, ext, gext, probe, amp_buf.at[buf, u], t,
                    win.at[u], xe.at[u], xo.at[u], ye.at[u], yo.at[u], pgrad,
                )
            )
        interleave(streams, LAG)
        return 0

    lax.fori_loop(0, groups, body, 0)


LAG = 1
U = 4


def run_slots(own_pos, counts, ext, amps, probe):
    vmem = pl.BlockSpec(memory_space=pltpu.VMEM)
    smem = pl.BlockSpec(memory_space=pltpu.SMEM)
    return pl.pallas_call(
        slots_kernel,
        out_shape=(jax.ShapeDtypeStruct(EXT, F32), jax.ShapeDtypeStruct((4, W, H), F32)),
        in_specs=[smem, smem, vmem, pl.BlockSpec(memory_space=pl.ANY), vmem, vmem],
        out_specs=(vmem, vmem),
        scratch_shapes=[
            VMEM((2, U, W, W), F32),
            VMEM((4, 2, W, W), BF16),
            VMEM((U, 2, W, W), F32),
            VMEM((U, 2, W, W), BF16),
            VMEM((U, 2, W, W), BF16),
            VMEM((U, W, W), F32),
            VMEM((U, W, W), F32),
            pltpu.SemaphoreType.DMA((2,)),
        ],
        compiler_params=pltpu.CompilerParams(vmem_limit_bytes=28 * MIB),
        name="slots",
    )(own_pos, counts, ext, amps, probe, jnp.asarray(tables()))


def place():
    row, col = lax.axis_index("row"), lax.axis_index("col")
    z, x_lo = row // 2, row % 2
    x_hi, y, core = col // 8, (col // 2) % 4, col % 2
    return row, col, x_hi * 2 + x_lo, y, z, core


def at_chip(x, y, z, core):
    return (z * 2 + x % 2, (x // 2) * 8 + y * 2 + core)


def remote(src, dst, sems, n, device):
    return pltpu.make_async_remote_copy(
        src_ref=src, dst_ref=dst, send_sem=sems[0].at[n], recv_sem=sems[1].at[n],
        device_id=device, device_id_type=MESH,
    )


def block(start, count):
    return pl.ds(pl.multiple_of(start, 8), count)


def greet(devices):
    barrier = pltpu.get_barrier_semaphore()
    for device in devices:
        pl.semaphore_signal(barrier, inc=1, device_id=device, device_id_type=MESH)
    return barrier


def when(cond, *actions):
    @pl.when(cond)
    def _():
        for action in actions:
            action()


def area(ref, tile, row, rows):
    return ref.at[:, pl.ds(tile, 2), pl.ds(row, rows), :]


def back_kernel(
    gext, part, out, out_p, corner_in, right_in, below_l_in, below_r_in, seam_in, relay_in, below_sum,
    full, got0, acc0, got1, acc1, got2,
    h_send, h_recv, r_send, r_recv, m_send, m_recv, p_send, p_recv, x_send, x_recv,
):
    row, col, x, y, z, core = place()
    down, up = ((row + 1) % N_ROW, col), ((row + N_ROW - 1) % N_ROW, col)
    right, left = (row, (col + 1) % N_COL), (row, (col + N_COL - 1) % N_COL)
    mate = (row, col + 1 - 2 * core)
    pair, place_in_pair = (x + 1) // 2 % 2, x // 2
    near, far = place_in_pair * 4 + y, pair * 4 + z

    def near_peer(q):
        return (near + q) % 8

    def near_id(q):
        n = near_peer(q)
        return at_chip(pair + n // 4 * (3 - 2 * pair), n % 4, z, core)

    def far_peer(q):
        return (far + q) % 8

    def far_id(q):
        n = far_peer(q)
        return at_chip(n // 4 + place_in_pair * (3 - 2 * (n // 4)), y, n % 4, core)

    at_seam, past_seam = col == SEAM, col == SEAM + 1
    x_plus, x_minus = (x + 1) % 4, (x + 3) % 4
    is_relay = (y == BACK_Y) & (core == x // 2)
    has_down, has_up = row < N_ROW - 1, row > 0
    sends_right = (col < N_COL - 1) & (col != SEAM)
    gets_left = (col > 0) & (col != SEAM + 1)
    relay_plus = at_chip(x_plus, BACK_Y, z, x_plus // 2)
    relay_minus = at_chip(x_minus, BACK_Y, z, x_minus // 2)
    serves_upper = (x == 1) | (x == 2)
    relay_source = at_chip(jnp.where(serves_upper, x_minus, x_plus), 3, z, 1)
    relay_dest = at_chip(jnp.where(serves_upper, x_plus, x_minus), 0, z, 0)
    diagonal = ((row + 1) % N_ROW, SEAM + 1)
    diagonal_from = ((row + N_ROW - 1) % N_ROW, SEAM)

    barrier = greet([mate, down, up, left, right] + [near_id(q) for q in range(1, 8)] + [far_id(q) for q in range(1, 8)])

    @pl.when(at_seam)
    def _():
        greet([relay_plus, relay_minus, diagonal])

    @pl.when(past_seam)
    def _():
        greet([relay_plus, relay_minus, diagonal_from])

    @pl.when(is_relay)
    def _():
        greet([relay_source, relay_dest])

    extra = jnp.where(at_seam | past_seam, 3, 0) + jnp.where(is_relay, 2, 0)
    pl.semaphore_wait(barrier, 19 + extra)

    halo = (h_send, h_recv)
    corner = remote(area(gext, 4, T, W), corner_in, halo, 0, right)
    cols = remote(area(gext, 4, 0, W), area(right_in, 0, 0, W), halo, 1, right)
    cols2 = remote(area(gext, 4, W, W), area(right_in, 0, W, W), halo, 2, right)
    seam_corner = remote(area(gext, 4, T, W), seam_in, halo, 3, diagonal)
    to_plus = remote(area(gext, 4, 0, W), relay_in, halo, 4, relay_plus)
    to_minus = remote(area(gext, 4, W, W), relay_in, halo, 5, relay_minus)
    relay_upper = remote(relay_in, area(right_in, 0, 0, W), halo, 6, relay_dest)
    relay_lower = remote(relay_in, area(right_in, 0, W, W), halo, 7, relay_dest)
    pieces_r, pieces_l = [], []
    at = 0
    for n, rows in enumerate(PIECES_R):
        pieces_r.append(remote(area(gext, 2, T + at, rows), area(below_r_in, 0, at, rows), (r_send, r_recv), n, down))
        at += rows
    at = 0
    for n, rows in enumerate(PIECES_L):
        sems = (r_send, r_recv)
        pieces_l.append(remote(area(below_sum, 0, at, rows), area(below_l_in, 0, at, rows), sems, len(PIECES_R) + n, down))
        at += rows

    def start(copies):
        for copy in copies:
            copy.start()

    def wait(copies):
        for copy in copies:
            copy.wait()

    swap = remote(part.at[pl.ds(2 * (1 - core), 2)], got0, (m_send, m_recv), 0, mate)
    swap.start()
    when(at_seam, to_plus.start, to_minus.start)
    when(at_seam & has_down, seam_corner.start)
    when(sends_right, corner.start)
    when(has_down, pieces_r[0].start)
    swap.wait()
    for n in range(2):
        acc0[pl.ds(n * W, W), :] = part[2 * core + n] + got0[n]
    spread = [
        remote(acc0.at[block(near_peer(q) * 64, 64)], got1.at[q - 1], (p_send, p_recv), q - 1, near_id(q))
        for q in range(1, 8)
    ]
    start(spread)
    when(sends_right, cols.start)
    below_sum[...] = area(gext, 0, T, W)[...]

    @pl.when(gets_left)
    def _():
        corner.wait_recv()
        below_sum[...] += corner_in[...]

    wait(spread)
    total = acc0[block(near * 64, 64), :]
    for q in range(7):
        total = total + got1[q]
    acc1[...] = total
    spread = [
        remote(acc1.at[block(far_peer(q) * 8, 8)], got2.at[q - 1], (x_send, x_recv), q - 1, far_id(q))
        for q in range(1, 8)
    ]
    start(spread)
    wait(spread)
    base1 = core * 512 + near * 64
    own = block(base1 + far * 8, 8)
    total = acc1[block(far * 8, 8), :]
    for q in range(7):
        total = total + got2[q]
    full[own, :] = total
    spread = [remote(full.at[own], full.at[own], (x_send, x_recv), 6 + q, far_id(q)) for q in range(1, 8)]
    start(spread)
    wait(spread)
    own1 = block(base1, 64)
    spread = [remote(full.at[own1], full.at[own1], (p_send, p_recv), 6 + q, near_id(q)) for q in range(1, 8)]
    start(spread)
    when(is_relay & serves_upper, to_plus.wait_recv, relay_upper.start)
    when(is_relay & jnp.logical_not(serves_upper), to_minus.wait_recv, relay_lower.start)
    when(has_down, *[copy.start for copy in pieces_r[1:] + pieces_l])
    when(sends_right, cols2.start)
    for n in range(T // H):
        out[:, :, pl.ds(n * H, H)] = gext[:, n, pl.ds(0, T), :]
    wait(spread)
    own0 = block(core * 512, 512)
    swap = remote(full.at[own0], full.at[own0], (m_send, m_recv), 1, mate)
    swap.start()
    swap.wait()
    for p in range(2):
        for half in range(2):
            out_p[p, :, pl.ds(H * half, H)] = full[pl.ds((2 * p + half) * W, W), :]

    def add(value, rows, at):
        for n in range(2):
            out[:, pl.ds(0, rows), pl.ds((at + n) * H, H)] += value[:, n]

    @pl.when(has_up)
    def _():
        for copy in pieces_r:
            copy.wait_recv()
        add(below_r_in, W, 2)

    @pl.when(gets_left)
    def _():
        cols.wait_recv()
        cols2.wait_recv()
        add(right_in, T, 0)

    @pl.when(past_seam)
    def _():
        relay_upper.wait_recv()
        relay_lower.wait_recv()
        add(right_in, T, 0)

    @pl.when(has_up)
    def _():
        for copy in pieces_l:
            copy.wait_recv()
        add(below_l_in, W, 0)

    @pl.when(past_seam & has_up)
    def _():
        seam_corner.wait_recv()
        add(seam_in, W, 0)

    when(sends_right, corner.wait_send, cols.wait_send, cols2.wait_send)
    when(has_down, *[copy.wait_send for copy in pieces_r + pieces_l])
    when(at_seam, to_plus.wait_send, to_minus.wait_send)
    when(at_seam & has_down, seam_corner.wait_send)
    when(is_relay & serves_upper, relay_upper.wait_send)
    when(is_relay & jnp.logical_not(serves_upper), relay_lower.wait_send)


PIECES_R = (128, 128)
PIECES_L = (256,)


def back(gext, part):
    dma = pltpu.SemaphoreType.DMA
    vmem = pl.BlockSpec(memory_space=pltpu.VMEM)
    square = VMEM((2, 2, W, H), F32)
    return pl.pallas_call(
        back_kernel,
        out_shape=(jax.ShapeDtypeStruct((2, T, T), F32), jax.ShapeDtypeStruct((2, W, W), F32)),
        in_specs=[vmem, vmem],
        out_specs=(vmem, vmem),
        scratch_shapes=[
            square, VMEM((2, 2, T, H), F32), square, square, square, square, square,
            VMEM((4 * W, H), F32), VMEM((2, W, H), F32), VMEM((2 * W, H), F32),
            VMEM((7, 64, H), F32), VMEM((64, H), F32), VMEM((7, 8, H), F32),
            dma((8,)), dma((8,)), dma((3,)), dma((3,)), dma((2,)), dma((2,)), dma((14,)), dma((14,)), dma((14,)), dma((14,)),
        ],
        compiler_params=pltpu.CompilerParams(
            collective_id=1, has_side_effects=True, vmem_limit_bytes=24 * MIB
        ),
        name="back",
    )(gext, part)


def ahead_kernel(tile, amps, ext, amps_out, relay_in, amp_buf, h_send, h_recv, t_sem, a_sem):
    row, col, x, y, z, core = place()
    down, up = ((row + 1) % N_ROW, col), ((row + N_ROW - 1) % N_ROW, col)
    to_right, to_left = (row, (col + 1) % N_COL), (row, (col + N_COL - 1) % N_COL)
    at_seam, past_seam = col == SEAM, col == SEAM + 1
    has_down, has_up = row < N_ROW - 1, row > 0
    sends_left = (col > 0) & (col != SEAM + 1)
    gets_right = (col < N_COL - 1) & (col != SEAM)
    source, target = at_chip((x + 2) % 4, 0, z, 0), at_chip((x + 2) % 4, 3, z, 1)
    is_relay = (x < 2) & (y < 3) & (core == 1)
    relay_target = at_chip(x, 3, z, 1)

    lanes = [
        pltpu.make_async_copy(tile.at[:, :, pl.ds(H * n, H)], ext.at[:, n, pl.ds(0, T), :], t_sem.at[n])
        for n in range(T // H)
    ]
    halves = [
        pltpu.make_async_copy(amps.at[:, :, pl.ds(H * n, H)], amp_buf.at[:, n], a_sem.at[n])
        for n in range(2)
    ]
    for copy in lanes + halves:
        copy.start()
    barrier = greet([down, up, to_left, to_right])

    @pl.when(past_seam)
    def _():
        greet([at_chip((x + 2) % 4, q, z, 1) for q in range(3)] + [((row + N_ROW - 1) % N_ROW, SEAM)])

    @pl.when(at_seam)
    def _():
        greet([at_chip(x, q, z, 1) for q in range(3)] + [((row + 1) % N_ROW, SEAM + 1)])

    @pl.when(is_relay)
    def _():
        greet([source, relay_target])

    extra = jnp.where(at_seam | past_seam, 4, 0) + jnp.where(is_relay, 2, 0)
    pl.semaphore_wait(barrier, 4 + extra)

    halo = (h_send, h_recv)
    cols = remote(area(ext, 0, 0, T), area(ext, 4, 0, T), halo, 0, to_left)
    rows_l = remote(area(ext, 0, 0, W), area(ext, 0, T, W), halo, 1, up)
    rows_r = remote(area(ext, 2, 0, W), area(ext, 2, T, W), halo, 2, up)
    on_left = remote(area(ext, 0, T, W), area(ext, 4, T, W), halo, 3, to_left)
    seam_corner = remote(area(ext, 0, 0, W), area(ext, 4, T, W), halo, 4, ((row + N_ROW - 1) % N_ROW, SEAM))
    parts = [
        remote(area(ext, 0, H * q, H), relay_in, halo, 5 + q, at_chip((x + 2) % 4, q, z, 1)) for q in range(3)
    ]
    parts.append(remote(area(ext, 0, 3 * H, H), area(ext, 4, 3 * H, H), halo, 8, target))
    arrived = remote(relay_in, relay_in, halo, 5 + y % 3, relay_target)
    passed = remote(relay_in, area(ext, 4, H * (y % 3), H), halo, 9 + y % 3, relay_target)
    got = [remote(relay_in, area(ext, 4, H * q, H), halo, 9 + q, relay_target) for q in range(3)]

    lanes[0].wait()
    lanes[1].wait()
    when(past_seam, *[copy.start for copy in parts])
    when(past_seam & has_up, seam_corner.start)
    when(has_up, rows_l.start)
    when(sends_left, cols.start)
    lanes[2].wait()
    lanes[3].wait()
    when(has_up, rows_r.start)
    for copy in halves:
        copy.wait()

    source_at = lax.broadcasted_iota(jnp.int32, (W, W), 0)
    place_at = lax.broadcasted_iota(jnp.int32, (W, W), 1)
    odd = (place_at >= H).astype(jnp.int32)
    chosen = (source_at == 2 * (place_at - H * odd) + odd).astype(F32).astype(BF16)

    def reorder_slot(k, _):
        half = jnp.concatenate(
            [
                jnp.concatenate([amp_buf[k, n, pl.ds(start, H, stride=2), :] for n in range(2)], axis=1)
                for start in range(2)
            ],
            axis=0,
        )
        high, mid = high_low(half)
        low = (half - high.astype(F32) - mid.astype(F32)).astype(BF16)
        amps_out[k] = dot(high, chosen) + dot(mid, chosen) + dot(low, chosen)
        return 0

    lax.fori_loop(0, amps.shape[0], reorder_slot, 0)
    when(is_relay, arrived.wait_recv, passed.start)
    when(has_down, rows_l.wait_recv)
    when(has_down & sends_left, on_left.start)
    when(has_down, rows_r.wait_recv)
    when(gets_right, cols.wait_recv)
    when(at_seam, *[copy.wait_recv for copy in got], parts[3].wait_recv)
    when(gets_right & has_down, on_left.wait_recv)
    when(at_seam & has_down, seam_corner.wait_recv)
    when(sends_left, cols.wait_send)
    when(has_up, rows_l.wait_send, rows_r.wait_send)
    when(has_down & sends_left, on_left.wait_send)
    when(past_seam, *[copy.wait_send for copy in parts])
    when(past_seam & has_up, seam_corner.wait_send)
    when(is_relay, passed.wait_send)


def ahead(tile, amps):
    dma = pltpu.SemaphoreType.DMA
    vmem = pl.BlockSpec(memory_space=pltpu.VMEM)
    hbm = pl.BlockSpec(memory_space=pltpu.HBM)
    return pl.pallas_call(
        ahead_kernel,
        out_shape=(jax.ShapeDtypeStruct(EXT, F32), jax.ShapeDtypeStruct(amps.shape, F32)),
        in_specs=[hbm, hbm],
        out_specs=(vmem, vmem),
        scratch_shapes=[
            VMEM((2, 2, H, H), F32), VMEM((amps.shape[0], 2, W, H), F32),
            dma((12,)), dma((12,)), dma((T // H,)), dma((2,)),
        ],
        compiler_params=pltpu.CompilerParams(
            collective_id=0, has_side_effects=True, vmem_limit_bytes=24 * MIB
        ),
        name="ahead",
    )(tile, amps)


def on_device(object_tile, probe, amplitudes, positions, counts):
    ext, amps = ahead(object_tile, amplitudes[0, 0])
    gext, part = run_slots(positions[0, 0].T, counts, ext, amps, probe)
    return back(gext, part)


def solution(mesh):
    in_specs = (
        P(None, "row", "col"),
        P(),
        P("row", "col", None, None, None),
        P("row", "col", None, None),
        P("row", None),
    )
    out_specs = (P(None, "row", "col"), P())
    return jax.shard_map(
        on_device, mesh=mesh, in_specs=in_specs, out_specs=out_specs, check_vma=False
    )
```

```python
import math

import jax
import jax.numpy as jnp
import numpy as np
from jax import lax
from jax.experimental import pallas as pl
from jax.experimental.pallas import tpu as pltpu
from jax.sharding import PartitionSpec as P

smooth_term = 0.01
F32 = jnp.float32
BF16 = jnp.bfloat16
W = 256
H = 128
T = 512
CH = 32
TILES = 6
VMEM = pltpu.VMEM
MESH = pl.DeviceIdType.MESH
N_ROW, N_COL = 8, 16
SEAM = 7

EXT = (2, TILES, T + W, H)
MIB = 1024 * 1024


def tables():
    n = np.arange(H)
    even = np.exp(-2j * np.pi * np.outer(n, n) / H) / math.sqrt(W)
    odd = np.exp(-2j * np.pi * n / W)[:, None] * even

    def real_form(z):
        return np.block([[z.real, z.imag], [-z.imag, z.real]])

    pair = [real_form(even), real_form(odd)]
    return np.stack(pair + [table.T for table in pair]).astype(np.float32)


def high_low(value):
    high = value.astype(BF16)
    return high, (value - high.astype(F32)).astype(BF16)


def put(ref, rows, cols, value):
    ref[0, rows, cols], ref[1, rows, cols] = high_low(value)


def dot(a, b):
    return jnp.dot(a, b, preferred_element_type=F32)


def by_right(x, t, n):
    return dot(x[0], t[n, 0]) + dot(x[1], t[n, 0]) + dot(x[0], t[n, 1])


def by_left(x, t, n):
    return dot(t[n, 0], x[0]) + dot(t[n, 0], x[1]) + dot(t[n, 1], x[0])


def slot_steps(r, c, live, ext, gext, probe, amp, t, win, xe, xo, ye, yo, pgrad):
    j0 = lax.shift_right_logical(c, 7)
    s = lax.bitwise_and(c, 127)
    back_shift = lax.bitwise_and(128 - s, 127)
    lane = lax.broadcasted_iota(jnp.int32, (CH, H), 1)
    first = lane < 128 - s
    left, right, both = pl.ds(0, H), pl.ds(H, H), pl.ds(0, W)
    for i in range(W // CH):
        rows = pl.ds(i * CH, CH)
        parts = []
        for p in range(2):
            q = [
                pltpu.roll(ext[p, j0 + n, pl.ds(r + i * CH, CH), :], back_shift, 1)
                for n in range(3)
            ]
            a = jnp.where(first, q[0], q[1])
            b = jnp.where(first, q[1], q[2])
            win[p, rows, left] = a
            win[p, rows, right] = b
            parts.append((a, b))
        (are, bre), (aim, bim) = parts
        pra, prb = probe[0, rows, left], probe[0, rows, right]
        pia, pib = probe[1, rows, left], probe[1, rows, right]
        ea_re = pra * are - pia * aim
        ea_im = pra * aim + pia * are
        eb_re = prb * bre - pib * bim
        eb_im = prb * bim + pib * bre
        put(xe, rows, left, ea_re + eb_re)
        put(xe, rows, right, ea_im + eb_im)
        put(xo, rows, left, ea_re - eb_re)
        put(xo, rows, right, ea_im - eb_im)
    yield
    ye[...] = by_right(xe, t, 0)
    yo[...] = by_right(xo, t, 1)
    yield
    for i in range(H // CH):
        top = pl.ds(i * CH, CH)
        bot = pl.ds(H + i * CH, CH)
        for cols, y in ((left, ye), (right, yo)):
            for part, lanes in ((0, left), (H, right)):
                a, b = y[top, lanes], y[bot, lanes]
                put(xe, pl.ds(part + i * CH, CH), cols, a + b)
                put(xo, pl.ds(part + i * CH, CH), cols, a - b)
    yield
    ye[...] = by_left(xe, t, 2)
    yo[...] = by_left(xo, t, 3)
    yield
    for i in range(H // CH):
        for at, y, x in ((0, ye, xe), (H, yo, xo)):
            re = y[pl.ds(i * CH, CH), :]
            im = y[pl.ds(H + i * CH, CH), :]
            a = amp[pl.ds(at + i * CH, CH), :]
            f = (2.0 - (2.0 * a) * lax.rsqrt(re * re + im * im + smooth_term)) * live
            put(x, pl.ds(i * CH, CH), both, f * re)
            put(x, pl.ds(H + i * CH, CH), both, f * im)
    yield
    ye[...] = by_left(xe, t, 0)
    yo[...] = by_left(xo, t, 1)
    yield
    for i in range(H // CH):
        for part, lanes in ((0, left), (H, right)):
            e = ye[pl.ds(part + i * CH, CH), :]
            o = yo[pl.ds(part + i * CH, CH), :]
            for at, value in ((0, e + o), (H, e - o)):
                rows = pl.ds(at + i * CH, CH)
                put(xe, rows, lanes, value[:, 0:H])
                put(xo, rows, lanes, value[:, H:W])
    yield
    ye[...] = by_right(xe, t, 2)
    yo[...] = by_right(xo, t, 3)
    yield
    later = lane >= s
    for i in range(W // CH):
        rows = pl.ds(i * CH, CH)
        e_re, e_im = ye[rows, left], ye[rows, right]
        o_re, o_im = yo[rows, left], yo[rows, right]
        terms = []
        for n, cols, b_re, b_im in ((0, left, e_re + o_re, e_im + o_im), (1, right, e_re - o_re, e_im - o_im)):
            pr, pi = probe[0, rows, cols], probe[1, rows, cols]
            wr, wi = win[0, rows, cols], win[1, rows, cols]
            pgrad[n, rows, :] += wr * b_re + wi * b_im
            pgrad[2 + n, rows, :] += wr * b_im - wi * b_re
            terms.append((pr * b_re + pi * b_im, pr * b_im - pi * b_re))
        for p in range(2):
            ra = pltpu.roll(terms[0][p], s, 1)
            rb = pltpu.roll(terms[1][p], s, 1)
            at = pl.ds(r + i * CH, CH)
            gext[p, j0, at, :] += jnp.where(later, ra, 0.0)
            gext[p, j0 + 1, at, :] += jnp.where(later, rb, ra)
            gext[p, j0 + 2, at, :] += jnp.where(later, 0.0, rb)
    yield


def interleave(streams, lag):
    waiting = [[stream, n * lag] for n, stream in enumerate(streams)]
    while waiting:
        for item in list(waiting):
            if item[1] > 0:
                item[1] -= 1
            elif next(item[0], waiting) is waiting:
                waiting.remove(item)


def slots_kernel(
    pos, counts, ext, amps, probe, table, gext, pgrad, amp_buf, t, win, xe, xo, ye, yo, amp_sem
):
    count = counts[0, lax.axis_index("col")]
    groups = lax.div(count + U - 1, U)

    def amp_copy(n, buf):
        return pltpu.make_async_copy(amps.at[pl.ds(U * n, U)], amp_buf.at[buf], amp_sem.at[buf])

    @pl.when(count > 0)
    def _():
        amp_copy(0, 0).start()

    gext[...] = jnp.zeros_like(gext)
    pgrad[...] = jnp.zeros_like(pgrad)
    for n in range(4):
        t[n, 0], t[n, 1] = high_low(table[n])

    def body(n, _):
        buf = lax.bitwise_and(n, 1)

        @pl.when(n + 1 < groups)
        def _():
            amp_copy(n + 1, 1 - buf).start()

        amp_copy(n, buf).wait()
        streams = []
        for u in range(U):
            k = U * n + u
            live = (k < count).astype(F32)
            streams.append(
                slot_steps(
                    pos[0, k], pos[1, k], live, ext, gext, probe, amp_buf.at[buf, u], t,
                    win.at[u], xe.at[u], xo.at[u], ye.at[u], yo.at[u], pgrad,
                )
            )
        interleave(streams, LAG)
        return 0

    lax.fori_loop(0, groups, body, 0)


LAG = 1
U = 4


def run_slots(own_pos, counts, ext, amps, probe):
    vmem = pl.BlockSpec(memory_space=pltpu.VMEM)
    smem = pl.BlockSpec(memory_space=pltpu.SMEM)
    return pl.pallas_call(
        slots_kernel,
        out_shape=(jax.ShapeDtypeStruct(EXT, F32), jax.ShapeDtypeStruct((4, W, H), F32)),
        in_specs=[smem, smem, vmem, pl.BlockSpec(memory_space=pl.ANY), vmem, vmem],
        out_specs=(vmem, vmem),
        scratch_shapes=[
            VMEM((2, U, W, W), F32),
            VMEM((4, 2, W, W), BF16),
            VMEM((U, 2, W, W), F32),
            VMEM((U, 2, W, W), BF16),
            VMEM((U, 2, W, W), BF16),
            VMEM((U, W, W), F32),
            VMEM((U, W, W), F32),
            pltpu.SemaphoreType.DMA((2,)),
        ],
        compiler_params=pltpu.CompilerParams(vmem_limit_bytes=28 * MIB),
        name="slots",
    )(own_pos, counts, ext, amps, probe, jnp.asarray(tables()))


def place():
    row, col = lax.axis_index("row"), lax.axis_index("col")
    z, x_lo = row // 2, row % 2
    x_hi, y, core = col // 8, (col // 2) % 4, col % 2
    return row, col, x_hi * 2 + x_lo, y, z, core


def at_chip(x, y, z, core):
    return (z * 2 + x % 2, (x // 2) * 8 + y * 2 + core)


def remote(src, dst, sems, n, device):
    return pltpu.make_async_remote_copy(
        src_ref=src, dst_ref=dst, send_sem=sems[0].at[n], recv_sem=sems[1].at[n],
        device_id=device, device_id_type=MESH,
    )


def block(start, count):
    return pl.ds(pl.multiple_of(start, 8), count)


def greet(devices):
    barrier = pltpu.get_barrier_semaphore()
    for device in devices:
        pl.semaphore_signal(barrier, inc=1, device_id=device, device_id_type=MESH)
    return barrier


def when(cond, *actions):
    @pl.when(cond)
    def _():
        for action in actions:
            action()


def area(ref, tile, row, rows):
    return ref.at[:, pl.ds(tile, 2), pl.ds(row, rows), :]


def at_rows(ref, tile, row, rows):
    return ref.at[:, pl.ds(tile, 2), block(row, rows), :]


def back_kernel(
    gext, part, out, out_p, corner_in, right_in, below_l_in, below_r_in, seam_in, relay_in, below_sum,
    full, got0, acc0, got1, acc1, got2,
    h_send, h_recv, r_send, r_recv, m_send, m_recv, p_send, p_recv, x_send, x_recv,
):
    row, col, x, y, z, core = place()
    down, up = ((row + 1) % N_ROW, col), ((row + N_ROW - 1) % N_ROW, col)
    right, left = (row, (col + 1) % N_COL), (row, (col + N_COL - 1) % N_COL)
    mate = (row, col + 1 - 2 * core)
    pair, place_in_pair = (x + 1) // 2 % 2, x // 2
    near, far = place_in_pair * 4 + y, pair * 4 + z

    def near_peer(q):
        return (near + q) % 8

    def near_id(q):
        n = near_peer(q)
        return at_chip(pair + n // 4 * (3 - 2 * pair), n % 4, z, core)

    def far_peer(q):
        return (far + q) % 8

    def far_id(q):
        n = far_peer(q)
        return at_chip(n // 4 + place_in_pair * (3 - 2 * (n // 4)), y, n % 4, core)

    at_seam, past_seam = col == SEAM, col == SEAM + 1
    side, idle_side = (5 - x) % 4, (3 - x) % 4
    half, other_half = jnp.where(x == 0, 0, W), jnp.where(x == 0, W, 0)
    relays_half, relays_quarter = (y == 3) & (core == 0) & (x < 2), (y == 3) & (x >= 2)
    is_relay = relays_half | relays_quarter
    source = at_chip(jnp.where(x < 2, 1 - x, 3 - x), 3, z, 1)
    target = at_chip(jnp.where(x < 2, 3 - x, 5 - x), 0, z, 0)
    has_down, has_up = row < N_ROW - 1, row > 0
    sends_right = (col < N_COL - 1) & (col != SEAM)
    gets_left = (col > 0) & (col != SEAM + 1)
    diagonal = ((row + 1) % N_ROW, SEAM + 1)
    diagonal_from = ((row + N_ROW - 1) % N_ROW, SEAM)

    barrier = greet([mate, down, up, left, right] + [near_id(q) for q in range(1, 8)] + [far_id(q) for q in range(1, 8)])

    @pl.when(at_seam)
    def _():
        greet([at_chip(side, 3, z, 0)] + [at_chip(idle_side, 3, z, n) for n in range(2)] + [diagonal])

    @pl.when(past_seam)
    def _():
        greet([at_chip(idle_side, 3, z, 0)] + [at_chip(side, 3, z, n) for n in range(2)] + [diagonal_from])

    @pl.when(is_relay)
    def _():
        greet([source, target])

    extra = jnp.where(at_seam | past_seam, 4, 0) + jnp.where(is_relay, 2, 0)
    pl.semaphore_wait(barrier, 19 + extra)

    halo = (h_send, h_recv)
    corner = remote(area(gext, 4, T, W), corner_in, halo, 0, right)
    cols = remote(area(gext, 4, 0, W), area(right_in, 0, 0, W), halo, 1, right)
    cols2 = remote(area(gext, 4, W, W), area(right_in, 0, W, W), halo, 2, right)
    seam_corner = remote(area(gext, 4, T, W), seam_in, halo, 3, diagonal)
    quarter_in = relay_in.at[:, :, pl.ds(0, H), :]
    parts = [remote(at_rows(gext, 4, half, W), relay_in, halo, 4, at_chip(side, 3, z, 0))]
    for n in range(2):
        parts.append(remote(at_rows(gext, 4, other_half + H * n, H), quarter_in, halo, 5 + n, at_chip(idle_side, 3, z, n)))
    half_in = remote(relay_in, relay_in, halo, 4, target)
    half_on = remote(relay_in, at_rows(right_in, 0, jnp.where(x == 1, 0, W), W), halo, 7, target)
    quarter = remote(quarter_in, quarter_in, halo, 5 + core, target)
    quarter_on = remote(quarter_in, at_rows(right_in, 0, jnp.where(x == 3, W, 0) + H * core, H), halo, 8 + core, target)
    got = [remote(relay_in, area(right_in, 0, 0, W), halo, 7, target)]
    got += [remote(quarter_in, area(right_in, 0, 0, H), halo, 8 + n, target) for n in range(2)]
    pieces_r, pieces_l = [], []
    at = 0
    for n, rows in enumerate(PIECES_R):
        pieces_r.append(remote(area(gext, 2, T + at, rows), area(below_r_in, 0, at, rows), (r_send, r_recv), n, down))
        at += rows
    at = 0
    for n, rows in enumerate(PIECES_L):
        sems = (r_send, r_recv)
        pieces_l.append(remote(area(below_sum, 0, at, rows), area(below_l_in, 0, at, rows), sems, len(PIECES_R) + n, down))
        at += rows

    def start(copies):
        for copy in copies:
            copy.start()

    def wait(copies):
        for copy in copies:
            copy.wait()

    swap = remote(part.at[pl.ds(2 * (1 - core), 2)], got0, (m_send, m_recv), 0, mate)
    swap.start()
    when(at_seam, parts[1].start, parts[2].start, parts[0].start)
    when(at_seam & has_down, seam_corner.start)
    when(sends_right, corner.start)
    when(has_down, pieces_r[0].start)
    swap.wait()
    for n in range(2):
        acc0[pl.ds(n * W, W), :] = part[2 * core + n] + got0[n]
    spread = [
        remote(acc0.at[block(near_peer(q) * 64, 64)], got1.at[q - 1], (p_send, p_recv), q - 1, near_id(q))
        for q in range(1, 8)
    ]
    start(spread)
    when(sends_right, cols.start)
    below_sum[...] = area(gext, 0, T, W)[...]

    @pl.when(gets_left)
    def _():
        corner.wait_recv()
        below_sum[...] += corner_in[...]

    wait(spread)
    total = acc0[block(near * 64, 64), :]
    for q in range(7):
        total = total + got1[q]
    acc1[...] = total
    spread = [
        remote(acc1.at[block(far_peer(q) * 8, 8)], got2.at[q - 1], (x_send, x_recv), q - 1, far_id(q))
        for q in range(1, 8)
    ]
    start(spread)
    wait(spread)
    base1 = core * 512 + near * 64
    own = block(base1 + far * 8, 8)
    total = acc1[block(far * 8, 8), :]
    for q in range(7):
        total = total + got2[q]
    full[own, :] = total
    when(relays_quarter, quarter.wait_recv, quarter_on.start)
    spread = [remote(full.at[own], full.at[own], (x_send, x_recv), 6 + q, far_id(q)) for q in range(1, 8)]
    start(spread)
    wait(spread)
    own1 = block(base1, 64)
    spread = [remote(full.at[own1], full.at[own1], (p_send, p_recv), 6 + q, near_id(q)) for q in range(1, 8)]
    start(spread)
    when(relays_half, half_in.wait_recv, half_on.start)
    when(has_down, *[copy.start for copy in pieces_r[1:] + pieces_l])
    when(sends_right, cols2.start)
    for n in range(T // H):
        out[:, :, pl.ds(n * H, H)] = gext[:, n, pl.ds(0, T), :]
    wait(spread)
    own0 = block(core * 512, 512)
    swap = remote(full.at[own0], full.at[own0], (m_send, m_recv), 1, mate)
    swap.start()
    swap.wait()
    for p in range(2):
        for half in range(2):
            out_p[p, :, pl.ds(H * half, H)] = full[pl.ds((2 * p + half) * W, W), :]

    def add(value, rows, at):
        for n in range(2):
            out[:, pl.ds(0, rows), pl.ds((at + n) * H, H)] += value[:, n]

    @pl.when(has_up)
    def _():
        for copy in pieces_r:
            copy.wait_recv()
        add(below_r_in, W, 2)

    @pl.when(gets_left)
    def _():
        cols.wait_recv()
        cols2.wait_recv()
        add(right_in, T, 0)

    @pl.when(past_seam)
    def _():
        for copy in got:
            copy.wait_recv()
        add(right_in, T, 0)

    @pl.when(has_up)
    def _():
        for copy in pieces_l:
            copy.wait_recv()
        add(below_l_in, W, 0)

    @pl.when(past_seam & has_up)
    def _():
        seam_corner.wait_recv()
        add(seam_in, W, 0)

    when(sends_right, corner.wait_send, cols.wait_send, cols2.wait_send)
    when(has_down, *[copy.wait_send for copy in pieces_r + pieces_l])
    when(at_seam, *[copy.wait_send for copy in parts])
    when(at_seam & has_down, seam_corner.wait_send)
    when(relays_quarter, quarter_on.wait_send)
    when(relays_half, half_on.wait_send)


PIECES_R = (128, 128)
PIECES_L = (256,)


def back(gext, part):
    dma = pltpu.SemaphoreType.DMA
    vmem = pl.BlockSpec(memory_space=pltpu.VMEM)
    square = VMEM((2, 2, W, H), F32)
    return pl.pallas_call(
        back_kernel,
        out_shape=(jax.ShapeDtypeStruct((2, T, T), F32), jax.ShapeDtypeStruct((2, W, W), F32)),
        in_specs=[vmem, vmem],
        out_specs=(vmem, vmem),
        scratch_shapes=[
            square, VMEM((2, 2, T, H), F32), square, square, square, square, square,
            VMEM((4 * W, H), F32), VMEM((2, W, H), F32), VMEM((2 * W, H), F32),
            VMEM((7, 64, H), F32), VMEM((64, H), F32), VMEM((7, 8, H), F32),
            dma((10,)), dma((10,)), dma((3,)), dma((3,)), dma((2,)), dma((2,)), dma((14,)), dma((14,)), dma((14,)), dma((14,)),
        ],
        compiler_params=pltpu.CompilerParams(
            collective_id=1, has_side_effects=True, vmem_limit_bytes=24 * MIB
        ),
        name="back",
    )(gext, part)


def ahead_kernel(tile, amps, ext, amps_out, relay_in, amp_buf, h_send, h_recv, t_sem, a_sem):
    row, col, x, y, z, core = place()
    down, up = ((row + 1) % N_ROW, col), ((row + N_ROW - 1) % N_ROW, col)
    to_right, to_left = (row, (col + 1) % N_COL), (row, (col + N_COL - 1) % N_COL)
    at_seam, past_seam = col == SEAM, col == SEAM + 1
    has_down, has_up = row < N_ROW - 1, row > 0
    sends_left = (col > 0) & (col != SEAM + 1)
    gets_right = (col < N_COL - 1) & (col != SEAM)
    side, idle_side = (5 - x) % 4, (3 - x) % 4
    half, other_half = jnp.where(x == 2, 0, W), jnp.where(x == 2, W, 0)
    relays_half, relays_quarter = (y == 0) & (core == 1) & (x >= 2), (y == 0) & (x < 2)
    is_relay = relays_half | relays_quarter
    source = at_chip(jnp.where(x >= 2, 5 - x, 3 - x), 0, z, 0)
    target = at_chip(jnp.where(x >= 2, 3 - x, 1 - x), 3, z, 1)

    lanes = [
        pltpu.make_async_copy(tile.at[:, :, pl.ds(H * n, H)], ext.at[:, n, pl.ds(0, T), :], t_sem.at[n])
        for n in range(T // H)
    ]
    halves = [
        pltpu.make_async_copy(amps.at[:, :, pl.ds(H * n, H)], amp_buf.at[:, n], a_sem.at[n])
        for n in range(2)
    ]
    for copy in lanes + halves:
        copy.start()
    barrier = greet([down, up, to_left, to_right])

    @pl.when(past_seam)
    def _():
        greet([at_chip(side, 0, z, 1)] + [at_chip(idle_side, 0, z, n) for n in range(2)])
        greet([((row + N_ROW - 1) % N_ROW, SEAM)])

    @pl.when(at_seam)
    def _():
        greet([at_chip((3 - x) % 4, 0, z, 1)] + [at_chip((1 - x) % 4, 0, z, n) for n in range(2)])
        greet([((row + 1) % N_ROW, SEAM + 1)])

    @pl.when(is_relay)
    def _():
        greet([source, target])

    extra = jnp.where(at_seam | past_seam, 4, 0) + jnp.where(is_relay, 2, 0)
    pl.semaphore_wait(barrier, 4 + extra)

    halo = (h_send, h_recv)
    cols = remote(area(ext, 0, 0, T), area(ext, 4, 0, T), halo, 0, to_left)
    rows_l = remote(area(ext, 0, 0, W), area(ext, 0, T, W), halo, 1, up)
    rows_r = remote(area(ext, 2, 0, W), area(ext, 2, T, W), halo, 2, up)
    on_left = remote(area(ext, 0, T, W), area(ext, 4, T, W), halo, 3, to_left)
    seam_corner = remote(area(ext, 0, 0, W), area(ext, 4, T, W), halo, 4, ((row + N_ROW - 1) % N_ROW, SEAM))
    quarter_in = relay_in.at[:, :, pl.ds(0, H), :]
    parts = [remote(at_rows(ext, 0, half, W), relay_in, halo, 5, at_chip(side, 0, z, 1))]
    for n in range(2):
        parts.append(remote(at_rows(ext, 0, other_half + H * n, H), quarter_in, halo, 6 + n, at_chip(idle_side, 0, z, n)))
    half_in = remote(relay_in, relay_in, halo, 5, target)
    half_on = remote(relay_in, at_rows(ext, 4, jnp.where(x == 3, 0, W), W), halo, 8, target)
    quarter = remote(quarter_in, quarter_in, halo, 6 + core, target)
    quarter_on = remote(quarter_in, at_rows(ext, 4, jnp.where(x == 1, W, 0) + H * core, H), halo, 9 + core, target)
    got = [remote(relay_in, area(ext, 4, 0, W), halo, 8, target)]
    got += [remote(quarter_in, area(ext, 4, 0, H), halo, 9 + n, target) for n in range(2)]

    lanes[0].wait()
    lanes[1].wait()
    when(past_seam, parts[1].start, parts[2].start, parts[0].start)
    when(past_seam & has_up, seam_corner.start)
    when(has_up, rows_l.start)
    when(sends_left, cols.start)
    lanes[2].wait()
    lanes[3].wait()
    when(has_up, rows_r.start)
    for copy in halves:
        copy.wait()

    source_at = lax.broadcasted_iota(jnp.int32, (W, W), 0)
    place_at = lax.broadcasted_iota(jnp.int32, (W, W), 1)
    odd = (place_at >= H).astype(jnp.int32)
    chosen = (source_at == 2 * (place_at - H * odd) + odd).astype(F32).astype(BF16)

    def reorder_slot(k, _):
        half = jnp.concatenate(
            [
                jnp.concatenate([amp_buf[k, n, pl.ds(start, H, stride=2), :] for n in range(2)], axis=1)
                for start in range(2)
            ],
            axis=0,
        )
        high, mid = high_low(half)
        low = (half - high.astype(F32) - mid.astype(F32)).astype(BF16)
        amps_out[k] = dot(high, chosen) + dot(mid, chosen) + dot(low, chosen)
        return 0

    lax.fori_loop(0, amps.shape[0] // 2, reorder_slot, 0)
    when(relays_quarter, quarter.wait_recv, quarter_on.start)
    when(relays_half, half_in.wait_recv, half_on.start)
    lax.fori_loop(amps.shape[0] // 2, amps.shape[0], reorder_slot, 0)
    when(has_down, rows_l.wait_recv)
    when(has_down & sends_left, on_left.start)
    when(has_down, rows_r.wait_recv)
    when(gets_right, cols.wait_recv)
    when(at_seam, *[copy.wait_recv for copy in got])
    when(gets_right & has_down, on_left.wait_recv)
    when(at_seam & has_down, seam_corner.wait_recv)
    when(sends_left, cols.wait_send)
    when(has_up, rows_l.wait_send, rows_r.wait_send)
    when(has_down & sends_left, on_left.wait_send)
    when(past_seam, *[copy.wait_send for copy in parts])
    when(past_seam & has_up, seam_corner.wait_send)
    when(relays_quarter, quarter_on.wait_send)
    when(relays_half, half_on.wait_send)


def ahead(tile, amps):
    dma = pltpu.SemaphoreType.DMA
    vmem = pl.BlockSpec(memory_space=pltpu.VMEM)
    hbm = pl.BlockSpec(memory_space=pltpu.HBM)
    return pl.pallas_call(
        ahead_kernel,
        out_shape=(jax.ShapeDtypeStruct(EXT, F32), jax.ShapeDtypeStruct(amps.shape, F32)),
        in_specs=[hbm, hbm],
        out_specs=(vmem, vmem),
        scratch_shapes=[
            VMEM((2, 2, W, H), F32), VMEM((amps.shape[0], 2, W, H), F32),
            dma((11,)), dma((11,)), dma((T // H,)), dma((2,)),
        ],
        compiler_params=pltpu.CompilerParams(
            collective_id=0, has_side_effects=True, vmem_limit_bytes=24 * MIB
        ),
        name="ahead",
    )(pltpu.with_memory_space_constraint(tile, pltpu.HBM), pltpu.with_memory_space_constraint(amps, pltpu.HBM))


def on_device(object_tile, probe, amplitudes, positions, counts):
    ext, amps = ahead(object_tile, amplitudes[0, 0])
    gext, part = run_slots(positions[0, 0].T, counts, ext, amps, probe)
    return back(gext, part)


def solution(mesh):
    in_specs = (
        P(None, "row", "col"),
        P(),
        P("row", "col", None, None, None),
        P("row", "col", None, None),
        P("row", None),
    )
    out_specs = (P(None, "row", "col"), P())
    return jax.shard_map(
        on_device, mesh=mesh, in_specs=in_specs, out_specs=out_specs, check_vma=False
    )
```

```python
import math

import jax
import jax.numpy as jnp
import numpy as np
from jax import lax
from jax.experimental import pallas as pl
from jax.experimental.pallas import tpu as pltpu
from jax.sharding import PartitionSpec as P

smooth_term = 0.01
F32 = jnp.float32
BF16 = jnp.bfloat16
W = 256
H = 128
T = 512
CH = 32
TILES = 6
VMEM = pltpu.VMEM
MESH = pl.DeviceIdType.MESH
N_ROW, N_COL = 8, 16
SEAM = 7

EXT = (2, TILES, T + W, H)
MIB = 1024 * 1024


def tables():
    n = np.arange(H)
    even = np.exp(-2j * np.pi * np.outer(n, n) / H) / math.sqrt(W)
    odd = np.exp(-2j * np.pi * n / W)[:, None] * even

    def real_form(z):
        return np.block([[z.real, z.imag], [-z.imag, z.real]])

    pair = [real_form(even), real_form(odd)]
    return np.stack(pair + [table.T for table in pair]).astype(np.float32)


def high_low(value):
    high = value.astype(BF16)
    return high, (value - high.astype(F32)).astype(BF16)


def put(ref, rows, cols, value):
    ref[0, rows, cols], ref[1, rows, cols] = high_low(value)


def dot(a, b):
    return jnp.dot(a, b, preferred_element_type=F32)


def by_right(x, t, n):
    return dot(x[0], t[n, 0]) + dot(x[1], t[n, 0]) + dot(x[0], t[n, 1])


def by_left(x, t, n):
    return dot(t[n, 0], x[0]) + dot(t[n, 0], x[1]) + dot(t[n, 1], x[0])


def slot_steps(r, c, live, ext, gext, probe, amp, t, win, xe, xo, ye, yo, pgrad):
    j0 = lax.shift_right_logical(c, 7)
    s = lax.bitwise_and(c, 127)
    back_shift = lax.bitwise_and(128 - s, 127)
    lane = lax.broadcasted_iota(jnp.int32, (CH, H), 1)
    first = lane < 128 - s
    left, right, both = pl.ds(0, H), pl.ds(H, H), pl.ds(0, W)
    for i in range(W // CH):
        rows = pl.ds(i * CH, CH)
        parts = []
        for p in range(2):
            q = [
                pltpu.roll(ext[p, j0 + n, pl.ds(r + i * CH, CH), :], back_shift, 1)
                for n in range(3)
            ]
            a = jnp.where(first, q[0], q[1])
            b = jnp.where(first, q[1], q[2])
            win[p, rows, left] = a
            win[p, rows, right] = b
            parts.append((a, b))
        (are, bre), (aim, bim) = parts
        pra, prb = probe[0, rows, left], probe[0, rows, right]
        pia, pib = probe[1, rows, left], probe[1, rows, right]
        ea_re = pra * are - pia * aim
        ea_im = pra * aim + pia * are
        eb_re = prb * bre - pib * bim
        eb_im = prb * bim + pib * bre
        put(xe, rows, left, ea_re + eb_re)
        put(xe, rows, right, ea_im + eb_im)
        put(xo, rows, left, ea_re - eb_re)
        put(xo, rows, right, ea_im - eb_im)
    yield
    ye[...] = by_right(xe, t, 0)
    yo[...] = by_right(xo, t, 1)
    yield
    for i in range(H // CH):
        top = pl.ds(i * CH, CH)
        bot = pl.ds(H + i * CH, CH)
        for cols, y in ((left, ye), (right, yo)):
            for part, lanes in ((0, left), (H, right)):
                a, b = y[top, lanes], y[bot, lanes]
                put(xe, pl.ds(part + i * CH, CH), cols, a + b)
                put(xo, pl.ds(part + i * CH, CH), cols, a - b)
    yield
    ye[...] = by_left(xe, t, 2)
    yo[...] = by_left(xo, t, 3)
    yield
    for i in range(H // CH):
        for at, y, x in ((0, ye, xe), (H, yo, xo)):
            re = y[pl.ds(i * CH, CH), :]
            im = y[pl.ds(H + i * CH, CH), :]
            a = amp[pl.ds(at + i * CH, CH), :]
            f = (2.0 - (2.0 * a) * lax.rsqrt(re * re + im * im + smooth_term)) * live
            put(x, pl.ds(i * CH, CH), both, f * re)
            put(x, pl.ds(H + i * CH, CH), both, f * im)
    yield
    ye[...] = by_left(xe, t, 0)
    yo[...] = by_left(xo, t, 1)
    yield
    for i in range(H // CH):
        for part, lanes in ((0, left), (H, right)):
            e = ye[pl.ds(part + i * CH, CH), :]
            o = yo[pl.ds(part + i * CH, CH), :]
            for at, value in ((0, e + o), (H, e - o)):
                rows = pl.ds(at + i * CH, CH)
                put(xe, rows, lanes, value[:, 0:H])
                put(xo, rows, lanes, value[:, H:W])
    yield
    ye[...] = by_right(xe, t, 2)
    yo[...] = by_right(xo, t, 3)
    yield
    later = lane >= s
    for i in range(W // CH):
        rows = pl.ds(i * CH, CH)
        e_re, e_im = ye[rows, left], ye[rows, right]
        o_re, o_im = yo[rows, left], yo[rows, right]
        terms = []
        for n, cols, b_re, b_im in ((0, left, e_re + o_re, e_im + o_im), (1, right, e_re - o_re, e_im - o_im)):
            pr, pi = probe[0, rows, cols], probe[1, rows, cols]
            wr, wi = win[0, rows, cols], win[1, rows, cols]
            pgrad[n, rows, :] += wr * b_re + wi * b_im
            pgrad[2 + n, rows, :] += wr * b_im - wi * b_re
            terms.append((pr * b_re + pi * b_im, pr * b_im - pi * b_re))
        for p in range(2):
            ra = pltpu.roll(terms[0][p], s, 1)
            rb = pltpu.roll(terms[1][p], s, 1)
            at = pl.ds(r + i * CH, CH)
            gext[p, j0, at, :] += jnp.where(later, ra, 0.0)
            gext[p, j0 + 1, at, :] += jnp.where(later, rb, ra)
            gext[p, j0 + 2, at, :] += jnp.where(later, 0.0, rb)
    yield


def interleave(streams, lag):
    waiting = [[stream, n * lag] for n, stream in enumerate(streams)]
    while waiting:
        for item in list(waiting):
            if item[1] > 0:
                item[1] -= 1
            elif next(item[0], waiting) is waiting:
                waiting.remove(item)


def slots_kernel(
    pos, counts, ext, amps, probe, table, gext, pgrad, amp_buf, t, win, xe, xo, ye, yo, amp_sem
):
    count = counts[0, lax.axis_index("col")]
    groups = lax.div(count + U - 1, U)

    def amp_copy(n, buf):
        return pltpu.make_async_copy(amps.at[pl.ds(U * n, U)], amp_buf.at[buf], amp_sem.at[buf])

    @pl.when(count > 0)
    def _():
        amp_copy(0, 0).start()

    gext[...] = jnp.zeros_like(gext)
    pgrad[...] = jnp.zeros_like(pgrad)
    for n in range(4):
        t[n, 0], t[n, 1] = high_low(table[n])

    def body(n, _):
        buf = lax.bitwise_and(n, 1)

        @pl.when(n + 1 < groups)
        def _():
            amp_copy(n + 1, 1 - buf).start()

        amp_copy(n, buf).wait()
        streams = []
        for u in range(U):
            k = U * n + u
            live = (k < count).astype(F32)
            streams.append(
                slot_steps(
                    pos[0, k], pos[1, k], live, ext, gext, probe, amp_buf.at[buf, u], t,
                    win.at[u], xe.at[u], xo.at[u], ye.at[u], yo.at[u], pgrad,
                )
            )
        interleave(streams, LAG)
        return 0

    lax.fori_loop(0, groups, body, 0)


LAG = 1
U = 4


def run_slots(own_pos, counts, ext, amps, probe):
    vmem = pl.BlockSpec(memory_space=pltpu.VMEM)
    smem = pl.BlockSpec(memory_space=pltpu.SMEM)
    return pl.pallas_call(
        slots_kernel,
        out_shape=(jax.ShapeDtypeStruct(EXT, F32), jax.ShapeDtypeStruct((4, W, H), F32)),
        in_specs=[smem, smem, vmem, pl.BlockSpec(memory_space=pl.ANY), vmem, vmem],
        out_specs=(vmem, vmem),
        scratch_shapes=[
            VMEM((2, U, W, W), F32),
            VMEM((4, 2, W, W), BF16),
            VMEM((U, 2, W, W), F32),
            VMEM((U, 2, W, W), BF16),
            VMEM((U, 2, W, W), BF16),
            VMEM((U, W, W), F32),
            VMEM((U, W, W), F32),
            pltpu.SemaphoreType.DMA((2,)),
        ],
        compiler_params=pltpu.CompilerParams(vmem_limit_bytes=28 * MIB),
        name="slots",
    )(own_pos, counts, ext, amps, probe, jnp.asarray(tables()))


def place():
    row, col = lax.axis_index("row"), lax.axis_index("col")
    z, x_lo = row // 2, row % 2
    x_hi, y, core = col // 8, (col // 2) % 4, col % 2
    return row, col, x_hi * 2 + x_lo, y, z, core


def at_chip(x, y, z, core):
    return (z * 2 + x % 2, (x // 2) * 8 + y * 2 + core)


def remote(src, dst, sems, n, device):
    return pltpu.make_async_remote_copy(
        src_ref=src, dst_ref=dst, send_sem=sems[0].at[n], recv_sem=sems[1].at[n],
        device_id=device, device_id_type=MESH,
    )


def block(start, count):
    return pl.ds(pl.multiple_of(start, 8), count)


def greet(devices):
    barrier = pltpu.get_barrier_semaphore()
    for device in devices:
        pl.semaphore_signal(barrier, inc=1, device_id=device, device_id_type=MESH)
    return barrier


def when(cond, *actions):
    @pl.when(cond)
    def _():
        for action in actions:
            action()


def area(ref, tile, row, rows):
    return ref.at[:, pl.ds(tile, 2), pl.ds(row, rows), :]


def at_rows(ref, tile, row, rows):
    return ref.at[:, pl.ds(tile, 2), block(row, rows), :]


def back_kernel(
    gext, part, out, out_p, corner_in, right_in, below_l_in, below_r_in, seam_in, relay_in, below_sum,
    full, got0, acc0, got1, acc1, got2,
    h_send, h_recv, r_send, r_recv, m_send, m_recv, p_send, p_recv, x_send, x_recv,
):
    row, col, x, y, z, core = place()
    down, up = ((row + 1) % N_ROW, col), ((row + N_ROW - 1) % N_ROW, col)
    right, left = (row, (col + 1) % N_COL), (row, (col + N_COL - 1) % N_COL)
    mate = (row, col + 1 - 2 * core)
    pair, place_in_pair = (x + 1) // 2 % 2, x // 2
    near, far = place_in_pair * 4 + y, pair * 4 + z

    def near_peer(q):
        return (near + q) % 8

    def near_id(q):
        n = near_peer(q)
        return at_chip(pair + n // 4 * (3 - 2 * pair), n % 4, z, core)

    def far_peer(q):
        return (far + q) % 8

    def far_id(q):
        n = far_peer(q)
        return at_chip(n // 4 + place_in_pair * (3 - 2 * (n // 4)), y, n % 4, core)

    at_seam, past_seam = col == SEAM, col == SEAM + 1
    side, idle_side = (5 - x) % 4, (3 - x) % 4
    half, other_half = jnp.where(x == 0, 0, W), jnp.where(x == 0, W, 0)
    relays_half, relays_quarter = (y == 3) & (core == 0) & (x < 2), (y == 3) & (x >= 2)
    is_relay = relays_half | relays_quarter
    source = at_chip(jnp.where(x < 2, 1 - x, 3 - x), 3, z, 1)
    target = at_chip(jnp.where(x < 2, 3 - x, 5 - x), 0, z, 0)
    has_down, has_up = row < N_ROW - 1, row > 0
    sends_right = (col < N_COL - 1) & (col != SEAM)
    gets_left = (col > 0) & (col != SEAM + 1)
    diagonal = ((row + 1) % N_ROW, SEAM + 1)
    diagonal_from = ((row + N_ROW - 1) % N_ROW, SEAM)

    barrier = greet([mate, down, up, left, right] + [near_id(q) for q in range(1, 8)] + [far_id(q) for q in range(1, 8)])

    @pl.when(at_seam)
    def _():
        greet([at_chip(side, 3, z, 0)] + [at_chip(idle_side, 3, z, n) for n in range(2)] + [diagonal])

    @pl.when(past_seam)
    def _():
        greet([at_chip(idle_side, 3, z, 0)] + [at_chip(side, 3, z, n) for n in range(2)] + [diagonal_from])

    @pl.when(is_relay)
    def _():
        greet([source, target])

    extra = jnp.where(at_seam | past_seam, 4, 0) + jnp.where(is_relay, 2, 0)
    pl.semaphore_wait(barrier, 19 + extra)

    halo = (h_send, h_recv)
    corner = remote(area(gext, 4, T, W), corner_in, halo, 0, right)
    cols = remote(area(gext, 4, 0, W), area(right_in, 0, 0, W), halo, 1, right)
    cols2 = remote(area(gext, 4, W, W), area(right_in, 0, W, W), halo, 2, right)
    seam_corner = remote(area(gext, 4, T, W), seam_in, halo, 3, diagonal)
    quarter_in = relay_in.at[:, :, pl.ds(0, H), :]
    parts = [remote(at_rows(gext, 4, half, W), relay_in, halo, 4, at_chip(side, 3, z, 0))]
    for n in range(2):
        parts.append(remote(at_rows(gext, 4, other_half + H * n, H), quarter_in, halo, 5 + n, at_chip(idle_side, 3, z, n)))
    half_in = remote(relay_in, relay_in, halo, 4, target)
    half_on = remote(relay_in, at_rows(right_in, 0, jnp.where(x == 1, 0, W), W), halo, 7, target)
    quarter = remote(quarter_in, quarter_in, halo, 5 + core, target)
    quarter_on = remote(quarter_in, at_rows(right_in, 0, jnp.where(x == 3, W, 0) + H * core, H), halo, 8 + core, target)
    got = [remote(relay_in, area(right_in, 0, 0, W), halo, 7, target)]
    got += [remote(quarter_in, area(right_in, 0, 0, H), halo, 8 + n, target) for n in range(2)]
    pieces_r, pieces_l = [], []
    at = 0
    for n, rows in enumerate(PIECES_R):
        pieces_r.append(remote(area(gext, 2, T + at, rows), area(below_r_in, 0, at, rows), (r_send, r_recv), n, down))
        at += rows
    at = 0
    for n, rows in enumerate(PIECES_L):
        sems = (r_send, r_recv)
        pieces_l.append(remote(area(below_sum, 0, at, rows), area(below_l_in, 0, at, rows), sems, len(PIECES_R) + n, down))
        at += rows

    def start(copies):
        for copy in copies:
            copy.start()

    def wait(copies):
        for copy in copies:
            copy.wait()

    swap = remote(part.at[pl.ds(2 * (1 - core), 2)], got0, (m_send, m_recv), 0, mate)
    swap.start()
    when(at_seam, parts[1].start, parts[2].start, parts[0].start)
    when(at_seam & has_down, seam_corner.start)
    when(sends_right, corner.start)
    when(has_down, pieces_r[0].start)
    swap.wait()
    for n in range(2):
        acc0[pl.ds(n * W, W), :] = part[2 * core + n] + got0[n]
    spread = [
        remote(acc0.at[block(near_peer(q) * 64, 64)], got1.at[q - 1], (p_send, p_recv), q - 1, near_id(q))
        for q in range(1, 8)
    ]
    start(spread)
    when(sends_right, cols.start)
    below_sum[...] = area(gext, 0, T, W)[...]

    @pl.when(gets_left)
    def _():
        corner.wait_recv()
        below_sum[...] += corner_in[...]

    wait(spread)
    total = acc0[block(near * 64, 64), :]
    for q in range(7):
        total = total + got1[q]
    acc1[...] = total
    spread = [
        remote(acc1.at[block(far_peer(q) * 8, 8)], got2.at[q - 1], (x_send, x_recv), q - 1, far_id(q))
        for q in range(1, 8)
    ]
    start(spread)
    wait(spread)
    base1 = core * 512 + near * 64
    own = block(base1 + far * 8, 8)
    total = acc1[block(far * 8, 8), :]
    for q in range(7):
        total = total + got2[q]
    full[own, :] = total
    when(relays_quarter, quarter.wait_recv, quarter_on.start)
    spread = [remote(full.at[own], full.at[own], (x_send, x_recv), 6 + q, far_id(q)) for q in range(1, 8)]
    start(spread)
    when(has_down, pieces_l[0].start)
    wait(spread)
    own1 = block(base1, 64)
    spread = [remote(full.at[own1], full.at[own1], (p_send, p_recv), 6 + q, near_id(q)) for q in range(1, 8)]
    start(spread)
    when(relays_half, half_in.wait_recv, half_on.start)
    when(has_down, *[copy.start for copy in pieces_l[1:]])
    when(sends_right, cols2.start)
    for n in range(T // H):
        out[:, :, pl.ds(n * H, H)] = gext[:, n, pl.ds(0, T), :]
    wait(spread)
    own0 = block(core * 512, 512)
    swap = remote(full.at[own0], full.at[own0], (m_send, m_recv), 1, mate)
    swap.start()
    swap.wait()
    for p in range(2):
        for half in range(2):
            out_p[p, :, pl.ds(H * half, H)] = full[pl.ds((2 * p + half) * W, W), :]

    def add(value, rows, at):
        for n in range(2):
            out[:, pl.ds(0, rows), pl.ds((at + n) * H, H)] += value[:, n]

    @pl.when(has_up)
    def _():
        for copy in pieces_r:
            copy.wait_recv()
        add(below_r_in, W, 2)

    @pl.when(gets_left)
    def _():
        cols.wait_recv()
        cols2.wait_recv()
        add(right_in, T, 0)

    @pl.when(past_seam)
    def _():
        for copy in got:
            copy.wait_recv()
        add(right_in, T, 0)

    @pl.when(has_up)
    def _():
        for copy in pieces_l:
            copy.wait_recv()
        add(below_l_in, W, 0)

    @pl.when(past_seam & has_up)
    def _():
        seam_corner.wait_recv()
        add(seam_in, W, 0)

    when(sends_right, corner.wait_send, cols.wait_send, cols2.wait_send)
    when(has_down, *[copy.wait_send for copy in pieces_r + pieces_l])
    when(at_seam, *[copy.wait_send for copy in parts])
    when(at_seam & has_down, seam_corner.wait_send)
    when(relays_quarter, quarter_on.wait_send)
    when(relays_half, half_on.wait_send)


PIECES_R = (256,)
PIECES_L = (64, 192)


def back(gext, part):
    dma = pltpu.SemaphoreType.DMA
    vmem = pl.BlockSpec(memory_space=pltpu.VMEM)
    square = VMEM((2, 2, W, H), F32)
    return pl.pallas_call(
        back_kernel,
        out_shape=(jax.ShapeDtypeStruct((2, T, T), F32), jax.ShapeDtypeStruct((2, W, W), F32)),
        in_specs=[vmem, vmem],
        out_specs=(vmem, vmem),
        scratch_shapes=[
            square, VMEM((2, 2, T, H), F32), square, square, square, square, square,
            VMEM((4 * W, H), F32), VMEM((2, W, H), F32), VMEM((2 * W, H), F32),
            VMEM((7, 64, H), F32), VMEM((64, H), F32), VMEM((7, 8, H), F32),
            dma((10,)), dma((10,)), dma((3,)), dma((3,)), dma((2,)), dma((2,)), dma((14,)), dma((14,)), dma((14,)), dma((14,)),
        ],
        compiler_params=pltpu.CompilerParams(
            collective_id=1, has_side_effects=True, vmem_limit_bytes=24 * MIB
        ),
        name="back",
    )(gext, part)


def ahead_kernel(tile, amps, ext, amps_out, relay_in, amp_buf, h_send, h_recv, t_sem, a_sem):
    row, col, x, y, z, core = place()
    down, up = ((row + 1) % N_ROW, col), ((row + N_ROW - 1) % N_ROW, col)
    to_right, to_left = (row, (col + 1) % N_COL), (row, (col + N_COL - 1) % N_COL)
    at_seam, past_seam = col == SEAM, col == SEAM + 1
    has_down, has_up = row < N_ROW - 1, row > 0
    sends_left = (col > 0) & (col != SEAM + 1)
    gets_right = (col < N_COL - 1) & (col != SEAM)
    side, idle_side = (5 - x) % 4, (3 - x) % 4
    half, other_half = jnp.where(x == 2, 0, W), jnp.where(x == 2, W, 0)
    relays_half, relays_quarter = (y == 0) & (core == 1) & (x >= 2), (y == 0) & (x < 2)
    is_relay = relays_half | relays_quarter
    source = at_chip(jnp.where(x >= 2, 5 - x, 3 - x), 0, z, 0)
    target = at_chip(jnp.where(x >= 2, 3 - x, 1 - x), 3, z, 1)

    lanes = [
        pltpu.make_async_copy(tile.at[:, :, pl.ds(H * n, H)], ext.at[:, n, pl.ds(0, T), :], t_sem.at[n])
        for n in range(T // H)
    ]
    halves = [
        pltpu.make_async_copy(amps.at[:, :, pl.ds(H * n, H)], amp_buf.at[:, n], a_sem.at[n])
        for n in range(2)
    ]
    for copy in lanes + halves:
        copy.start()
    barrier = greet([down, up, to_left, to_right])

    @pl.when(past_seam)
    def _():
        greet([at_chip(side, 0, z, 1)] + [at_chip(idle_side, 0, z, n) for n in range(2)])
        greet([((row + N_ROW - 1) % N_ROW, SEAM)])

    @pl.when(at_seam)
    def _():
        greet([at_chip((3 - x) % 4, 0, z, 1)] + [at_chip((1 - x) % 4, 0, z, n) for n in range(2)])
        greet([((row + 1) % N_ROW, SEAM + 1)])

    @pl.when(is_relay)
    def _():
        greet([source, target])

    extra = jnp.where(at_seam | past_seam, 4, 0) + jnp.where(is_relay, 2, 0)
    pl.semaphore_wait(barrier, 4 + extra)

    halo = (h_send, h_recv)
    cols = remote(area(ext, 0, 0, T), area(ext, 4, 0, T), halo, 0, to_left)
    rows_l = remote(area(ext, 0, 0, W), area(ext, 0, T, W), halo, 1, up)
    rows_r = remote(area(ext, 2, 0, W), area(ext, 2, T, W), halo, 2, up)
    on_left = remote(area(ext, 0, T, W), area(ext, 4, T, W), halo, 3, to_left)
    seam_corner = remote(area(ext, 0, 0, W), area(ext, 4, T, W), halo, 4, ((row + N_ROW - 1) % N_ROW, SEAM))
    quarter_in = relay_in.at[:, :, pl.ds(0, H), :]
    parts = [remote(at_rows(ext, 0, half, W), relay_in, halo, 5, at_chip(side, 0, z, 1))]
    for n in range(2):
        parts.append(remote(at_rows(ext, 0, other_half + H * n, H), quarter_in, halo, 6 + n, at_chip(idle_side, 0, z, n)))
    half_in = remote(relay_in, relay_in, halo, 5, target)
    half_on = remote(relay_in, at_rows(ext, 4, jnp.where(x == 3, 0, W), W), halo, 8, target)
    quarter = remote(quarter_in, quarter_in, halo, 6 + core, target)
    quarter_on = remote(quarter_in, at_rows(ext, 4, jnp.where(x == 1, W, 0) + H * core, H), halo, 9 + core, target)
    got = [remote(relay_in, area(ext, 4, 0, W), halo, 8, target)]
    got += [remote(quarter_in, area(ext, 4, 0, H), halo, 9 + n, target) for n in range(2)]

    lanes[0].wait()
    lanes[1].wait()
    when(past_seam, parts[1].start, parts[2].start, parts[0].start)
    when(past_seam & has_up, seam_corner.start)
    when(has_up, rows_l.start)
    when(sends_left, cols.start)
    lanes[2].wait()
    lanes[3].wait()
    when(has_up, rows_r.start)
    for copy in halves:
        copy.wait()

    source_at = lax.broadcasted_iota(jnp.int32, (W, W), 0)
    place_at = lax.broadcasted_iota(jnp.int32, (W, W), 1)
    odd = (place_at >= H).astype(jnp.int32)
    chosen = (source_at == 2 * (place_at - H * odd) + odd).astype(F32).astype(BF16)

    def reorder_slot(k, _):
        half = jnp.concatenate(
            [
                jnp.concatenate([amp_buf[k, n, pl.ds(start, H, stride=2), :] for n in range(2)], axis=1)
                for start in range(2)
            ],
            axis=0,
        )
        high, mid = high_low(half)
        low = (half - high.astype(F32) - mid.astype(F32)).astype(BF16)
        amps_out[k] = dot(high, chosen) + dot(mid, chosen) + dot(low, chosen)
        return 0

    lax.fori_loop(0, amps.shape[0] // 2, reorder_slot, 0)
    when(relays_quarter, quarter.wait_recv, quarter_on.start)
    when(relays_half, half_in.wait_recv, half_on.start)
    lax.fori_loop(amps.shape[0] // 2, amps.shape[0], reorder_slot, 0)
    when(has_down, rows_l.wait_recv)
    when(has_down & sends_left, on_left.start)
    when(has_down, rows_r.wait_recv)
    when(gets_right, cols.wait_recv)
    when(at_seam, *[copy.wait_recv for copy in got])
    when(gets_right & has_down, on_left.wait_recv)
    when(at_seam & has_down, seam_corner.wait_recv)
    when(sends_left, cols.wait_send)
    when(has_up, rows_l.wait_send, rows_r.wait_send)
    when(has_down & sends_left, on_left.wait_send)
    when(past_seam, *[copy.wait_send for copy in parts])
    when(past_seam & has_up, seam_corner.wait_send)
    when(relays_quarter, quarter_on.wait_send)
    when(relays_half, half_on.wait_send)


def ahead(tile, amps):
    dma = pltpu.SemaphoreType.DMA
    vmem = pl.BlockSpec(memory_space=pltpu.VMEM)
    hbm = pl.BlockSpec(memory_space=pltpu.HBM)
    return pl.pallas_call(
        ahead_kernel,
        out_shape=(jax.ShapeDtypeStruct(EXT, F32), jax.ShapeDtypeStruct(amps.shape, F32)),
        in_specs=[hbm, hbm],
        out_specs=(vmem, vmem),
        scratch_shapes=[
            VMEM((2, 2, W, H), F32), VMEM((amps.shape[0], 2, W, H), F32),
            dma((11,)), dma((11,)), dma((T // H,)), dma((2,)),
        ],
        compiler_params=pltpu.CompilerParams(
            collective_id=0, has_side_effects=True, vmem_limit_bytes=24 * MIB
        ),
        name="ahead",
    )(pltpu.with_memory_space_constraint(tile, pltpu.HBM), pltpu.with_memory_space_constraint(amps, pltpu.HBM))


def on_device(object_tile, probe, amplitudes, positions, counts):
    ext, amps = ahead(object_tile, amplitudes[0, 0])
    gext, part = run_slots(positions[0, 0].T, counts, ext, amps, probe)
    return back(gext, part)


def solution(mesh):
    in_specs = (
        P(None, "row", "col"),
        P(),
        P("row", "col", None, None, None),
        P("row", "col", None, None),
        P("row", None),
    )
    out_specs = (P(None, "row", "col"), P())
    return jax.shard_map(
        on_device, mesh=mesh, in_specs=in_specs, out_specs=out_specs, check_vma=False
    )
```

```python
import math

import jax
import jax.numpy as jnp
import numpy as np
from jax import lax
from jax.experimental import pallas as pl
from jax.experimental.pallas import tpu as pltpu
from jax.sharding import PartitionSpec as P

smooth_term = 0.01
F32 = jnp.float32
BF16 = jnp.bfloat16
W = 256
H = 128
T = 512
CH = 32
TILES = 6
VMEM = pltpu.VMEM
MESH = pl.DeviceIdType.MESH
N_ROW, N_COL = 8, 16
SEAM = 7

EXT = (2, TILES, T + W, H)
MIB = 1024 * 1024


def tables():
    n = np.arange(H)
    even = np.exp(-2j * np.pi * np.outer(n, n) / H) / math.sqrt(W)
    odd = np.exp(-2j * np.pi * n / W)[:, None] * even

    def real_form(z):
        return np.block([[z.real, z.imag], [-z.imag, z.real]])

    pair = [real_form(even), real_form(odd)]
    return np.stack(pair + [table.T for table in pair]).astype(np.float32)


def high_low(value):
    high = value.astype(BF16)
    return high, (value - high.astype(F32)).astype(BF16)


def put(ref, rows, cols, value):
    ref[0, rows, cols], ref[1, rows, cols] = high_low(value)


def dot(a, b):
    return jnp.dot(a, b, preferred_element_type=F32)


def by_right(x, t, n):
    both = dot(x[...].reshape(2 * W, W), t[n, 0])
    return both[:W] + both[W:] + dot(x[0], t[n, 1])


def by_left(x, t, n):
    both = dot(t[n].reshape(2 * W, W), x[0])
    return both[:W] + both[W:] + dot(t[n, 0], x[1])


def slot_steps(r, c, live, ext, gext, probe, amp, t, win, xe, xo, ye, yo, pgrad):
    j0 = lax.shift_right_logical(c, 7)
    s = lax.bitwise_and(c, 127)
    back_shift = lax.bitwise_and(128 - s, 127)
    lane = lax.broadcasted_iota(jnp.int32, (CH, H), 1)
    first = lane < 128 - s
    left, right, both = pl.ds(0, H), pl.ds(H, H), pl.ds(0, W)
    for i in range(W // CH):
        rows = pl.ds(i * CH, CH)
        parts = []
        for p in range(2):
            q = [
                pltpu.roll(ext[p, j0 + n, pl.ds(r + i * CH, CH), :], back_shift, 1)
                for n in range(3)
            ]
            a = jnp.where(first, q[0], q[1])
            b = jnp.where(first, q[1], q[2])
            win[p, rows, left] = a
            win[p, rows, right] = b
            parts.append((a, b))
        (are, bre), (aim, bim) = parts
        pra, prb = probe[0, rows, left], probe[0, rows, right]
        pia, pib = probe[1, rows, left], probe[1, rows, right]
        ea_re = pra * are - pia * aim
        ea_im = pra * aim + pia * are
        eb_re = prb * bre - pib * bim
        eb_im = prb * bim + pib * bre
        put(xe, rows, left, ea_re + eb_re)
        put(xe, rows, right, ea_im + eb_im)
        put(xo, rows, left, ea_re - eb_re)
        put(xo, rows, right, ea_im - eb_im)
    yield
    ye[...] = by_right(xe, t, 0)
    yo[...] = by_right(xo, t, 1)
    yield
    for i in range(H // CH):
        top = pl.ds(i * CH, CH)
        bot = pl.ds(H + i * CH, CH)
        for cols, y in ((left, ye), (right, yo)):
            for part, lanes in ((0, left), (H, right)):
                a, b = y[top, lanes], y[bot, lanes]
                put(xe, pl.ds(part + i * CH, CH), cols, a + b)
                put(xo, pl.ds(part + i * CH, CH), cols, a - b)
    yield
    ye[...] = by_left(xe, t, 2)
    yo[...] = by_left(xo, t, 3)
    yield
    for i in range(H // CH):
        for at, y, x in ((0, ye, xe), (H, yo, xo)):
            re = y[pl.ds(i * CH, CH), :]
            im = y[pl.ds(H + i * CH, CH), :]
            a = amp[pl.ds(at + i * CH, CH), :]
            f = (2.0 - (2.0 * a) * lax.rsqrt(re * re + im * im + smooth_term)) * live
            put(x, pl.ds(i * CH, CH), both, f * re)
            put(x, pl.ds(H + i * CH, CH), both, f * im)
    yield
    ye[...] = by_left(xe, t, 0)
    yo[...] = by_left(xo, t, 1)
    yield
    for i in range(H // CH):
        for part, lanes in ((0, left), (H, right)):
            e = ye[pl.ds(part + i * CH, CH), :]
            o = yo[pl.ds(part + i * CH, CH), :]
            for at, value in ((0, e + o), (H, e - o)):
                rows = pl.ds(at + i * CH, CH)
                put(xe, rows, lanes, value[:, 0:H])
                put(xo, rows, lanes, value[:, H:W])
    yield
    ye[...] = by_right(xe, t, 2)
    yo[...] = by_right(xo, t, 3)
    yield
    later = lane >= s
    for i in range(W // CH):
        rows = pl.ds(i * CH, CH)
        e_re, e_im = ye[rows, left], ye[rows, right]
        o_re, o_im = yo[rows, left], yo[rows, right]
        terms = []
        for n, cols, b_re, b_im in ((0, left, e_re + o_re, e_im + o_im), (1, right, e_re - o_re, e_im - o_im)):
            pr, pi = probe[0, rows, cols], probe[1, rows, cols]
            wr, wi = win[0, rows, cols], win[1, rows, cols]
            pgrad[n, rows, :] += wr * b_re + wi * b_im
            pgrad[2 + n, rows, :] += wr * b_im - wi * b_re
            terms.append((pr * b_re + pi * b_im, pr * b_im - pi * b_re))
        for p in range(2):
            ra = pltpu.roll(terms[0][p], s, 1)
            rb = pltpu.roll(terms[1][p], s, 1)
            at = pl.ds(r + i * CH, CH)
            gext[p, j0, at, :] += jnp.where(later, ra, 0.0)
            gext[p, j0 + 1, at, :] += jnp.where(later, rb, ra)
            gext[p, j0 + 2, at, :] += jnp.where(later, 0.0, rb)
    yield


def interleave(streams, lag):
    waiting = [[stream, n * lag] for n, stream in enumerate(streams)]
    while waiting:
        for item in list(waiting):
            if item[1] > 0:
                item[1] -= 1
            elif next(item[0], waiting) is waiting:
                waiting.remove(item)


def slots_kernel(
    pos, counts, ext, amps, probe, table, gext, pgrad, amp_buf, t, win, xe, xo, ye, yo, amp_sem
):
    count = counts[0, lax.axis_index("col")]
    groups = lax.div(count + U - 1, U)

    def amp_copy(n, buf):
        return pltpu.make_async_copy(amps.at[pl.ds(U * n, U)], amp_buf.at[buf], amp_sem.at[buf])

    @pl.when(count > 0)
    def _():
        amp_copy(0, 0).start()

    gext[...] = jnp.zeros_like(gext)
    pgrad[...] = jnp.zeros_like(pgrad)
    for n in range(4):
        t[n, 0], t[n, 1] = high_low(table[n])

    def body(n, _):
        buf = lax.bitwise_and(n, 1)

        @pl.when(n + 1 < groups)
        def _():
            amp_copy(n + 1, 1 - buf).start()

        amp_copy(n, buf).wait()
        streams = []
        for u in range(U):
            k = U * n + u
            live = (k < count).astype(F32)
            streams.append(
                slot_steps(
                    pos[0, k], pos[1, k], live, ext, gext, probe, amp_buf.at[buf, u], t,
                    win.at[u], xe.at[u], xo.at[u], ye.at[u], yo.at[u], pgrad,
                )
            )
        interleave(streams, LAG)
        return 0

    lax.fori_loop(0, groups, body, 0)


LAG = 1
U = 4


def run_slots(own_pos, counts, ext, amps, probe):
    vmem = pl.BlockSpec(memory_space=pltpu.VMEM)
    smem = pl.BlockSpec(memory_space=pltpu.SMEM)
    return pl.pallas_call(
        slots_kernel,
        out_shape=(jax.ShapeDtypeStruct(EXT, F32), jax.ShapeDtypeStruct((4, W, H), F32)),
        in_specs=[smem, smem, vmem, pl.BlockSpec(memory_space=pl.ANY), vmem, vmem],
        out_specs=(vmem, vmem),
        scratch_shapes=[
            VMEM((2, U, W, W), F32),
            VMEM((4, 2, W, W), BF16),
            VMEM((U, 2, W, W), F32),
            VMEM((U, 2, W, W), BF16),
            VMEM((U, 2, W, W), BF16),
            VMEM((U, W, W), F32),
            VMEM((U, W, W), F32),
            pltpu.SemaphoreType.DMA((2,)),
        ],
        compiler_params=pltpu.CompilerParams(vmem_limit_bytes=28 * MIB),
        name="slots",
    )(own_pos, counts, ext, amps, probe, jnp.asarray(tables()))


def place():
    row, col = lax.axis_index("row"), lax.axis_index("col")
    z, x_lo = row // 2, row % 2
    x_hi, y, core = col // 8, (col // 2) % 4, col % 2
    return row, col, x_hi * 2 + x_lo, y, z, core


def at_chip(x, y, z, core):
    return (z * 2 + x % 2, (x // 2) * 8 + y * 2 + core)


def remote(src, dst, sems, n, device):
    return pltpu.make_async_remote_copy(
        src_ref=src, dst_ref=dst, send_sem=sems[0].at[n], recv_sem=sems[1].at[n],
        device_id=device, device_id_type=MESH,
    )


def block(start, count):
    return pl.ds(pl.multiple_of(start, 8), count)


def greet(devices):
    barrier = pltpu.get_barrier_semaphore()
    for device in devices:
        pl.semaphore_signal(barrier, inc=1, device_id=device, device_id_type=MESH)
    return barrier


def when(cond, *actions):
    @pl.when(cond)
    def _():
        for action in actions:
            action()


def area(ref, tile, row, rows):
    return ref.at[:, pl.ds(tile, 2), pl.ds(row, rows), :]


def at_rows(ref, tile, row, rows):
    return ref.at[:, pl.ds(tile, 2), block(row, rows), :]


def back_kernel(
    gext, part, out, out_p, corner_in, right_in, below_l_in, below_r_in, seam_in, relay_in, below_sum,
    full, got0, acc0, got1, acc1, got2,
    h_send, h_recv, r_send, r_recv, m_send, m_recv, p_send, p_recv, x_send, x_recv,
):
    row, col, x, y, z, core = place()
    down, up = ((row + 1) % N_ROW, col), ((row + N_ROW - 1) % N_ROW, col)
    right, left = (row, (col + 1) % N_COL), (row, (col + N_COL - 1) % N_COL)
    mate = (row, col + 1 - 2 * core)
    pair, place_in_pair = (x + 1) // 2 % 2, x // 2
    near, far = place_in_pair * 4 + y, pair * 4 + z

    def near_peer(q):
        return (near + q) % 8

    def near_id(q):
        n = near_peer(q)
        return at_chip(pair + n // 4 * (3 - 2 * pair), n % 4, z, core)

    def far_peer(q):
        return (far + q) % 8

    def far_id(q):
        n = far_peer(q)
        return at_chip(n // 4 + place_in_pair * (3 - 2 * (n // 4)), y, n % 4, core)

    at_seam, past_seam = col == SEAM, col == SEAM + 1
    side, idle_side = (5 - x) % 4, (3 - x) % 4
    half, other_half = jnp.where(x == 0, 0, W), jnp.where(x == 0, W, 0)
    relays_half, relays_quarter = (y == 3) & (core == 0) & (x < 2), (y == 3) & (x >= 2)
    is_relay = relays_half | relays_quarter
    source = at_chip(jnp.where(x < 2, 1 - x, 3 - x), 3, z, 1)
    target = at_chip(jnp.where(x < 2, 3 - x, 5 - x), 0, z, 0)
    has_down, has_up = row < N_ROW - 1, row > 0
    sends_right = (col < N_COL - 1) & (col != SEAM)
    gets_left = (col > 0) & (col != SEAM + 1)
    diagonal = ((row + 1) % N_ROW, SEAM + 1)
    diagonal_from = ((row + N_ROW - 1) % N_ROW, SEAM)

    barrier = greet([mate, down, up, left, right] + [near_id(q) for q in range(1, 8)] + [far_id(q) for q in range(1, 8)])

    @pl.when(at_seam)
    def _():
        greet([at_chip(side, 3, z, 0)] + [at_chip(idle_side, 3, z, n) for n in range(2)] + [diagonal])

    @pl.when(past_seam)
    def _():
        greet([at_chip(idle_side, 3, z, 0)] + [at_chip(side, 3, z, n) for n in range(2)] + [diagonal_from])

    @pl.when(is_relay)
    def _():
        greet([source, target])

    extra = jnp.where(at_seam | past_seam, 4, 0) + jnp.where(is_relay, 2, 0)
    pl.semaphore_wait(barrier, 19 + extra)

    halo = (h_send, h_recv)
    corner = remote(area(gext, 4, T, W), corner_in, halo, 0, right)
    cols = remote(area(gext, 4, 0, W), area(right_in, 0, 0, W), halo, 1, right)
    cols2 = remote(area(gext, 4, W, W), area(right_in, 0, W, W), halo, 2, right)
    seam_corner = remote(area(gext, 4, T, W), seam_in, halo, 3, diagonal)
    quarter_in = relay_in.at[:, :, pl.ds(0, H), :]
    parts = [remote(at_rows(gext, 4, half, W), relay_in, halo, 4, at_chip(side, 3, z, 0))]
    for n in range(2):
        parts.append(remote(at_rows(gext, 4, other_half + H * n, H), quarter_in, halo, 5 + n, at_chip(idle_side, 3, z, n)))
    half_in = remote(relay_in, relay_in, halo, 4, target)
    half_on = remote(relay_in, at_rows(right_in, 0, jnp.where(x == 1, 0, W), W), halo, 7, target)
    quarter = remote(quarter_in, quarter_in, halo, 5 + core, target)
    quarter_on = remote(quarter_in, at_rows(right_in, 0, jnp.where(x == 3, W, 0) + H * core, H), halo, 8 + core, target)
    got = [remote(relay_in, area(right_in, 0, 0, W), halo, 7, target)]
    got += [remote(quarter_in, area(right_in, 0, 0, H), halo, 8 + n, target) for n in range(2)]
    pieces_r, pieces_l = [], []
    at = 0
    for n, rows in enumerate(PIECES_R):
        pieces_r.append(remote(area(gext, 2, T + at, rows), area(below_r_in, 0, at, rows), (r_send, r_recv), n, down))
        at += rows
    at = 0
    for n, rows in enumerate(PIECES_L):
        sems = (r_send, r_recv)
        pieces_l.append(remote(area(below_sum, 0, at, rows), area(below_l_in, 0, at, rows), sems, len(PIECES_R) + n, down))
        at += rows

    def start(copies):
        for copy in copies:
            copy.start()

    def wait(copies):
        for copy in copies:
            copy.wait()

    swap = remote(part.at[pl.ds(2 * (1 - core), 2)], got0, (m_send, m_recv), 0, mate)
    swap.start()
    when(at_seam, parts[1].start, parts[2].start, parts[0].start)
    when(at_seam & has_down, seam_corner.start)
    when(sends_right, corner.start)
    when(has_down, pieces_r[0].start)
    swap.wait()
    for n in range(2):
        acc0[pl.ds(n * W, W), :] = part[2 * core + n] + got0[n]
    spread = [
        remote(acc0.at[block(near_peer(q) * 64, 64)], got1.at[q - 1], (p_send, p_recv), q - 1, near_id(q))
        for q in range(1, 8)
    ]
    start(spread)
    when(sends_right, cols.start)
    below_sum[...] = area(gext, 0, T, W)[...]

    @pl.when(gets_left)
    def _():
        corner.wait_recv()
        below_sum[...] += corner_in[...]

    wait(spread)
    total = acc0[block(near * 64, 64), :]
    for q in range(7):
        total = total + got1[q]
    acc1[...] = total
    spread = [
        remote(acc1.at[block(far_peer(q) * 8, 8)], got2.at[q - 1], (x_send, x_recv), q - 1, far_id(q))
        for q in range(1, 8)
    ]
    start(spread)
    wait(spread)
    base1 = core * 512 + near * 64
    own = block(base1 + far * 8, 8)
    total = acc1[block(far * 8, 8), :]
    for q in range(7):
        total = total + got2[q]
    full[own, :] = total
    when(relays_quarter, quarter.wait_recv, quarter_on.start)
    spread = [remote(full.at[own], full.at[own], (x_send, x_recv), 6 + q, far_id(q)) for q in range(1, 8)]
    start(spread)
    when(has_down, pieces_l[0].start)
    wait(spread)
    own1 = block(base1, 64)
    spread = [remote(full.at[own1], full.at[own1], (p_send, p_recv), 6 + q, near_id(q)) for q in range(1, 8)]
    start(spread)
    when(relays_half, half_in.wait_recv, half_on.start)
    when(has_down, *[copy.start for copy in pieces_l[1:]])
    when(sends_right, cols2.start)
    for n in range(T // H):
        out[:, :, pl.ds(n * H, H)] = gext[:, n, pl.ds(0, T), :]
    wait(spread)
    own0 = block(core * 512, 512)
    swap = remote(full.at[own0], full.at[own0], (m_send, m_recv), 1, mate)
    swap.start()
    swap.wait()
    for p in range(2):
        for half in range(2):
            out_p[p, :, pl.ds(H * half, H)] = full[pl.ds((2 * p + half) * W, W), :]

    def add(value, rows, at):
        for n in range(2):
            out[:, pl.ds(0, rows), pl.ds((at + n) * H, H)] += value[:, n]

    @pl.when(has_up)
    def _():
        for copy in pieces_r:
            copy.wait_recv()
        add(below_r_in, W, 2)

    @pl.when(gets_left)
    def _():
        cols.wait_recv()
        cols2.wait_recv()
        add(right_in, T, 0)

    @pl.when(past_seam)
    def _():
        for copy in got:
            copy.wait_recv()
        add(right_in, T, 0)

    @pl.when(has_up)
    def _():
        for copy in pieces_l:
            copy.wait_recv()
        add(below_l_in, W, 0)

    @pl.when(past_seam & has_up)
    def _():
        seam_corner.wait_recv()
        add(seam_in, W, 0)

    when(sends_right, corner.wait_send, cols.wait_send, cols2.wait_send)
    when(has_down, *[copy.wait_send for copy in pieces_r + pieces_l])
    when(at_seam, *[copy.wait_send for copy in parts])
    when(at_seam & has_down, seam_corner.wait_send)
    when(relays_quarter, quarter_on.wait_send)
    when(relays_half, half_on.wait_send)


PIECES_R = (256,)
PIECES_L = (64, 192)


def back(gext, part):
    dma = pltpu.SemaphoreType.DMA
    vmem = pl.BlockSpec(memory_space=pltpu.VMEM)
    square = VMEM((2, 2, W, H), F32)
    return pl.pallas_call(
        back_kernel,
        out_shape=(jax.ShapeDtypeStruct((2, T, T), F32), jax.ShapeDtypeStruct((2, W, W), F32)),
        in_specs=[vmem, vmem],
        out_specs=(vmem, vmem),
        scratch_shapes=[
            square, VMEM((2, 2, T, H), F32), square, square, square, square, square,
            VMEM((4 * W, H), F32), VMEM((2, W, H), F32), VMEM((2 * W, H), F32),
            VMEM((7, 64, H), F32), VMEM((64, H), F32), VMEM((7, 8, H), F32),
            dma((10,)), dma((10,)), dma((3,)), dma((3,)), dma((2,)), dma((2,)), dma((14,)), dma((14,)), dma((14,)), dma((14,)),
        ],
        compiler_params=pltpu.CompilerParams(
            collective_id=1, has_side_effects=True, vmem_limit_bytes=24 * MIB
        ),
        name="back",
    )(gext, part)


def ahead_kernel(tile, amps, ext, amps_out, relay_in, amp_buf, h_send, h_recv, t_sem, a_sem):
    row, col, x, y, z, core = place()
    down, up = ((row + 1) % N_ROW, col), ((row + N_ROW - 1) % N_ROW, col)
    to_right, to_left = (row, (col + 1) % N_COL), (row, (col + N_COL - 1) % N_COL)
    at_seam, past_seam = col == SEAM, col == SEAM + 1
    has_down, has_up = row < N_ROW - 1, row > 0
    sends_left = (col > 0) & (col != SEAM + 1)
    gets_right = (col < N_COL - 1) & (col != SEAM)
    side, idle_side = (5 - x) % 4, (3 - x) % 4
    half, other_half = jnp.where(x == 2, 0, W), jnp.where(x == 2, W, 0)
    relays_half, relays_quarter = (y == 0) & (core == 1) & (x >= 2), (y == 0) & (x < 2)
    is_relay = relays_half | relays_quarter
    source = at_chip(jnp.where(x >= 2, 5 - x, 3 - x), 0, z, 0)
    target = at_chip(jnp.where(x >= 2, 3 - x, 1 - x), 3, z, 1)

    lanes = [
        pltpu.make_async_copy(tile.at[:, :, pl.ds(H * n, H)], ext.at[:, n, pl.ds(0, T), :], t_sem.at[n])
        for n in range(T // H)
    ]
    halves = [
        pltpu.make_async_copy(amps.at[:, :, pl.ds(H * n, H)], amp_buf.at[:, n], a_sem.at[n])
        for n in range(2)
    ]
    for copy in lanes + halves:
        copy.start()
    barrier = greet([down, up, to_left, to_right])

    @pl.when(past_seam)
    def _():
        greet([at_chip(side, 0, z, 1)] + [at_chip(idle_side, 0, z, n) for n in range(2)])
        greet([((row + N_ROW - 1) % N_ROW, SEAM)])

    @pl.when(at_seam)
    def _():
        greet([at_chip((3 - x) % 4, 0, z, 1)] + [at_chip((1 - x) % 4, 0, z, n) for n in range(2)])
        greet([((row + 1) % N_ROW, SEAM + 1)])

    @pl.when(is_relay)
    def _():
        greet([source, target])

    extra = jnp.where(at_seam | past_seam, 4, 0) + jnp.where(is_relay, 2, 0)
    pl.semaphore_wait(barrier, 4 + extra)

    halo = (h_send, h_recv)
    cols = remote(area(ext, 0, 0, T), area(ext, 4, 0, T), halo, 0, to_left)
    rows_l = remote(area(ext, 0, 0, W), area(ext, 0, T, W), halo, 1, up)
    rows_r = remote(area(ext, 2, 0, W), area(ext, 2, T, W), halo, 2, up)
    on_left = remote(area(ext, 0, T, W), area(ext, 4, T, W), halo, 3, to_left)
    seam_corner = remote(area(ext, 0, 0, W), area(ext, 4, T, W), halo, 4, ((row + N_ROW - 1) % N_ROW, SEAM))
    quarter_in = relay_in.at[:, :, pl.ds(0, H), :]
    parts = [remote(at_rows(ext, 0, half, W), relay_in, halo, 5, at_chip(side, 0, z, 1))]
    for n in range(2):
        parts.append(remote(at_rows(ext, 0, other_half + H * n, H), quarter_in, halo, 6 + n, at_chip(idle_side, 0, z, n)))
    half_in = remote(relay_in, relay_in, halo, 5, target)
    half_on = remote(relay_in, at_rows(ext, 4, jnp.where(x == 3, 0, W), W), halo, 8, target)
    quarter = remote(quarter_in, quarter_in, halo, 6 + core, target)
    quarter_on = remote(quarter_in, at_rows(ext, 4, jnp.where(x == 1, W, 0) + H * core, H), halo, 9 + core, target)
    got = [remote(relay_in, area(ext, 4, 0, W), halo, 8, target)]
    got += [remote(quarter_in, area(ext, 4, 0, H), halo, 9 + n, target) for n in range(2)]

    lanes[0].wait()
    lanes[1].wait()
    when(past_seam, parts[1].start, parts[2].start, parts[0].start)
    when(past_seam & has_up, seam_corner.start)
    when(has_up, rows_l.start)
    when(sends_left, cols.start)
    lanes[2].wait()
    lanes[3].wait()
    when(has_up, rows_r.start)
    for copy in halves:
        copy.wait()

    source_at = lax.broadcasted_iota(jnp.int32, (W, W), 0)
    place_at = lax.broadcasted_iota(jnp.int32, (W, W), 1)
    odd = (place_at >= H).astype(jnp.int32)
    chosen = (source_at == 2 * (place_at - H * odd) + odd).astype(F32).astype(BF16)

    def reorder_slot(k, _):
        half = jnp.concatenate(
            [
                jnp.concatenate([amp_buf[k, n, pl.ds(start, H, stride=2), :] for n in range(2)], axis=1)
                for start in range(2)
            ],
            axis=0,
        )
        high, mid = high_low(half)
        low = (half - high.astype(F32) - mid.astype(F32)).astype(BF16)
        amps_out[k] = dot(high, chosen) + dot(mid, chosen) + dot(low, chosen)
        return 0

    lax.fori_loop(0, amps.shape[0] // 2, reorder_slot, 0)
    when(relays_quarter, quarter.wait_recv, quarter_on.start)
    when(relays_half, half_in.wait_recv, half_on.start)
    lax.fori_loop(amps.shape[0] // 2, amps.shape[0], reorder_slot, 0)
    when(has_down, rows_l.wait_recv)
    when(has_down & sends_left, on_left.start)
    when(has_down, rows_r.wait_recv)
    when(gets_right, cols.wait_recv)
    when(at_seam, *[copy.wait_recv for copy in got])
    when(gets_right & has_down, on_left.wait_recv)
    when(at_seam & has_down, seam_corner.wait_recv)
    when(sends_left, cols.wait_send)
    when(has_up, rows_l.wait_send, rows_r.wait_send)
    when(has_down & sends_left, on_left.wait_send)
    when(past_seam, *[copy.wait_send for copy in parts])
    when(past_seam & has_up, seam_corner.wait_send)
    when(relays_quarter, quarter_on.wait_send)
    when(relays_half, half_on.wait_send)


def ahead(tile, amps):
    dma = pltpu.SemaphoreType.DMA
    vmem = pl.BlockSpec(memory_space=pltpu.VMEM)
    hbm = pl.BlockSpec(memory_space=pltpu.HBM)
    return pl.pallas_call(
        ahead_kernel,
        out_shape=(jax.ShapeDtypeStruct(EXT, F32), jax.ShapeDtypeStruct(amps.shape, F32)),
        in_specs=[hbm, hbm],
        out_specs=(vmem, vmem),
        scratch_shapes=[
            VMEM((2, 2, W, H), F32), VMEM((amps.shape[0], 2, W, H), F32),
            dma((11,)), dma((11,)), dma((T // H,)), dma((2,)),
        ],
        compiler_params=pltpu.CompilerParams(
            collective_id=0, has_side_effects=True, vmem_limit_bytes=24 * MIB
        ),
        name="ahead",
    )(pltpu.with_memory_space_constraint(tile, pltpu.HBM), pltpu.with_memory_space_constraint(amps, pltpu.HBM))


def on_device(object_tile, probe, amplitudes, positions, counts):
    ext, amps = ahead(object_tile, amplitudes[0, 0])
    gext, part = run_slots(positions[0, 0].T, counts, ext, amps, probe)
    return back(gext, part)


def solution(mesh):
    in_specs = (
        P(None, "row", "col"),
        P(),
        P("row", "col", None, None, None),
        P("row", "col", None, None),
        P("row", None),
    )
    out_specs = (P(None, "row", "col"), P())
    return jax.shard_map(
        on_device, mesh=mesh, in_specs=in_specs, out_specs=out_specs, check_vma=False
    )
```

```python
import math

import jax
import jax.numpy as jnp
import numpy as np
from jax import lax
from jax.experimental import pallas as pl
from jax.experimental.pallas import tpu as pltpu
from jax.sharding import PartitionSpec as P

smooth_term = 0.01
F32 = jnp.float32
BF16 = jnp.bfloat16
W = 256
H = 128
T = 512
CH = 32
TILES = 6
VMEM = pltpu.VMEM
MESH = pl.DeviceIdType.MESH
N_ROW, N_COL = 8, 16
SEAM = 7

EXT = (2, TILES, T + W, H)
MIB = 1024 * 1024


def tables():
    n = np.arange(H)
    even = np.exp(-2j * np.pi * np.outer(n, n) / H) / math.sqrt(W)
    odd = np.exp(-2j * np.pi * n / W)[:, None] * even

    def real_form(z):
        return np.block([[z.real, z.imag], [-z.imag, z.real]])

    pair = [real_form(even), real_form(odd)]
    return np.stack(pair + [table.T for table in pair]).astype(np.float32)


def high_low(value):
    high = value.astype(BF16)
    return high, (value - high.astype(F32)).astype(BF16)


def put(ref, rows, cols, value):
    ref[0, rows, cols], ref[1, rows, cols] = high_low(value)


def dot(a, b):
    return jnp.dot(a, b, preferred_element_type=F32)


def by_right(x, t, n):
    both = dot(x[...].reshape(2 * W, W), t[n, 0])
    return both[:W] + both[W:] + dot(x[0], t[n, 1])


def by_left(x, t, n):
    both = dot(t[n].reshape(2 * W, W), x[0])
    return both[:W] + both[W:] + dot(t[n, 0], x[1])


def slot_steps(r, c, live, ext, gext, probe, amp, t, win, xe, xo, ye, yo, pgrad):
    j0 = lax.shift_right_logical(c, 7)
    s = lax.bitwise_and(c, 127)
    back_shift = lax.bitwise_and(128 - s, 127)
    lane = lax.broadcasted_iota(jnp.int32, (CH, H), 1)
    first = lane < 128 - s
    left, right, both = pl.ds(0, H), pl.ds(H, H), pl.ds(0, W)
    for i in range(W // CH):
        rows = pl.ds(i * CH, CH)
        parts = []
        for p in range(2):
            q = [
                pltpu.roll(ext[p, j0 + n, pl.ds(r + i * CH, CH), :], back_shift, 1)
                for n in range(3)
            ]
            a = jnp.where(first, q[0], q[1])
            b = jnp.where(first, q[1], q[2])
            win[p, rows, left] = a
            win[p, rows, right] = b
            parts.append((a, b))
        (are, bre), (aim, bim) = parts
        pra, prb = probe[0, rows, left], probe[0, rows, right]
        pia, pib = probe[1, rows, left], probe[1, rows, right]
        ea_re = pra * are - pia * aim
        ea_im = pra * aim + pia * are
        eb_re = prb * bre - pib * bim
        eb_im = prb * bim + pib * bre
        put(xe, rows, left, ea_re + eb_re)
        put(xe, rows, right, ea_im + eb_im)
        put(xo, rows, left, ea_re - eb_re)
        put(xo, rows, right, ea_im - eb_im)
    yield
    ye[...] = by_right(xe, t, 0)
    yo[...] = by_right(xo, t, 1)
    yield
    for i in range(H // CH):
        top = pl.ds(i * CH, CH)
        bot = pl.ds(H + i * CH, CH)
        for cols, y in ((left, ye), (right, yo)):
            for part, lanes in ((0, left), (H, right)):
                a, b = y[top, lanes], y[bot, lanes]
                put(xe, pl.ds(part + i * CH, CH), cols, a + b)
                put(xo, pl.ds(part + i * CH, CH), cols, a - b)
    yield
    ye[...] = by_left(xe, t, 2)
    yo[...] = by_left(xo, t, 3)
    yield
    for i in range(H // CH):
        for at, y, x in ((0, ye, xe), (H, yo, xo)):
            re = y[pl.ds(i * CH, CH), :]
            im = y[pl.ds(H + i * CH, CH), :]
            a = amp[pl.ds(at + i * CH, CH), :]
            f = (2.0 - (2.0 * a) * lax.rsqrt(re * re + im * im + smooth_term)) * live
            put(x, pl.ds(i * CH, CH), both, f * re)
            put(x, pl.ds(H + i * CH, CH), both, f * im)
    yield
    ye[...] = by_left(xe, t, 0)
    yo[...] = by_left(xo, t, 1)
    yield
    for i in range(H // CH):
        for part, lanes in ((0, left), (H, right)):
            e = ye[pl.ds(part + i * CH, CH), :]
            o = yo[pl.ds(part + i * CH, CH), :]
            for at, value in ((0, e + o), (H, e - o)):
                rows = pl.ds(at + i * CH, CH)
                put(xe, rows, lanes, value[:, 0:H])
                put(xo, rows, lanes, value[:, H:W])
    yield
    ye[...] = by_right(xe, t, 2)
    yo[...] = by_right(xo, t, 3)
    yield
    later = lane >= s
    for i in range(W // CH):
        rows = pl.ds(i * CH, CH)
        e_re, e_im = ye[rows, left], ye[rows, right]
        o_re, o_im = yo[rows, left], yo[rows, right]
        terms = []
        for n, cols, b_re, b_im in ((0, left, e_re + o_re, e_im + o_im), (1, right, e_re - o_re, e_im - o_im)):
            pr, pi = probe[0, rows, cols], probe[1, rows, cols]
            wr, wi = win[0, rows, cols], win[1, rows, cols]
            pgrad[n, rows, :] += wr * b_re + wi * b_im
            pgrad[2 + n, rows, :] += wr * b_im - wi * b_re
            terms.append((pr * b_re + pi * b_im, pr * b_im - pi * b_re))
        for p in range(2):
            ra = pltpu.roll(terms[0][p], s, 1)
            rb = pltpu.roll(terms[1][p], s, 1)
            at = pl.ds(r + i * CH, CH)
            gext[p, j0, at, :] += jnp.where(later, ra, 0.0)
            gext[p, j0 + 1, at, :] += jnp.where(later, rb, ra)
            gext[p, j0 + 2, at, :] += jnp.where(later, 0.0, rb)
    yield


def interleave(streams, lag):
    waiting = [[stream, n * lag] for n, stream in enumerate(streams)]
    while waiting:
        for item in list(waiting):
            if item[1] > 0:
                item[1] -= 1
            elif next(item[0], waiting) is waiting:
                waiting.remove(item)


def slots_kernel(
    pos, counts, ext, amps, probe, table, gext, pgrad, amp_buf, t, win, xe, xo, ye, yo, amp_sem
):
    count = counts[0, lax.axis_index("col")]
    groups = lax.div(count + U - 1, U)

    def amp_copy(n, buf):
        return pltpu.make_async_copy(amps.at[pl.ds(U * n, U)], amp_buf.at[buf], amp_sem.at[buf])

    @pl.when(count > 0)
    def _():
        amp_copy(0, 0).start()

    gext[...] = jnp.zeros_like(gext)
    pgrad[...] = jnp.zeros_like(pgrad)
    for n in range(4):
        t[n, 0], t[n, 1] = high_low(table[n])

    def body(n, _):
        buf = lax.bitwise_and(n, 1)

        @pl.when(n + 1 < groups)
        def _():
            amp_copy(n + 1, 1 - buf).start()

        amp_copy(n, buf).wait()
        streams = []
        for u in range(U):
            k = U * n + u
            live = (k < count).astype(F32)
            streams.append(
                slot_steps(
                    pos[0, k], pos[1, k], live, ext, gext, probe, amp_buf.at[buf, u], t,
                    win.at[u], xe.at[u], xo.at[u], ye.at[u], yo.at[u], pgrad,
                )
            )
        interleave(streams, LAG)
        return 0

    lax.fori_loop(0, groups, body, 0)


LAG = 1
U = 4


def run_slots(own_pos, counts, ext, amps, probe):
    vmem = pl.BlockSpec(memory_space=pltpu.VMEM)
    smem = pl.BlockSpec(memory_space=pltpu.SMEM)
    return pl.pallas_call(
        slots_kernel,
        out_shape=(jax.ShapeDtypeStruct(EXT, F32), jax.ShapeDtypeStruct((4, W, H), F32)),
        in_specs=[smem, smem, vmem, pl.BlockSpec(memory_space=pl.ANY), vmem, vmem],
        out_specs=(vmem, vmem),
        scratch_shapes=[
            VMEM((2, U, W, W), F32),
            VMEM((4, 2, W, W), BF16),
            VMEM((U, 2, W, W), F32),
            VMEM((U, 2, W, W), BF16),
            VMEM((U, 2, W, W), BF16),
            VMEM((U, W, W), F32),
            VMEM((U, W, W), F32),
            pltpu.SemaphoreType.DMA((2,)),
        ],
        compiler_params=pltpu.CompilerParams(vmem_limit_bytes=28 * MIB),
        name="slots",
    )(own_pos, counts, ext, amps, probe, jnp.asarray(tables()))


def place():
    row, col = lax.axis_index("row"), lax.axis_index("col")
    z, x_lo = row // 2, row % 2
    x_hi, y, core = col // 8, (col // 2) % 4, col % 2
    return row, col, x_hi * 2 + x_lo, y, z, core


def at_chip(x, y, z, core):
    return (z * 2 + x % 2, (x // 2) * 8 + y * 2 + core)


def remote(src, dst, sems, n, device):
    return pltpu.make_async_remote_copy(
        src_ref=src, dst_ref=dst, send_sem=sems[0].at[n], recv_sem=sems[1].at[n],
        device_id=device, device_id_type=MESH,
    )


def block(start, count):
    return pl.ds(pl.multiple_of(start, 8), count)


def greet(devices):
    barrier = pltpu.get_barrier_semaphore()
    for device in devices:
        pl.semaphore_signal(barrier, inc=1, device_id=device, device_id_type=MESH)
    return barrier


def when(cond, *actions):
    @pl.when(cond)
    def _():
        for action in actions:
            action()


def area(ref, tile, row, rows):
    return ref.at[:, pl.ds(tile, 2), pl.ds(row, rows), :]


def at_rows(ref, tile, row, rows):
    return ref.at[:, pl.ds(tile, 2), block(row, rows), :]


def back_kernel(
    gext, part, out, out_p, corner_in, right_in, below_l_in, below_r_in, seam_in, relay_in, below_sum,
    full, got0, acc0, got1, acc1, got2,
    h_send, h_recv, r_send, r_recv, m_send, m_recv, p_send, p_recv, x_send, x_recv,
):
    row, col, x, y, z, core = place()
    down, up = ((row + 1) % N_ROW, col), ((row + N_ROW - 1) % N_ROW, col)
    right, left = (row, (col + 1) % N_COL), (row, (col + N_COL - 1) % N_COL)
    mate = (row, col + 1 - 2 * core)
    pair, place_in_pair = (x + 1) // 2 % 2, x // 2
    near, far = place_in_pair * 4 + y, pair * 4 + z

    def near_peer(q):
        return (near + q) % 8

    def near_id(q):
        n = near_peer(q)
        return at_chip(pair + n // 4 * (3 - 2 * pair), n % 4, z, core)

    def far_peer(q):
        return (far + q) % 8

    def far_id(q):
        n = far_peer(q)
        return at_chip(n // 4 + place_in_pair * (3 - 2 * (n // 4)), y, n % 4, core)

    at_seam, past_seam = col == SEAM, col == SEAM + 1
    side, idle_side = (5 - x) % 4, (3 - x) % 4
    half, other_half = jnp.where(x == 0, 0, W), jnp.where(x == 0, W, 0)
    relays_half, relays_quarter = (y == 3) & (core == 0) & (x < 2), (y == 3) & (x >= 2)
    is_relay = relays_half | relays_quarter
    source = at_chip(jnp.where(x < 2, 1 - x, 3 - x), 3, z, 1)
    target = at_chip(jnp.where(x < 2, 3 - x, 5 - x), 0, z, 0)
    has_down, has_up = row < N_ROW - 1, row > 0
    sends_right = (col < N_COL - 1) & (col != SEAM)
    gets_left = (col > 0) & (col != SEAM + 1)
    diagonal = ((row + 1) % N_ROW, SEAM + 1)
    diagonal_from = ((row + N_ROW - 1) % N_ROW, SEAM)

    barrier = greet([mate, down, up, left, right] + [near_id(q) for q in range(1, 8)] + [far_id(q) for q in range(1, 8)])

    @pl.when(at_seam)
    def _():
        greet([at_chip(side, 3, z, 0)] + [at_chip(idle_side, 3, z, n) for n in range(2)] + [diagonal])

    @pl.when(past_seam)
    def _():
        greet([at_chip(idle_side, 3, z, 0)] + [at_chip(side, 3, z, n) for n in range(2)] + [diagonal_from])

    @pl.when(is_relay)
    def _():
        greet([source, target])

    extra = jnp.where(at_seam | past_seam, 4, 0) + jnp.where(is_relay, 2, 0)
    pl.semaphore_wait(barrier, 19 + extra)

    halo = (h_send, h_recv)
    corner = remote(area(gext, 4, T, W), corner_in, halo, 0, right)
    cols = remote(area(gext, 4, 0, W), area(right_in, 0, 0, W), halo, 1, right)
    cols2 = remote(area(gext, 4, W, W), area(right_in, 0, W, W), halo, 2, right)
    seam_corner = remote(area(gext, 4, T, W), seam_in, halo, 3, diagonal)
    quarter_in = relay_in.at[:, :, pl.ds(0, H), :]
    parts = [remote(at_rows(gext, 4, half, W), relay_in, halo, 4, at_chip(side, 3, z, 0))]
    for n in range(2):
        parts.append(remote(at_rows(gext, 4, other_half + H * n, H), quarter_in, halo, 5 + n, at_chip(idle_side, 3, z, n)))
    half_in = remote(relay_in, relay_in, halo, 4, target)
    half_on = remote(relay_in, at_rows(right_in, 0, jnp.where(x == 1, 0, W), W), halo, 7, target)
    quarter = remote(quarter_in, quarter_in, halo, 5 + core, target)
    quarter_on = remote(quarter_in, at_rows(right_in, 0, jnp.where(x == 3, W, 0) + H * core, H), halo, 8 + core, target)
    got = [remote(relay_in, area(right_in, 0, 0, W), halo, 7, target)]
    got += [remote(quarter_in, area(right_in, 0, 0, H), halo, 8 + n, target) for n in range(2)]
    pieces_r, pieces_l = [], []
    at = 0
    for n, rows in enumerate(PIECES_R):
        pieces_r.append(remote(area(gext, 2, T + at, rows), area(below_r_in, 0, at, rows), (r_send, r_recv), n, down))
        at += rows
    at = 0
    for n, rows in enumerate(PIECES_L):
        sems = (r_send, r_recv)
        pieces_l.append(remote(area(below_sum, 0, at, rows), area(below_l_in, 0, at, rows), sems, len(PIECES_R) + n, down))
        at += rows

    def start(copies):
        for copy in copies:
            copy.start()

    def wait(copies):
        for copy in copies:
            copy.wait()

    swap = remote(part.at[pl.ds(2 * (1 - core), 2)], got0, (m_send, m_recv), 0, mate)
    swap.start()
    when(at_seam, parts[1].start, parts[2].start, parts[0].start)
    when(at_seam & has_down, seam_corner.start)
    when(sends_right, corner.start)
    when(has_down, pieces_r[0].start)
    swap.wait()
    for n in range(2):
        acc0[pl.ds(n * W, W), :] = part[2 * core + n] + got0[n]
    spread = [
        remote(acc0.at[block(near_peer(q) * 64, 64)], got1.at[q - 1], (p_send, p_recv), q - 1, near_id(q))
        for q in range(1, 8)
    ]
    start(spread)
    when(sends_right, cols.start)
    below_sum[...] = area(gext, 0, T, W)[...]

    @pl.when(gets_left)
    def _():
        corner.wait_recv()
        below_sum[...] += corner_in[...]

    wait(spread)
    total = acc0[block(near * 64, 64), :]
    for q in range(7):
        total = total + got1[q]
    acc1[...] = total
    spread = [
        remote(acc1.at[block(far_peer(q) * 8, 8)], got2.at[q - 1], (x_send, x_recv), q - 1, far_id(q))
        for q in range(1, 8)
    ]
    start(spread)
    wait(spread)
    base1 = core * 512 + near * 64
    own = block(base1 + far * 8, 8)
    total = acc1[block(far * 8, 8), :]
    for q in range(7):
        total = total + got2[q]
    full[own, :] = total
    when(relays_quarter, quarter.wait_recv, quarter_on.start)
    spread = [remote(full.at[own], full.at[own], (x_send, x_recv), 6 + q, far_id(q)) for q in range(1, 8)]
    start(spread)
    when(has_down, pieces_l[0].start)
    wait(spread)
    own1 = block(base1, 64)
    spread = [remote(full.at[own1], full.at[own1], (p_send, p_recv), 6 + q, near_id(q)) for q in range(1, 8)]
    start(spread)
    when(relays_half, half_in.wait_recv, half_on.start)
    when(has_down, *[copy.start for copy in pieces_l[1:]])
    when(sends_right, cols2.start)
    for n in range(T // H):
        out[:, :, pl.ds(n * H, H)] = gext[:, n, pl.ds(0, T), :]
    wait(spread)
    own0 = block(core * 512, 512)
    swap = remote(full.at[own0], full.at[own0], (m_send, m_recv), 1, mate)
    swap.start()
    swap.wait()
    for p in range(2):
        for half in range(2):
            out_p[p, :, pl.ds(H * half, H)] = full[pl.ds((2 * p + half) * W, W), :]

    def add(value, rows, at):
        for n in range(2):
            out[:, pl.ds(0, rows), pl.ds((at + n) * H, H)] += value[:, n]

    @pl.when(has_up)
    def _():
        for copy in pieces_r:
            copy.wait_recv()
        add(below_r_in, W, 2)

    @pl.when(gets_left)
    def _():
        cols.wait_recv()
        cols2.wait_recv()
        add(right_in, T, 0)

    @pl.when(past_seam)
    def _():
        for copy in got:
            copy.wait_recv()
        add(right_in, T, 0)

    @pl.when(has_up)
    def _():
        for copy in pieces_l:
            copy.wait_recv()
        add(below_l_in, W, 0)

    @pl.when(past_seam & has_up)
    def _():
        seam_corner.wait_recv()
        add(seam_in, W, 0)

    when(sends_right, corner.wait_send, cols.wait_send, cols2.wait_send)
    when(has_down, *[copy.wait_send for copy in pieces_r + pieces_l])
    when(at_seam, *[copy.wait_send for copy in parts])
    when(at_seam & has_down, seam_corner.wait_send)
    when(relays_quarter, quarter_on.wait_send)
    when(relays_half, half_on.wait_send)


PIECES_R = (256,)
PIECES_L = (128, 128)


def back(gext, part):
    dma = pltpu.SemaphoreType.DMA
    vmem = pl.BlockSpec(memory_space=pltpu.VMEM)
    square = VMEM((2, 2, W, H), F32)
    return pl.pallas_call(
        back_kernel,
        out_shape=(jax.ShapeDtypeStruct((2, T, T), F32), jax.ShapeDtypeStruct((2, W, W), F32)),
        in_specs=[vmem, vmem],
        out_specs=(vmem, vmem),
        scratch_shapes=[
            square, VMEM((2, 2, T, H), F32), square, square, square, square, square,
            VMEM((4 * W, H), F32), VMEM((2, W, H), F32), VMEM((2 * W, H), F32),
            VMEM((7, 64, H), F32), VMEM((64, H), F32), VMEM((7, 8, H), F32),
            dma((10,)), dma((10,)), dma((3,)), dma((3,)), dma((2,)), dma((2,)), dma((14,)), dma((14,)), dma((14,)), dma((14,)),
        ],
        compiler_params=pltpu.CompilerParams(
            collective_id=1, has_side_effects=True, vmem_limit_bytes=24 * MIB
        ),
        name="back",
    )(gext, part)


def ahead_kernel(tile, amps, ext, amps_out, relay_in, amp_buf, h_send, h_recv, t_sem, a_sem):
    row, col, x, y, z, core = place()
    down, up = ((row + 1) % N_ROW, col), ((row + N_ROW - 1) % N_ROW, col)
    to_right, to_left = (row, (col + 1) % N_COL), (row, (col + N_COL - 1) % N_COL)
    at_seam, past_seam = col == SEAM, col == SEAM + 1
    has_down, has_up = row < N_ROW - 1, row > 0
    sends_left = (col > 0) & (col != SEAM + 1)
    gets_right = (col < N_COL - 1) & (col != SEAM)
    side, idle_side = (5 - x) % 4, (3 - x) % 4
    half, other_half = jnp.where(x == 2, 0, W), jnp.where(x == 2, W, 0)
    relays_half, relays_quarter = (y == 0) & (core == 1) & (x >= 2), (y == 0) & (x < 2)
    is_relay = relays_half | relays_quarter
    source = at_chip(jnp.where(x >= 2, 5 - x, 3 - x), 0, z, 0)
    target = at_chip(jnp.where(x >= 2, 3 - x, 1 - x), 3, z, 1)

    lanes = [
        pltpu.make_async_copy(tile.at[:, :, pl.ds(H * n, H)], ext.at[:, n, pl.ds(0, T), :], t_sem.at[n])
        for n in range(T // H)
    ]
    halves = [
        pltpu.make_async_copy(amps.at[:, :, pl.ds(H * n, H)], amp_buf.at[:, n], a_sem.at[n])
        for n in range(2)
    ]
    for copy in lanes + halves:
        copy.start()
    barrier = greet([down, up, to_left, to_right])

    @pl.when(past_seam)
    def _():
        greet([at_chip(side, 0, z, 1)] + [at_chip(idle_side, 0, z, n) for n in range(2)])
        greet([((row + N_ROW - 1) % N_ROW, SEAM)])

    @pl.when(at_seam)
    def _():
        greet([at_chip((3 - x) % 4, 0, z, 1)] + [at_chip((1 - x) % 4, 0, z, n) for n in range(2)])
        greet([((row + 1) % N_ROW, SEAM + 1)])

    @pl.when(is_relay)
    def _():
        greet([source, target])

    extra = jnp.where(at_seam | past_seam, 4, 0) + jnp.where(is_relay, 2, 0)
    pl.semaphore_wait(barrier, 4 + extra)

    halo = (h_send, h_recv)
    cols = remote(area(ext, 0, 0, T), area(ext, 4, 0, T), halo, 0, to_left)
    rows_l = remote(area(ext, 0, 0, W), area(ext, 0, T, W), halo, 1, up)
    rows_r = remote(area(ext, 2, 0, W), area(ext, 2, T, W), halo, 2, up)
    on_left = remote(area(ext, 0, T, W), area(ext, 4, T, W), halo, 3, to_left)
    seam_corner = remote(area(ext, 0, 0, W), area(ext, 4, T, W), halo, 4, ((row + N_ROW - 1) % N_ROW, SEAM))
    quarter_in = relay_in.at[:, :, pl.ds(0, H), :]
    parts = [remote(at_rows(ext, 0, half, W), relay_in, halo, 5, at_chip(side, 0, z, 1))]
    for n in range(2):
        parts.append(remote(at_rows(ext, 0, other_half + H * n, H), quarter_in, halo, 6 + n, at_chip(idle_side, 0, z, n)))
    half_in = remote(relay_in, relay_in, halo, 5, target)
    half_on = remote(relay_in, at_rows(ext, 4, jnp.where(x == 3, 0, W), W), halo, 8, target)
    quarter = remote(quarter_in, quarter_in, halo, 6 + core, target)
    quarter_on = remote(quarter_in, at_rows(ext, 4, jnp.where(x == 1, W, 0) + H * core, H), halo, 9 + core, target)
    got = [remote(relay_in, area(ext, 4, 0, W), halo, 8, target)]
    got += [remote(quarter_in, area(ext, 4, 0, H), halo, 9 + n, target) for n in range(2)]

    lanes[0].wait()
    lanes[1].wait()
    when(past_seam, parts[1].start, parts[2].start, parts[0].start)
    when(past_seam & has_up, seam_corner.start)
    when(has_up, rows_l.start)
    when(sends_left, cols.start)
    lanes[2].wait()
    lanes[3].wait()
    when(has_up, rows_r.start)
    for copy in halves:
        copy.wait()

    source_at = lax.broadcasted_iota(jnp.int32, (W, W), 0)
    place_at = lax.broadcasted_iota(jnp.int32, (W, W), 1)
    odd = (place_at >= H).astype(jnp.int32)
    chosen = (source_at == 2 * (place_at - H * odd) + odd).astype(F32).astype(BF16)

    def reorder_slot(k, _):
        half = jnp.concatenate(
            [
                jnp.concatenate([amp_buf[k, n, pl.ds(start, H, stride=2), :] for n in range(2)], axis=1)
                for start in range(2)
            ],
            axis=0,
        )
        high, mid = high_low(half)
        low = (half - high.astype(F32) - mid.astype(F32)).astype(BF16)
        amps_out[k] = dot(high, chosen) + dot(mid, chosen) + dot(low, chosen)
        return 0

    lax.fori_loop(0, amps.shape[0] // 2, reorder_slot, 0)
    when(relays_quarter, quarter.wait_recv, quarter_on.start)
    when(relays_half, half_in.wait_recv, half_on.start)
    lax.fori_loop(amps.shape[0] // 2, amps.shape[0], reorder_slot, 0)
    when(has_down, rows_l.wait_recv)
    when(has_down & sends_left, on_left.start)
    when(has_down, rows_r.wait_recv)
    when(gets_right, cols.wait_recv)
    when(at_seam, *[copy.wait_recv for copy in got])
    when(gets_right & has_down, on_left.wait_recv)
    when(at_seam & has_down, seam_corner.wait_recv)
    when(sends_left, cols.wait_send)
    when(has_up, rows_l.wait_send, rows_r.wait_send)
    when(has_down & sends_left, on_left.wait_send)
    when(past_seam, *[copy.wait_send for copy in parts])
    when(past_seam & has_up, seam_corner.wait_send)
    when(relays_quarter, quarter_on.wait_send)
    when(relays_half, half_on.wait_send)


def ahead(tile, amps):
    dma = pltpu.SemaphoreType.DMA
    vmem = pl.BlockSpec(memory_space=pltpu.VMEM)
    hbm = pl.BlockSpec(memory_space=pltpu.HBM)
    return pl.pallas_call(
        ahead_kernel,
        out_shape=(jax.ShapeDtypeStruct(EXT, F32), jax.ShapeDtypeStruct(amps.shape, F32)),
        in_specs=[hbm, hbm],
        out_specs=(vmem, vmem),
        scratch_shapes=[
            VMEM((2, 2, W, H), F32), VMEM((amps.shape[0], 2, W, H), F32),
            dma((11,)), dma((11,)), dma((T // H,)), dma((2,)),
        ],
        compiler_params=pltpu.CompilerParams(
            collective_id=0, has_side_effects=True, vmem_limit_bytes=24 * MIB
        ),
        name="ahead",
    )(pltpu.with_memory_space_constraint(tile, pltpu.HBM), pltpu.with_memory_space_constraint(amps, pltpu.HBM))


def on_device(object_tile, probe, amplitudes, positions, counts):
    ext, amps = ahead(object_tile, amplitudes[0, 0])
    gext, part = run_slots(positions[0, 0].T, counts, ext, amps, probe)
    return back(gext, part)


def solution(mesh):
    in_specs = (
        P(None, "row", "col"),
        P(),
        P("row", "col", None, None, None),
        P("row", "col", None, None),
        P("row", None),
    )
    out_specs = (P(None, "row", "col"), P())
    return jax.shard_map(
        on_device, mesh=mesh, in_specs=in_specs, out_specs=out_specs, check_vma=False
    )
```
